128 devices in a mesh: gore: 16 (over y, z_lo, core), band: 8 (over x, z_hi).
Axes of the slice: x: 4, y: 4, z: 4 (z_hi: 2, z_lo: 2; z = z_hi * 2 + z_lo), core: 2. Of those that a mesh axis runs over, the one named last changes fastest.
Arguments:
- displacement: float32 [3, 2048, 2048], P(None, 'gore', 'band'), may hold values from -2.5 to 2.5
- stiffness: float32 [2048, 2048], P('gore', 'band'), may hold values from 0.5 to 4
- pressure: float32 [2048, 2048], P('gore', 'band'), may hold values from 0.5 to 1.5
- yield_points: int32 [1024], P(('gore', 'band')), may hold values from 0 to 32767, as said below
- route: int32 [1024, 1], P(('gore', 'band')), may hold values from 0 to 15; in each aligned block of 8 rows (0 to 7, 8 to 15, ...) at most 2 rows name the same one
- cell_state: float32 [1024, 3, 13824], P(('gore', 'band')), may hold values from -3 to 3
- weave: float32 [13824], replicated, may hold values from 1 to 8
Outputs:
- nodal_force: float32 [3, 2048, 2048], P(None, 'gore', 'band')
- cell_strain: float32 [4096, 3, 13824], P(('gore', 'band'))
The draws below stay inside these ranges and needn't reach their ends.
Inputs may be any that keep to these rules, and one draw needn't show every extreme that they name: `yield_points`: the 8 entries of one device are distinct node numbers of its 128 x 256 block, counted row by row. `route`: among the 8 rows of one device no worker index appears more than 2 times, and some device reaches 2.
All inputs are finite; a program needn't handle non-finite values.
Results may differ from the reference program's by a relative error of at most 0.0001.
Values sent between devices are 32-bit elements; how exact they have to be, the bound alone decides.
A program may use at most 192 MiB of HBM per device.

```python
import math
import jax
import jax.numpy as jnp
import numpy as np
from jax import lax

G = 24
VOX = 13824
SWEEPS = 2
NG_DEV = 128
NB_DEV = 256
CAP = 8
MOST = 2
SLOTS = 32
YIELD = 1024
NODES_GORE = 2048
NODES_BAND = 2048
N_GORE = 16
N_BAND = 8


def draw_yield_points(key, part):
    devices = N_GORE * N_BAND
    points = NG_DEV * NB_DEV
    device_keys = jax.random.split(key, devices)
    position = jnp.arange(points, dtype=jnp.int32)
    upper = max(1, 2 ** 30 // points)

    def one_device(device_key, device_number):
        scores = jax.random.randint(device_key, (points,), 0, upper, dtype=jnp.int32) * points + position
        forced = (device_number == 0) & ((position == 0) | (position == points - 1))
        scores = jnp.where(forced, position // max(1, points - 1) - 2, scores)
        ranking = jnp.argsort(scores, stable=True)[:CAP]
        return ranking.astype(jnp.int32)
    chosen = jax.vmap(one_device)(device_keys, jnp.arange(devices, dtype=jnp.int32))
    return chosen.reshape(devices * CAP)


def block_levels(stream_key, extent, pieces, smallest, largest):
    level, own = 1.0, jax.random.fold_in(stream_key, 6)
    for dim, shards_of in pieces:
        draws = jnp.exp(jax.random.uniform(jax.random.fold_in(own, dim), (shards_of,), jnp.float32, smallest / len(pieces), largest / len(pieces)))
        level = level * jnp.repeat(draws, extent[dim] // shards_of).reshape([-1 if axis == dim else 1 for axis in range(len(extent))])
    return level


def assign_block(key, own, number, rows, amount, top, reach, slope):
    sequence = jax.random.permutation(key, amount)
    heavy_load, common = shares(amount, rows * top, reach, slope, True), shares(amount, rows * top, reach, slope, False)
    places = jnp.arange(amount)

    def named(sizes, offset_by):
        used = int((sizes > 0).sum())
        fixed = max(1, used // 4)
        moved = fixed + (places - fixed + offset_by * (used - fixed)) % max(1, amount - fixed)
        return jnp.zeros((amount,), jnp.int32).at[sequence[jnp.where(places < fixed, places, moved)]].set(jnp.asarray(sizes, jnp.int32))

    sizes = jnp.where(number % 4 == 0, named(heavy_load, number // 4), named(common, number - number // 4 - 1))
    mixed = jax.random.permutation(jax.random.fold_in(own, 3), amount)
    source_of, taker = mixed[0:amount // 2 * 2:2], mixed[1:amount // 2 * 2:2]
    margin = jnp.minimum(sizes[source_of] - 1, reach - sizes[taker]) // 2
    margin = jnp.where((source_of == sequence[0]) | (taker == sequence[0]) | (sizes[taker] == 0), 0, jnp.maximum(margin, 0))
    moved = jax.random.randint(jax.random.fold_in(own, 4), (amount // 2,), 0, 1 << 20) % (margin + 1)
    sizes = sizes.at[source_of].add(-moved).at[taker].add(moved)
    items = jnp.searchsorted(jnp.cumsum(sizes), jnp.arange(rows * top), side="right").astype(jnp.int32)
    listing = items.reshape(top, rows).T
    listing = listing[jax.random.permutation(jax.random.fold_in(own, 1), rows)]
    offset_by = jax.random.randint(jax.random.fold_in(own, 2), (rows, 1), 0, top)
    return jnp.take_along_axis(listing, (jnp.arange(top)[None, :] + offset_by) % top, axis=1)


def shares(number_of, total, bound, slope, full):
    loads = [(1 << 20) // math.isqrt(grade ** slope) + 1 for grade in range(1, number_of + 1)]
    largest = bound if full else min(bound, max(-(-total // number_of), total * loads[0] // sum(loads)))
    least = 1 if total - largest >= number_of - 1 else 0
    holding, rest = [largest] + [least] * (number_of - 1), total - largest - least * (number_of - 1)
    while rest > 0:
        candidates = [i for i in range(1, number_of) if holding[i] < largest] or [i for i in range(1, number_of) if holding[i] < bound]
        pool, left = sum([loads[i] for i in candidates]), rest
        for i in candidates:
            addition = min(bound - holding[i], max(1, left * loads[i] // pool), rest)
            holding[i] = holding[i] + addition
            rest = rest - addition
    return np.array(holding)


def normal_values(own_key, dims, deviation, most, shards=(), kind=jnp.bfloat16):
    entries = deviation * jax.random.normal(own_key, dims, jnp.float32)
    if shards:
        entries = entries * block_levels(own_key, dims, shards, -0.22, 0.18)
    return jnp.clip(entries, -most, most).astype(kind)


def setup_inputs(seed: int = 0) -> dict:
    seeds = jax.random.split(jax.random.key(seed), 8)
    displacement = normal_values(seeds[0], (3, NODES_GORE, NODES_BAND), 0.4, 2.5, ((1, 16), (2, 8)), jnp.float32)
    stiffness = jnp.clip(jnp.exp(math.log(4.0) - 2.0794415 * jax.random.uniform(seeds[1], (NODES_GORE, NODES_BAND), jnp.float32) ** block_levels(seeds[1], (NODES_GORE, NODES_BAND), ((0, 16), (1, 8)), -0.2, 0.2)), 0.5, 4.0)
    pressure = jnp.clip(0.5 + 1.0 * jax.random.uniform(seeds[2], (NODES_GORE, NODES_BAND), jnp.float32) ** block_levels(seeds[2], (NODES_GORE, NODES_BAND), ((0, 16), (1, 8)), -0.2, 0.2), 0.5, 1.5)
    yield_points = draw_yield_points(jax.random.fold_in(seeds[7], 71), 0)
    route_keys = jax.random.split(jax.random.fold_in(seeds[4], 1), YIELD // CAP)
    route_turns = jax.random.permutation(jax.random.fold_in(seeds[4], 3), YIELD // CAP)
    route = jax.vmap(lambda own, number: assign_block(jax.random.fold_in(seeds[4], 2), own, number, CAP, N_GORE, 1, MOST, 2))(route_keys, route_turns).reshape((YIELD, 1))
    cell_state = normal_values(seeds[5], (YIELD, 3, VOX), 0.5, 3.0, ((0, 128),), jnp.float32)
    weave = jnp.clip(jnp.exp(jax.random.uniform(seeds[6], (VOX,), jnp.float32, math.log(1.0), math.log(8.0))), 1.0, 8.0)
    return dict(displacement=displacement, stiffness=stiffness, pressure=pressure, yield_points=yield_points, route=route, cell_state=cell_state, weave=weave)


BETA = 0.5
REFERENCE_STIFF = 10.0
POISSON = 0.3


def spectral_weight(grid_side):
    wave_index = jnp.arange(grid_side, dtype=jnp.int32)
    sines = jnp.sin(wave_index.astype(jnp.float32) * (2.0 * math.pi / grid_side))
    square = sines * sines
    summed = square[:, None, None] + square[None, :, None] + square[None, None, :]
    level = (wave_index % (grid_side // 2)) == 0
    silent = level[:, None, None] & level[None, :, None] & level[None, None, :]
    return jnp.where(silent, 0.0, 1.0 / (REFERENCE_STIFF * jnp.where(silent, 1.0, summed)))


def central(values, direction):
    return (jnp.roll(values, -1, direction) - jnp.roll(values, 1, direction)) * 0.5


def yarn_law(strain_field, stiff_field):
    magnitude = jnp.sum(strain_field * strain_field, axis=0)
    return stiff_field * (1.0 + BETA * magnitude / (1.0 + magnitude)) * strain_field


def solve_cell(state_row, drive_row, stiff_field, weight):
    strain_field = state_row.astype(jnp.float32).reshape(3, G, G, G)
    strain_field = strain_field - jnp.mean(strain_field, axis=(1, 2, 3), keepdims=True) + drive_row.astype(jnp.float32)[:, None, None, None]
    for iteration in range(SWEEPS):
        stress_field = yarn_law(strain_field, stiff_field)
        source = central(stress_field[0], 0) + central(stress_field[1], 1) + central(stress_field[2], 2)
        potential = jnp.real(jnp.fft.ifftn(jnp.fft.fftn(source) * weight))
        strain_field = strain_field + jnp.stack([central(potential, 0), central(potential, 1), central(potential, 2)])
    stress_field = yarn_law(strain_field, stiff_field)
    return strain_field.reshape(3, G * G * G), jnp.mean(stress_field, axis=(1, 2, 3))


def gore_diff(values):
    return central(values, 1)


def band_diff(values):
    padded = jnp.pad(values, ((0, 0), (0, 0), (1, 1)))
    return (padded[:, :, 2:] - padded[:, :, :-2]) * 0.5


def membrane_strain(gore_slope, band_slope):
    return jnp.stack([gore_slope[0] + 0.5 * gore_slope[2] * gore_slope[2],
                      band_slope[1] + 0.5 * band_slope[2] * band_slope[2],
                      0.5 * (band_slope[0] + gore_slope[1]) + 0.5 * gore_slope[2] * band_slope[2]])


def linear_stress(strain, stiffness):
    return jnp.stack([stiffness * (strain[0] + POISSON * strain[1]),
                      stiffness * (strain[1] + POISSON * strain[0]),
                      stiffness * (1.0 - POISSON) * strain[2]])


def stress_fluxes(stress, gore_slope, band_slope):
    return jnp.stack([stress[0], stress[2], stress[1],
                      stress[0] * gore_slope[2] + stress[2] * band_slope[2],
                      stress[2] * gore_slope[2] + stress[1] * band_slope[2]])


def assemble(gore_flux, band_flux, pressure):
    return jnp.stack([gore_flux[0] + band_flux[1], gore_flux[1] + band_flux[2], gore_flux[3] + band_flux[4] + pressure])


def reference(displacement, stiffness, pressure, yield_points, route, cell_state, weave):
    gore_slope = gore_diff(displacement)
    band_slope = band_diff(displacement)
    strain = membrane_strain(gore_slope, band_slope)
    devices = N_GORE * N_BAND
    entry_index = jnp.arange(devices * CAP, dtype=jnp.int32)
    device = entry_index // CAP
    gore_of = device // N_BAND
    band_of = device % N_BAND
    node_row = gore_of * NG_DEV + yield_points // NB_DEV
    node_col = band_of * NB_DEV + yield_points % NB_DEV
    flat_index = (node_row * (NB_DEV * N_BAND) + node_col).astype(jnp.int32)
    cell_drive = jnp.take(strain.reshape(3, -1), flat_index, axis=1).T
    stiff_field = weave.reshape(G, G, G)
    weight = spectral_weight(G)

    def one_cell(cell_pair):
        return solve_cell(cell_pair[0], cell_pair[1], stiff_field, weight)

    new_states, cell_stress = lax.map(one_cell, (cell_state, cell_drive))
    workers = route[:, 0].reshape(devices, CAP)
    onehot = (workers[:, :, None] == jnp.arange(N_GORE, dtype=jnp.int32)[None, None, :]).astype(jnp.int32)
    earlier = (jnp.cumsum(onehot, axis=1) - onehot).astype(jnp.int32)
    slot_rank = jnp.sum(earlier * onehot, axis=2).astype(jnp.int32).reshape(-1)
    target = ((route[:, 0] * N_BAND + band_of) * SLOTS + gore_of * MOST + slot_rank).astype(jnp.int32)
    cell_strain = jnp.zeros((devices * SLOTS, 3, G * G * G), jnp.float32).at[target].set(new_states)
    stress = linear_stress(strain, stiffness).reshape(3, -1).at[:, flat_index].set(cell_stress.T)
    stress = stress.reshape(3, NG_DEV * N_GORE, NB_DEV * N_BAND)
    fluxes = stress_fluxes(stress, gore_slope, band_slope)
    nodal_force = assemble(gore_diff(fluxes), band_diff(fluxes), pressure)
    return nodal_force, cell_strain
```

```python
import math

import jax
import jax.numpy as jnp
import numpy as np
from jax import lax
from jax.experimental import pallas as pl
from jax.experimental.pallas import tpu as pltpu
from jax.sharding import PartitionSpec as P

G = 24
PLANE = G * G
VOX = G * G * G
SWEEPS = 2
POISSON = 0.3
CAP = 8
MOST = 2
ROWS = 3 * VOX // 128
PACK = 328
MESH = pl.DeviceIdType.MESH
F32 = jnp.float32
BF16 = jnp.bfloat16


def tables():
    n = np.arange(G)
    phase = 2.0 * np.pi * (np.outer(n, n) % G) / G
    hartley = (np.cos(phase) + np.sin(phase)) / math.sqrt(G)
    plane = np.kron(hartley, hartley)
    line = np.kron(hartley, np.eye(CAP))

    def split(a):
        high = a.astype(np.float32).astype(jnp.bfloat16)
        low = (a - high.astype(np.float64)).astype(np.float32).astype(jnp.bfloat16)
        return high, low

    square = np.sin(phase[1]) ** 2
    summed = square[:, None, None] + square[None, :, None] + square[None, None, :]
    level = n % (G // 2) == 0
    silent = level[:, None, None] & level[None, :, None] & level[None, None, :]
    weight = np.where(silent, 0.0, 1.0 / (10.0 * np.where(silent, 1.0, summed)))
    plane_high, plane_low = split(plane)
    line_high, line_low = split(line)
    return (
        plane_high,
        plane_low,
        np.concatenate([line_high, line_low], axis=0),
        weight.reshape(G, 1, PLANE).astype(np.float32),
    )


def shifted(v, k):
    k = k % v.shape[1]
    return jnp.concatenate([v[:, k:], v[:, :k]], axis=1)


def diff_upper(v):
    return shifted(v, G) - shifted(v, -G)


def diff_lower(v, low):
    forward = jnp.where(low == G - 1, shifted(v, 1 - G), shifted(v, 1))
    backward = jnp.where(low == 0, shifted(v, G - 1), shifted(v, -1))
    return forward - backward


def to_row(column):
    n = column.shape[0]
    diagonal = lax.broadcasted_iota(jnp.int32, (n, n), 0) == lax.broadcasted_iota(jnp.int32, (n, n), 1)
    return jnp.sum(jnp.where(diagonal, column, 0.0), axis=0, keepdims=True)


def to_column(row):
    n = row.shape[1]
    diagonal = lax.broadcasted_iota(jnp.int32, (n, n), 0) == lax.broadcasted_iota(jnp.int32, (n, n), 1)
    return jnp.sum(jnp.where(diagonal, row, 0.0), axis=1, keepdims=True)


def gore_diff(v, before, after):
    down = jnp.concatenate([v[1:], after], axis=0)
    up = jnp.concatenate([before, v[:-1]], axis=0)
    return (down - up) * 0.5


def band_diff(v, before, after):
    right = jnp.concatenate([v[:, 1:], after], axis=1)
    left = jnp.concatenate([before, v[:, :-1]], axis=1)
    return (right - left) * 0.5


def kernel(
    n_gore, n_band,
    yield_ref, route_ref, disp_ref, stiff_ref, press_ref, state_ref, weave_ref,
    plane_hi_ref, plane_lo_ref, line_ref, weight_ref,
    force_ref, recv_ref,
    halo_g, halo_b, got_g, got_b, slopes, strain_s,
    e_s, s_pad, d_s, x_s, f_s, cells, send,
    halo_send, halo_recv, send_sem, recv_sem, own_sem,
):
    g, b = lax.axis_index("gore"), lax.axis_index("band")
    up, down = lax.rem(g + 1, n_gore), lax.rem(g + n_gore - 1, n_gore)
    right, left = lax.rem(b + 1, n_band), lax.rem(b + n_band - 1, n_band)
    nodes_g, nodes_b = stiff_ref.shape

    barrier = pltpu.get_barrier_semaphore()
    for d in range(1, n_gore):
        pl.semaphore_signal(barrier, inc=1, device_id=(lax.rem(g + d, n_gore), b), device_id_type=MESH)
    pl.semaphore_signal(barrier, inc=1, device_id=(g, right), device_id_type=MESH)
    pl.semaphore_signal(barrier, inc=1, device_id=(g, left), device_id_type=MESH)

    def halo_copies(k):
        out = []
        for side, target in enumerate(((down, b), (up, b), (g, left), (g, right))):
            source, place = (halo_g, got_g) if side < 2 else (halo_b, got_b)
            out.append(
                pltpu.make_async_remote_copy(
                    src_ref=source.at[2 * k + side % 2],
                    dst_ref=place.at[2 * k + side % 2],
                    send_sem=halo_send.at[4 * k + side],
                    recv_sem=halo_recv.at[4 * k + side],
                    device_id=target,
                    device_id_type=MESH,
                )
            )
        return out

    for c in range(3):
        v = disp_ref[c]
        halo_g[0, c : c + 1, :] = v[0:1]
        halo_g[1, c : c + 1, :] = v[nodes_g - 1 :]
        halo_b[0, c : c + 1, :] = to_row(v[:, 0:1])
        halo_b[1, c : c + 1, :] = to_row(v[:, nodes_b - 1 :])
    pl.semaphore_wait(barrier, n_gore + 1)
    first = halo_copies(0)
    for copy in first:
        copy.start()

    def load_states(i, sums):
        out = []
        for c in range(3):
            pair = state_ref[c, :, pl.ds(pl.multiple_of(i * 2 * PLANE, 128), 2 * PLANE)]
            even, odd = pair[:, :PLANE], pair[:, PLANE:]
            e_s[c, pl.ds(pl.multiple_of(i * 16, 16), 16), :] = jnp.concatenate([even, odd], axis=0)
            out.append(sums[c] + even + odd)
        return tuple(out)

    zero = jnp.zeros((CAP, PLANE), F32)
    sums = lax.fori_loop(0, G // 2, load_states, (zero, zero, zero))
    means = [jnp.sum(s, axis=1, keepdims=True) * (1.0 / VOX) for s in sums]

    for copy in first:
        copy.wait()

    inner_left, inner_right = b > 0, b < n_band - 1
    for c in range(3):
        v = disp_ref[c]
        before = jnp.where(inner_left, to_column(got_b[1, c : c + 1, :]), 0.0)
        after = jnp.where(inner_right, to_column(got_b[0, c : c + 1, :]), 0.0)
        slopes[c] = gore_diff(v, got_g[1, c : c + 1, :], got_g[0, c : c + 1, :])
        slopes[3 + c] = band_diff(v, before, after)
    gz, bz = slopes[2], slopes[5]
    strain_s[0] = slopes[0] + 0.5 * gz * gz
    strain_s[1] = slopes[4] + 0.5 * bz * bz
    strain_s[2] = 0.5 * (slopes[3] + slopes[1]) + 0.5 * gz * bz

    cell_row = lax.broadcasted_iota(jnp.int32, (CAP, 1), 0)
    lane = lax.broadcasted_iota(jnp.int32, (CAP, nodes_b), 1)
    points = [yield_ref[r] for r in range(CAP)]
    wanted = jnp.zeros((CAP, 1), jnp.int32)
    for r in range(CAP):
        wanted = jnp.where(cell_row == r, lax.rem(points[r], nodes_b), wanted)
    shift = []
    for c in range(3):
        rows = [strain_s[c, pl.ds(lax.div(points[r], nodes_b), 1), :] for r in range(CAP)]
        rows = jnp.concatenate(rows, axis=0)
        drive = jnp.sum(jnp.where(lane == wanted, rows, 0.0), axis=1, keepdims=True)
        drive = drive - means[c]
        shift.append(jnp.concatenate([drive, drive], axis=0))

    low = lax.rem(lax.broadcasted_iota(jnp.int32, (16, PLANE), 1), G)

    def stiffness_of(i):
        even = jnp.broadcast_to(weave_ref[2 * i], (CAP, PLANE))
        odd = jnp.broadcast_to(weave_ref[2 * i + 1], (CAP, PLANE))
        return jnp.concatenate([even, odd], axis=0)

    def advance(i, sweep):
        at = pl.multiple_of(i * 16, 16)
        e = [e_s[c, pl.ds(at, 16), :] for c in range(3)]
        if sweep == 0:
            e = [e[c] + shift[c] for c in range(3)]
        else:
            middle = f_s[pl.ds(at + 8, 16), :]
            e[0] = e[0] + 0.5 * (f_s[pl.ds(at + 16, 16), :] - f_s[pl.ds(at, 16), :])
            e[1] = e[1] + 0.5 * diff_upper(middle)
            e[2] = e[2] + 0.5 * diff_lower(middle, low)
        size = e[0] * e[0] + e[1] * e[1] + e[2] * e[2]
        factor = stiffness_of(i) * (1.5 - 0.5 / (1.0 + size))
        return at, e, [factor * v for v in e]

    def parts(v):
        high = v.astype(BF16)
        return high, (v - high.astype(F32)).astype(BF16)

    def lines(v):
        high, rest = parts(v)
        both = jnp.dot(line_ref[...], high, preferred_element_type=F32)
        n = G * CAP
        return both[:n] + both[n:] + jnp.dot(line_ref[0:n, :], rest, preferred_element_type=F32)

    def planes(both):
        n = G * CAP
        out = jnp.dot(both, plane_hi_ref[...], preferred_element_type=F32)
        return out[:n] + out[n:] + jnp.dot(both[:n], plane_lo_ref[...], preferred_element_type=F32)

    for sweep in range(SWEEPS):

        def law(i, carry, sweep=sweep):
            at, e, s = advance(i, sweep)
            for c in range(3):
                e_s[c, pl.ds(at, 16), :] = e[c]
            s_pad[pl.ds(at + 8, 16), :] = s[0]
            d_s[pl.ds(at, 16), :] = diff_upper(s[1]) + diff_lower(s[2], low)
            return carry

        lax.fori_loop(0, G // 2, law, 0)
        s_pad[0:8, :] = s_pad[G * 8 : G * 8 + 8, :]
        s_pad[G * 8 + 8 :, :] = s_pad[8:16, :]

        def source(i, carry):
            at = pl.multiple_of(i * 16, 16)
            v = 0.5 * (s_pad[pl.ds(at + 16, 16), :] - s_pad[pl.ds(at, 16), :] + d_s[pl.ds(at, 16), :])
            high, rest = parts(v)
            x_s[pl.ds(at, 16), :] = high
            x_s[pl.ds(G * CAP + at, 16), :] = rest
            return carry

        lax.fori_loop(0, G // 2, source, 0)
        spectrum = lines(planes(x_s[...]))
        weight = jnp.broadcast_to(weight_ref[...], (G, CAP, PLANE)).reshape(G * CAP, PLANE)
        back = lines(spectrum * weight)
        high, rest = parts(back)
        x_s[0 : G * CAP, :] = high
        x_s[G * CAP :, :] = rest
        f_s[8 : G * 8 + 8, :] = planes(x_s[...])
        f_s[0:8, :] = f_s[G * 8 : G * 8 + 8, :]
        f_s[G * 8 + 8 :, :] = f_s[8:16, :]

    def finish(i, sums):
        at, e, s = advance(i, SWEEPS)
        out = []
        for c in range(3):
            wide = jnp.concatenate([e[c][0:8], e[c][8:16]], axis=1)
            for t in range(2 * PLANE // 128):
                row = pl.multiple_of((c * (VOX // 128) + i * 9 + t) * CAP, CAP)
                cells[pl.ds(row, CAP), :] = wide[:, 128 * t : 128 * t + 128]
            out.append(sums[c] + s[c][0:8] + s[c][8:16])
        return tuple(out)

    sums = lax.fori_loop(0, G // 2, finish, (zero, zero, zero))
    point_stress = [jnp.sum(s, axis=1, keepdims=True) * (1.0 / VOX) for s in sums]

    stiff = stiff_ref[...]
    e11, e22, e12 = strain_s[0], strain_s[1], strain_s[2]
    stress = [
        stiff * (e11 + POISSON * e22),
        stiff * (e22 + POISSON * e11),
        stiff * (1.0 - POISSON) * e12,
    ]
    node = lax.broadcasted_iota(jnp.int32, stiff.shape, 0) * nodes_b + lax.broadcasted_iota(jnp.int32, stiff.shape, 1)
    for r in range(CAP):
        here = node == points[r]
        for c in range(3):
            stress[c] = jnp.where(here, point_stress[c][r : r + 1, :], stress[c])
    s11, s22, s12 = stress
    gz, bz = slopes[2], slopes[5]
    t1 = s11 * gz + s12 * bz
    t2 = s12 * gz + s22 * bz
    over_gore, over_band = [s11, s12, t1], [s12, s22, t2]
    for c in range(3):
        halo_g[2, c : c + 1, :] = over_gore[c][0:1]
        halo_g[3, c : c + 1, :] = over_gore[c][nodes_g - 1 :]
        halo_b[2, c : c + 1, :] = to_row(over_band[c][:, 0:1])
        halo_b[3, c : c + 1, :] = to_row(over_band[c][:, nodes_b - 1 :])
    second = halo_copies(1)
    for copy in second:
        copy.start()
    slopes[0] = s11
    slopes[1] = s12
    slopes[3] = s22
    slopes[4] = t1
    slopes[5] = t2

    workers = [route_ref[r] for r in range(CAP)]

    def slot_copy(d):
        return pltpu.make_async_remote_copy(
            src_ref=send.at[d],
            dst_ref=recv_ref.at[g],
            send_sem=send_sem.at[d],
            recv_sem=recv_sem.at[d],
            device_id=(lax.rem(g + d, n_gore), b),
            device_id_type=MESH,
        )

    def pack(d):
        worker = lax.rem(g + d, n_gore)
        one, two = jnp.int32(CAP), jnp.int32(CAP)
        for r in reversed(range(CAP)):
            named = workers[r] == worker
            two = jnp.where(named, one, two)
            one = jnp.where(named, r, one)
        for k, cell in enumerate((one, two)):
            filled = cell < CAP
            begin = lax.rem(cell, CAP)

            def rows(m, carry):
                v = cells[pl.ds(m * 64 + begin, 8, stride=CAP), :]
                send[d, k, pl.ds(pl.multiple_of(m * 8, 8), 8), :] = jnp.where(filled, v, 0.0)
                return carry

            lax.fori_loop(0, PACK // 8, rows, 0, unroll=True)

    cells[ROWS * CAP :, :] = jnp.zeros((PACK * CAP - ROWS * CAP, 128), F32)

    def dispatch(d, carry):
        pack(d)
        slot_copy(d).start()
        return carry

    lax.fori_loop(1, n_gore, dispatch, 0)
    pack(0)
    own = pltpu.make_async_copy(send.at[0], recv_ref.at[g], own_sem)
    own.start()

    for copy in second:
        copy.wait()
    edge = []
    for c in range(3):
        before = jnp.where(inner_left, to_column(got_b[3, c : c + 1, :]), 0.0)
        after = jnp.where(inner_right, to_column(got_b[2, c : c + 1, :]), 0.0)
        edge.append((before, after))
    pairs = ((0, 1), (1, 3), (4, 5))
    for c, (p, q) in enumerate(pairs):
        value = gore_diff(slopes[p], got_g[3, c : c + 1, :], got_g[2, c : c + 1, :])
        value = value + band_diff(slopes[q], *edge[c])
        if c == 2:
            value = value + press_ref[...]
        force_ref[c] = value

    own.wait()

    def settle(d, carry):
        copy = slot_copy(d)
        copy.wait_send()
        copy.wait_recv()
        return carry

    lax.fori_loop(1, n_gore, settle, 0)


def layout_kernel(slots, recv_ref, out_ref, got, made, in_sem, out_sem):
    tiles = VOX // 128
    spans = []
    for c in range(3):
        low = c * tiles // 8 * 8
        high = min(-(-(c + 1) * tiles // 8) * 8, PACK)
        spans.append((low, high))
    loads = []
    for c, (low, high) in enumerate(spans):
        place = got.at[c, :, 0 : high - low, :]
        loads.append(pltpu.make_async_copy(recv_ref.at[:, low:high, :], place, in_sem.at[c]))
        loads[-1].start()
    stores = []
    for c, (low, _) in enumerate(spans):
        loads[c].wait()
        for t in range(slots // 8):

            def column(j, carry):
                v = got[c, 8 * t : 8 * t + 8, pl.ds(c * tiles - low + 4 * j, 4), :]
                for s in range(4):
                    made[c, 8 * t : 8 * t + 8, pl.ds(pl.multiple_of((4 * j + s) * 128, 128), 128)] = v[:, s, :]
                return carry

            lax.fori_loop(0, tiles // 4, column, 0)
        stores.append(pltpu.make_async_copy(made.at[c], out_ref.at[c], out_sem.at[c]))
        stores[-1].start()
    for copy in stores:
        copy.wait()


def local(displacement, stiffness, pressure, yield_points, route, cell_state, weave):
    n_gore, n_band = lax.axis_size("gore"), lax.axis_size("band")
    slots = n_gore * MOST
    nodes_g, nodes_b = stiffness.shape
    plane_high, plane_low, line, weight = tables()
    vmem, smem = pl.BlockSpec(memory_space=pltpu.VMEM), pl.BlockSpec(memory_space=pltpu.SMEM)
    any_space = pl.BlockSpec(memory_space=pl.ANY)
    n = G * CAP

    def run(*args):
        return pl.pallas_call(
            lambda *refs: kernel(n_gore, n_band, *refs),
            out_shape=(
                jax.ShapeDtypeStruct((3, nodes_g, nodes_b), F32),
                jax.ShapeDtypeStruct((n_gore, MOST, PACK, 128), F32),
            ),
            in_specs=[smem, smem] + [vmem] * 9,
            out_specs=(vmem, any_space),
            scratch_shapes=[
                pltpu.VMEM((4, 8, nodes_b), F32),
                pltpu.VMEM((4, 8, nodes_g), F32),
                pltpu.VMEM((4, 8, nodes_b), F32),
                pltpu.VMEM((4, 8, nodes_g), F32),
                pltpu.VMEM((6, nodes_g, nodes_b), F32),
                pltpu.VMEM((3, nodes_g, nodes_b), F32),
                pltpu.VMEM((3, n, PLANE), F32),
                pltpu.VMEM((n + 16, PLANE), F32),
                pltpu.VMEM((n, PLANE), F32),
                pltpu.VMEM((2 * n, PLANE), BF16),
                pltpu.VMEM((n + 16, PLANE), F32),
                pltpu.VMEM((PACK * CAP, 128), F32),
                pltpu.VMEM((n_gore, MOST, PACK, 128), F32),
                pltpu.SemaphoreType.DMA((8,)),
                pltpu.SemaphoreType.DMA((8,)),
                pltpu.SemaphoreType.DMA((n_gore,)),
                pltpu.SemaphoreType.DMA((n_gore,)),
                pltpu.SemaphoreType.DMA,
            ],
            compiler_params=pltpu.CompilerParams(
                collective_id=0, has_side_effects=True, vmem_limit_bytes=48 * 2**20
            ),
            name="cells",
        )(*args)

    force, recv = run(
        yield_points,
        route.reshape(-1),
        displacement,
        stiffness,
        pressure,
        cell_state.transpose(1, 0, 2),
        weave.reshape(G, 1, PLANE),
        jnp.asarray(plane_high),
        jnp.asarray(plane_low),
        jnp.asarray(line),
        jnp.asarray(weight),
    )
    cell_strain = pl.pallas_call(
        lambda *refs: layout_kernel(slots, *refs),
        out_shape=jax.ShapeDtypeStruct((3, slots, VOX), F32),
        in_specs=[any_space],
        out_specs=any_space,
        scratch_shapes=[
            pltpu.VMEM((3, slots, 120, 128), F32),
            pltpu.VMEM((3, slots, VOX), F32),
            pltpu.SemaphoreType.DMA((3,)),
            pltpu.SemaphoreType.DMA((3,)),
        ],
        compiler_params=pltpu.CompilerParams(vmem_limit_bytes=32 * 2**20),
        name="layout",
    )(recv.reshape(slots, PACK, 128))
    return force, cell_strain.transpose(1, 0, 2)


def solution(mesh):
    return jax.shard_map(
        local,
        mesh=mesh,
        in_specs=(
            P(None, "gore", "band"),
            P("gore", "band"),
            P("gore", "band"),
            P(("gore", "band")),
            P(("gore", "band"), None),
            P(("gore", "band"), None, None),
            P(),
        ),
        out_specs=(P(None, "gore", "band"), P(("gore", "band"), None, None)),
        check_vma=False,
    )
```

```python
import math

import jax
import jax.numpy as jnp
import numpy as np
from jax import lax
from jax.experimental import pallas as pl
from jax.experimental.pallas import tpu as pltpu
from jax.sharding import PartitionSpec as P

G = 24
PLANE = G * G
VOX = G * G * G
SWEEPS = 2
POISSON = 0.3
CAP = 8
MOST = 2
ROWS = 3 * VOX // 128
PACK = 328
RING, LINE, CORE = 4, 2, 2
GROUP = RING * LINE * CORE
RING_FIRST, LINE_SECOND, LINE_FIRST, RING_SECOND = 5, 10, 8, 6
STEPS = (1, 3, 2)
FINAL_RING = RING * RING_FIRST
FINAL_LINE = FINAL_RING + LINE_SECOND
FINAL = FINAL_LINE + RING * RING_SECOND
MESH = pl.DeviceIdType.MESH
F32 = jnp.float32
BF16 = jnp.bfloat16


def tables():
    n = np.arange(G)
    phase = 2.0 * np.pi * (np.outer(n, n) % G) / G
    hartley = (np.cos(phase) + np.sin(phase)) / math.sqrt(G)
    plane = np.kron(hartley, hartley)
    line = np.kron(hartley, np.eye(CAP))

    def split(a):
        high = a.astype(np.float32).astype(jnp.bfloat16)
        low = (a - high.astype(np.float64)).astype(np.float32).astype(jnp.bfloat16)
        return high, low

    square = np.sin(phase[1]) ** 2
    summed = square[:, None, None] + square[None, :, None] + square[None, None, :]
    level = n % (G // 2) == 0
    silent = level[:, None, None] & level[None, :, None] & level[None, None, :]
    weight = np.where(silent, 0.0, 1.0 / (10.0 * np.where(silent, 1.0, summed)))
    plane_high, plane_low = split(plane)
    line_high, line_low = split(line)
    return (
        plane_high,
        plane_low,
        np.concatenate([line_high, line_low], axis=0),
        weight.reshape(G, 1, PLANE).astype(np.float32),
    )


def shifted(v, k):
    k = k % v.shape[1]
    return jnp.concatenate([v[:, k:], v[:, :k]], axis=1)


def diff_upper(v):
    return shifted(v, G) - shifted(v, -G)


def diff_lower(v, low):
    forward = jnp.where(low == G - 1, shifted(v, 1 - G), shifted(v, 1))
    backward = jnp.where(low == 0, shifted(v, G - 1), shifted(v, -1))
    return forward - backward


def to_row(column):
    n = column.shape[0]
    diagonal = lax.broadcasted_iota(jnp.int32, (n, n), 0) == lax.broadcasted_iota(jnp.int32, (n, n), 1)
    return jnp.sum(jnp.where(diagonal, column, 0.0), axis=0, keepdims=True)


def to_column(row):
    n = row.shape[1]
    diagonal = lax.broadcasted_iota(jnp.int32, (n, n), 0) == lax.broadcasted_iota(jnp.int32, (n, n), 1)
    return jnp.sum(jnp.where(diagonal, row, 0.0), axis=1, keepdims=True)


def gore_diff(v, before, after):
    down = jnp.concatenate([v[1:], after], axis=0)
    up = jnp.concatenate([before, v[:-1]], axis=0)
    return (down - up) * 0.5


def band_diff(v, before, after):
    right = jnp.concatenate([v[:, 1:], after], axis=1)
    left = jnp.concatenate([before, v[:, :-1]], axis=1)
    return (right - left) * 0.5


def rank_of(key, key_column, earlier):
    return jnp.sum(jnp.where((key_column == key) & earlier, 1.0, 0.0), axis=0, keepdims=True)


def routing(worker, g):
    n = GROUP * CAP
    lane = lax.broadcasted_iota(jnp.int32, (1, n), 1)
    to = worker.astype(jnp.int32)
    source = lane >> 3
    to_y, to_z = to >> 2, (to >> 1) & 1
    from_y, from_z, from_c = source >> 2, (source >> 1) & 1, source & 1
    y, z, c = g >> 2, (g >> 1) & 1, g & 1
    crossing, first = to_z != from_z, from_c == 0
    alone = -1 - lane
    earlier = lax.broadcasted_iota(jnp.int32, (n, n), 0) < lax.broadcasted_iota(jnp.int32, (n, n), 1)

    def rank(key):
        key = key.astype(F32)
        return rank_of(key, to_column(key), earlier).astype(jnp.int32)

    ring_first = rank(source * RING + to_y)
    line_second = rank(jnp.where(first & crossing, from_z * RING + to_y, alone))
    line_first = rank(jnp.where(crossing, source, alone))
    ring_second = rank(jnp.where(first, alone, (from_y * RING + to_y) * LINE + to_z))
    slot = rank(source * GROUP + to)
    over = first & ((ring_first >= RING_FIRST) | (crossing & (line_second >= LINE_SECOND)))
    over = over | (jnp.logical_not(first) & (ring_second >= RING_SECOND))

    own, mine = source == g, from_c == c
    at_ring = c == 0
    cell = lane & 7
    place1_ring = jnp.where(own, to_y * RING_FIRST + ring_first, -1)
    place1 = jnp.where(at_ring, place1_ring, jnp.where(own & crossing, line_first, -1))
    place2_ring = jnp.where(mine & crossing & (from_z == z) & (to_y == y), line_second, -1)
    place2_line = jnp.where(mine & (from_y == y) & (to_z == z), to_y * RING_SECOND + ring_second, -1)
    place2 = jnp.where(at_ring, place2_ring, place2_line)
    from_ring = from_y * RING_FIRST + ring_first
    from_line = jnp.where(from_z == z, cell, CAP + line_first)
    index2 = jnp.where(at_ring, from_ring, from_line)
    place3 = jnp.where(to == g, source * MOST + slot, -1)
    index3 = jnp.where(crossing, FINAL_RING + line_second, from_ring)
    index3 = jnp.where(first, index3, FINAL_LINE + from_y * RING_SECOND + ring_second)

    column = lax.broadcasted_iota(jnp.int32, (n, n), 1).astype(F32)

    def listing(place, index):
        place, index = to_column(place.astype(F32)), to_column(index.astype(F32) + 1.0)
        return jnp.sum(jnp.where(place == column, index, 0.0), axis=0, keepdims=True).astype(jnp.int32)

    over = jnp.sum(jnp.where(over, 1.0, 0.0), axis=1, keepdims=True)
    return listing(place1, cell), listing(place2, index2), listing(place3, index3), over


def kernel(
    n_gore, n_band,
    yield_hbm, route_hbm, disp_hbm, stiff_hbm, press_hbm, state_hbm, weave_hbm,
    plane_hi_hbm, plane_lo_hbm, line_hbm, weight_hbm,
    force_ref, flag_ref, result_ref, own_ref,
    yield_ref, route_ref, disp_ref, stiff_ref, press_ref, state_ref, weave_ref,
    plane_hi_ref, plane_lo_ref, line_ref, weight_ref,
    halo_g, halo_b, got_g, got_b, slopes, strain_s,
    e_s, w_s, s_pad, d_s, x_s, f_s, cells,
    names, names_got, flag, flag_got, table_v, table,
    own, send1, send2, ring_got, line_got, final, chosen,
    in_sem, halo_send, halo_recv, name_send, name_recv, flag_send, flag_recv, table_sem,
    hop1_send, hop1_recv, hop2_send, hop2_recv, share_send, share_recv, local_sem, out_sem,
):
    g, b = lax.axis_index("gore"), lax.axis_index("band")
    y, z, core = lax.div(g, LINE * CORE), lax.rem(lax.div(g, CORE), LINE), lax.rem(g, CORE)
    up, down = lax.rem(g + 1, n_gore), lax.rem(g + n_gore - 1, n_gore)
    right, left = lax.rem(b + 1, n_band), lax.rem(b + n_band - 1, n_band)
    nodes_g, nodes_b = stiff_ref.shape

    barrier = pltpu.get_barrier_semaphore()
    for d in range(1, n_gore):
        pl.semaphore_signal(barrier, inc=1, device_id=(lax.rem(g + d, n_gore), b), device_id_type=MESH)
    for d in range(1, n_band):
        pl.semaphore_signal(barrier, inc=1, device_id=(g, lax.rem(b + d, n_band)), device_id_type=MESH)

    operands = (
        (route_hbm, route_ref), (disp_hbm, disp_ref), (yield_hbm, yield_ref), (state_hbm, state_ref),
        (weave_hbm, weave_ref), (stiff_hbm, stiff_ref), (plane_hi_hbm, plane_hi_ref),
        (plane_lo_hbm, plane_lo_ref), (line_hbm, line_ref), (weight_hbm, weight_ref), (press_hbm, press_ref),
    )
    loads = [pltpu.make_async_copy(p, q, in_sem.at[i]) for i, (p, q) in enumerate(operands)]
    for copy in loads:
        copy.start()

    def halo_copies(k):
        out = []
        for side, target in enumerate(((down, b), (up, b), (g, left), (g, right))):
            source, place = (halo_g, got_g) if side < 2 else (halo_b, got_b)
            out.append(
                pltpu.make_async_remote_copy(
                    src_ref=source.at[2 * k + side % 2],
                    dst_ref=place.at[2 * k + side % 2],
                    send_sem=halo_send.at[4 * k + side],
                    recv_sem=halo_recv.at[4 * k + side],
                    device_id=target,
                    device_id_type=MESH,
                )
            )
        return out

    def name_copy(d):
        return pltpu.make_async_remote_copy(
            src_ref=names, dst_ref=names_got.at[g], send_sem=name_send.at[d], recv_sem=name_recv.at[d],
            device_id=(lax.rem(g + d, n_gore), b), device_id_type=MESH,
        )

    def flag_copy(d):
        return pltpu.make_async_remote_copy(
            src_ref=flag, dst_ref=flag_got.at[b], send_sem=flag_send.at[d], recv_sem=flag_recv.at[d],
            device_id=(g, lax.rem(b + d, n_band)), device_id_type=MESH,
        )

    loads[0].wait()
    place = lax.broadcasted_iota(jnp.int32, (8, 128), 1)
    named = jnp.zeros((8, 128), jnp.int32)
    for r in range(CAP):
        named = jnp.where(place == g * CAP + r, route_ref[r], named)
    names[...] = named
    loads[1].wait()
    for c in range(3):
        v = disp_ref[c]
        halo_g[0, c : c + 1, :] = v[0:1]
        halo_g[1, c : c + 1, :] = v[nodes_g - 1 :]
        halo_b[0, c : c + 1, :] = to_row(v[:, 0:1])
        halo_b[1, c : c + 1, :] = to_row(v[:, nodes_b - 1 :])
    pl.semaphore_wait(barrier, n_gore + n_band - 2)
    first = halo_copies(0)
    for copy in first:
        copy.start()
    for d in range(1, n_gore):
        name_copy(d).start()

    loads[3].wait()
    loads[4].wait()

    def load_states(i, sums):
        at = pl.multiple_of(i * 16, 16)
        out = []
        for c in range(3):
            pair = state_ref[c, :, pl.ds(pl.multiple_of(i * 2 * PLANE, 128), 2 * PLANE)]
            even, odd = pair[:, :PLANE], pair[:, PLANE:]
            e_s[c, pl.ds(at, 16), :] = jnp.concatenate([even, odd], axis=0)
            out.append(sums[c] + even + odd)
        rows = [jnp.broadcast_to(weave_ref[pl.ds(i * 9 + t, 1), :], (CAP, 128)) for t in range(9)]
        pair = jnp.concatenate(rows, axis=1)
        w_s[pl.ds(at, 16), :] = jnp.concatenate([pair[:, :PLANE], pair[:, PLANE:]], axis=0)
        return tuple(out)

    zero = jnp.zeros((CAP, PLANE), F32)
    sums = lax.fori_loop(0, G // 2, load_states, (zero, zero, zero))
    means = [jnp.sum(s, axis=1, keepdims=True) * (1.0 / VOX) for s in sums]

    for d in range(1, n_gore):
        name_copy(d).wait()
    for copy in first:
        copy.wait()

    worker = names[0:1, :]
    for d in range(1, n_gore):
        worker = worker + names_got[lax.rem(g + d, n_gore), 0:1, :]
    list1, list2, list3, over = routing(worker.astype(F32), g)
    table_v[0:1, :] = list1
    table_v[1:2, :] = list2
    table_v[2:3, :] = list3
    to_scalars = pltpu.make_async_copy(table_v, table, table_sem)
    to_scalars.start()
    flag[...] = jnp.broadcast_to(over, (8, 128)).astype(jnp.int32)
    for d in range(1, n_band):
        flag_copy(d).start()

    inner_left, inner_right = b > 0, b < n_band - 1
    for c in range(3):
        v = disp_ref[c]
        before = jnp.where(inner_left, to_column(got_b[1, c : c + 1, :]), 0.0)
        after = jnp.where(inner_right, to_column(got_b[0, c : c + 1, :]), 0.0)
        slopes[c] = gore_diff(v, got_g[1, c : c + 1, :], got_g[0, c : c + 1, :])
        slopes[3 + c] = band_diff(v, before, after)
    gz, bz = slopes[2], slopes[5]
    strain_s[0] = slopes[0] + 0.5 * gz * gz
    strain_s[1] = slopes[4] + 0.5 * bz * bz
    strain_s[2] = 0.5 * (slopes[3] + slopes[1]) + 0.5 * gz * bz

    loads[2].wait()
    cell_row = lax.broadcasted_iota(jnp.int32, (CAP, 1), 0)
    lane = lax.broadcasted_iota(jnp.int32, (CAP, nodes_b), 1)
    points = [yield_ref[r] for r in range(CAP)]
    wanted = jnp.zeros((CAP, 1), jnp.int32)
    for r in range(CAP):
        wanted = jnp.where(cell_row == r, lax.rem(points[r], nodes_b), wanted)
    shift = []
    for c in range(3):
        rows = [strain_s[c, pl.ds(lax.div(points[r], nodes_b), 1), :] for r in range(CAP)]
        rows = jnp.concatenate(rows, axis=0)
        drive = jnp.sum(jnp.where(lane == wanted, rows, 0.0), axis=1, keepdims=True)
        drive = drive - means[c]
        shift.append(jnp.concatenate([drive, drive], axis=0))

    low = lax.rem(lax.broadcasted_iota(jnp.int32, (16, PLANE), 1), G)

    def advance(i, sweep):
        at = pl.multiple_of(i * 16, 16)
        e = [e_s[c, pl.ds(at, 16), :] for c in range(3)]
        if sweep == 0:
            e = [e[c] + shift[c] for c in range(3)]
        else:
            middle = f_s[pl.ds(at + 8, 16), :]
            e[0] = e[0] + 0.5 * (f_s[pl.ds(at + 16, 16), :] - f_s[pl.ds(at, 16), :])
            e[1] = e[1] + 0.5 * diff_upper(middle)
            e[2] = e[2] + 0.5 * diff_lower(middle, low)
        size = e[0] * e[0] + e[1] * e[1] + e[2] * e[2]
        factor = w_s[pl.ds(at, 16), :] * (1.5 - 0.5 / (1.0 + size))
        return at, e, [factor * v for v in e]

    def parts(v):
        high = v.astype(BF16)
        return high, (v - high.astype(F32)).astype(BF16)

    def lines(v):
        high, rest = parts(v)
        both = jnp.dot(line_ref[...], high, preferred_element_type=F32)
        n = G * CAP
        return both[:n] + both[n:] + jnp.dot(line_ref[0:n, :], rest, preferred_element_type=F32)

    def planes(both):
        n = G * CAP
        out = jnp.dot(both, plane_hi_ref[...], preferred_element_type=F32)
        return out[:n] + out[n:] + jnp.dot(both[:n], plane_lo_ref[...], preferred_element_type=F32)

    for copy in loads[5:]:
        copy.wait()
    for sweep in range(SWEEPS):

        def law(i, carry, sweep=sweep):
            at, e, s = advance(i, sweep)
            for c in range(3):
                e_s[c, pl.ds(at, 16), :] = e[c]
            s_pad[pl.ds(at + 8, 16), :] = s[0]
            d_s[pl.ds(at, 16), :] = diff_upper(s[1]) + diff_lower(s[2], low)
            return carry

        lax.fori_loop(0, G // 2, law, 0)
        s_pad[0:8, :] = s_pad[G * 8 : G * 8 + 8, :]
        s_pad[G * 8 + 8 :, :] = s_pad[8:16, :]

        def source(i, carry):
            at = pl.multiple_of(i * 16, 16)
            v = 0.5 * (s_pad[pl.ds(at + 16, 16), :] - s_pad[pl.ds(at, 16), :] + d_s[pl.ds(at, 16), :])
            high, rest = parts(v)
            x_s[pl.ds(at, 16), :] = high
            x_s[pl.ds(G * CAP + at, 16), :] = rest
            return carry

        lax.fori_loop(0, G // 2, source, 0)
        spectrum = lines(planes(x_s[...]))
        weight = jnp.broadcast_to(weight_ref[...], (G, CAP, PLANE)).reshape(G * CAP, PLANE)
        back = lines(spectrum * weight)
        high, rest = parts(back)
        x_s[0 : G * CAP, :] = high
        x_s[G * CAP :, :] = rest
        f_s[8 : G * 8 + 8, :] = planes(x_s[...])
        f_s[0:8, :] = f_s[G * 8 : G * 8 + 8, :]
        f_s[G * 8 + 8 :, :] = f_s[8:16, :]

    def finish(i, sums):
        at, e, s = advance(i, SWEEPS)
        out = []
        for c in range(3):
            wide = jnp.concatenate([e[c][0:8], e[c][8:16]], axis=1)
            for t in range(2 * PLANE // 128):
                row = pl.multiple_of((c * (VOX // 128) + i * 9 + t) * CAP, CAP)
                cells[pl.ds(row, CAP), :] = wide[:, 128 * t : 128 * t + 128]
            out.append(sums[c] + s[c][0:8] + s[c][8:16])
        return tuple(out)

    sums = lax.fori_loop(0, G // 2, finish, (zero, zero, zero))
    point_stress = [jnp.sum(s, axis=1, keepdims=True) * (1.0 / VOX) for s in sums]

    stiff = stiff_ref[...]
    e11, e22, e12 = strain_s[0], strain_s[1], strain_s[2]
    stress = [
        stiff * (e11 + POISSON * e22),
        stiff * (e22 + POISSON * e11),
        stiff * (1.0 - POISSON) * e12,
    ]
    node = lax.broadcasted_iota(jnp.int32, stiff.shape, 0) * nodes_b + lax.broadcasted_iota(jnp.int32, stiff.shape, 1)
    for r in range(CAP):
        here = node == points[r]
        for c in range(3):
            stress[c] = jnp.where(here, point_stress[c][r : r + 1, :], stress[c])
    s11, s22, s12 = stress
    gz, bz = slopes[2], slopes[5]
    t1 = s11 * gz + s12 * bz
    t2 = s12 * gz + s22 * bz
    over_gore, over_band = [s11, s12, t1], [s12, s22, t2]
    for c in range(3):
        halo_g[2, c : c + 1, :] = over_gore[c][0:1]
        halo_g[3, c : c + 1, :] = over_gore[c][nodes_g - 1 :]
        halo_b[2, c : c + 1, :] = to_row(over_band[c][:, 0:1])
        halo_b[3, c : c + 1, :] = to_row(over_band[c][:, nodes_b - 1 :])
    second = halo_copies(1)
    for copy in second:
        copy.start()
    slopes[0] = s11
    slopes[1] = s12
    slopes[3] = s22
    slopes[4] = t1
    slopes[5] = t2

    cells[ROWS * CAP :, :] = jnp.zeros((PACK * CAP - ROWS * CAP, 128), F32)
    for r in range(CAP):

        def gather(m, carry, r=r):
            own[r, pl.ds(pl.multiple_of(m * 8, 8), 8), :] = cells[pl.ds(m * 64 + r, 8, stride=CAP), :]
            return carry

        lax.fori_loop(0, PACK // 8, gather, 0, unroll=True)
    keep = pltpu.make_async_copy(own, own_ref, local_sem.at[0])
    keep.start()
    to_scalars.wait()

    def at_index(row, position, bound):
        return jnp.clip(table[row, position] - 1, 0, bound - 1)

    def hop(semaphores, slot, source, place, ring_place, line_place, core_place):
        send, recv = semaphores
        return pltpu.make_async_remote_copy(
            src_ref=source, dst_ref=place, send_sem=send.at[slot], recv_sem=recv.at[slot],
            device_id=((ring_place * LINE + line_place) * CORE + core_place, b), device_id_type=MESH,
        )

    one, two, three = (hop1_send, hop1_recv), (hop2_send, hop2_recv), (share_send, share_recv)

    def ring_first(j):
        to = lax.rem(y + STEPS[j], RING)
        n = RING_FIRST
        return hop(one, j, send1.at[pl.ds(j * n, n)], ring_got.at[pl.ds(y * n, n)], to, z, 0)

    def line_first():
        return hop(one, 0, send1.at[pl.ds(0, LINE_FIRST)], line_got, y, 1 - z, 1)

    half = LINE_SECOND // 2

    def line_second(j):
        span = pl.ds(j * half, half)
        return hop(two, j, send2.at[span], final.at[pl.ds(FINAL_RING + j * half, half)], y, 1 - z, 0)

    def ring_second(j):
        to = lax.rem(y + STEPS[j], RING)
        n = RING_SECOND
        return hop(two, j, send2.at[pl.ds(j * n, n)], final.at[pl.ds(FINAL_LINE + y * n, n)], to, z, 1)

    def share_ring(j):
        if j == 0:
            return hop(three, 0, ring_got, final.at[pl.ds(0, FINAL_RING)], y, z, 1)
        span = final.at[pl.ds(FINAL_RING + (j - 1) * half, half)]
        return hop(three, j, span, span, y, z, 1)

    def share_line(j):
        from_y = y if j == 0 else lax.rem(y + RING - STEPS[j - 1], RING)
        span = final.at[pl.ds(FINAL_LINE + from_y * RING_SECOND, RING_SECOND)]
        return hop(three, j, span, span, y, z, 0)

    def share_line_in(j):
        from_y = y if j == 0 else lax.rem(y + RING - STEPS[j - 1], RING)
        span = final.at[pl.ds(FINAL_LINE + from_y * RING_SECOND, RING_SECOND)]
        return hop(three, j, span, span, y, z, 1)

    def share_ring_in(j):
        low, n = (0, FINAL_RING) if j == 0 else (FINAL_RING + (j - 1) * half, half)
        span = final.at[pl.ds(low, n)]
        return hop(three, j, span, span, y, z, 0)

    @pl.when(core == 0)
    def _():
        for j in range(RING):
            to = lax.rem(y + (STEPS[j] if j < 3 else 0), RING)

            def fill(p, carry, j=j, to=to):
                cell = at_index(0, to * RING_FIRST + p, CAP)
                for m in range(PACK // 8):
                    v = own[cell, 8 * m : 8 * m + 8, :]
                    if j < 3:
                        send1[j * RING_FIRST + p, 8 * m : 8 * m + 8, :] = v
                    else:
                        ring_got[y * RING_FIRST + p, 8 * m : 8 * m + 8, :] = v
                return carry

            lax.fori_loop(0, RING_FIRST, fill, 0)
            if j < 3:
                ring_first(j).start()

    @pl.when(core == 1)
    def _():
        def fill(p, carry):
            cell = at_index(0, p, CAP)
            for m in range(PACK // 8):
                send1[p, 8 * m : 8 * m + 8, :] = own[cell, 8 * m : 8 * m + 8, :]
            return carry

        lax.fori_loop(0, LINE_FIRST, fill, 0)
        line_first().start()

    for copy in second:
        copy.wait()
    edge = []
    for c in range(3):
        before = jnp.where(inner_left, to_column(got_b[3, c : c + 1, :]), 0.0)
        after = jnp.where(inner_right, to_column(got_b[2, c : c + 1, :]), 0.0)
        edge.append((before, after))
    pairs = ((0, 1), (1, 3), (4, 5))
    for c, (p, q) in enumerate(pairs):
        value = gore_diff(slopes[p], got_g[3, c : c + 1, :], got_g[2, c : c + 1, :])
        value = value + band_diff(slopes[q], *edge[c])
        if c == 2:
            value = value + press_ref[...]
        force_ref[c] = value
    for d in range(1, n_band):
        flag_copy(d).wait()
    total = flag[...]
    for d in range(1, n_band):
        total = total + flag_got[lax.rem(b + d, n_band)]
    flag_ref[...] = total

    @pl.when(core == 0)
    def _():
        for j in range(3):
            ring_first(j).wait()
        for j in range(2):

            def fill(p, carry):
                cell = at_index(1, p, FINAL_RING)
                for m in range(PACK // 8):
                    send2[p, 8 * m : 8 * m + 8, :] = ring_got[cell, 8 * m : 8 * m + 8, :]
                return carry

            lax.fori_loop(j * half, (j + 1) * half, fill, 0)
            line_second(j).start()
        share_ring(0).start()
        stay = pltpu.make_async_copy(ring_got, final.at[pl.ds(0, FINAL_RING)], local_sem.at[1])
        stay.start()
        for j in range(2):
            line_second(j).wait()
            share_ring(1 + j).start()
        stay.wait()
        for j in range(3):
            share_ring(j).wait_send()
        for j in range(4):
            share_line_in(j).wait_recv()

    @pl.when(core == 1)
    def _():
        line_first().wait()
        for j in range(4):
            to = lax.rem(y + (STEPS[j] if j < 3 else 0), RING)

            def fill(p, carry, j=j, to=to):
                index = at_index(1, to * RING_SECOND + p, 2 * CAP)
                mine = index < CAP
                here, there = jnp.minimum(index, CAP - 1), jnp.maximum(index - CAP, 0)
                for m in range(PACK // 8):
                    v = jnp.where(mine, own[here, 8 * m : 8 * m + 8, :], line_got[there, 8 * m : 8 * m + 8, :])
                    if j < 3:
                        send2[j * RING_SECOND + p, 8 * m : 8 * m + 8, :] = v
                    else:
                        final[FINAL_LINE + y * RING_SECOND + p, 8 * m : 8 * m + 8, :] = v
                return carry

            lax.fori_loop(0, RING_SECOND, fill, 0)
            if j < 3:
                ring_second(j).start()
        share_line(0).start()
        for j in range(3):
            ring_second(j).wait()
            share_line(1 + j).start()
        for j in range(4):
            share_line(j).wait_send()
        for j in range(3):
            share_ring_in(j).wait_recv()

    stores = []
    for t in range(GROUP * MOST // 8):

        def choose(p, carry):
            filled = table[2, p] > 0
            cell = at_index(2, p, FINAL)
            for m in range(PACK // 8):
                chosen[p, 8 * m : 8 * m + 8, :] = jnp.where(filled, final[cell, 8 * m : 8 * m + 8, :], 0.0)
            return carry

        lax.fori_loop(8 * t, 8 * t + 8, choose, 0)
        span = pl.ds(8 * t, 8)
        stores.append(pltpu.make_async_copy(chosen.at[span], result_ref.at[span], out_sem.at[t]))
        stores[-1].start()
    keep.wait()
    for copy in stores:
        copy.wait()


def layout_kernel(slots, recv_ref, out_ref, got, made, in_sem, out_sem):
    tiles = VOX // 128
    spans = []
    for c in range(3):
        low = c * tiles // 8 * 8
        high = min(-(-(c + 1) * tiles // 8) * 8, PACK)
        spans.append((low, high))
    loads = []
    for c, (low, high) in enumerate(spans):
        place = got.at[c, :, 0 : high - low, :]
        loads.append(pltpu.make_async_copy(recv_ref.at[:, low:high, :], place, in_sem.at[c]))
        loads[-1].start()
    stores = []
    for c, (low, _) in enumerate(spans):
        loads[c].wait()
        for t in range(slots // 8):

            def column(j, carry):
                v = got[c, 8 * t : 8 * t + 8, pl.ds(c * tiles - low + 4 * j, 4), :]
                for s in range(4):
                    made[c, 8 * t : 8 * t + 8, pl.ds(pl.multiple_of((4 * j + s) * 128, 128), 128)] = v[:, s, :]
                return carry

            lax.fori_loop(0, tiles // 4, column, 0)
        stores.append(pltpu.make_async_copy(made.at[c], out_ref.at[c], out_sem.at[c]))
        stores[-1].start()
    for copy in stores:
        copy.wait()


def fast_layout(slots, result):
    any_space = pl.BlockSpec(memory_space=pltpu.HBM)
    return pl.pallas_call(
        lambda *refs: layout_kernel(slots, *refs),
        out_shape=jax.ShapeDtypeStruct((3, slots, VOX), F32),
        in_specs=[any_space],
        out_specs=any_space,
        scratch_shapes=[
            pltpu.VMEM((3, slots, 120, 128), F32),
            pltpu.VMEM((3, slots, VOX), F32),
            pltpu.SemaphoreType.DMA((3,)),
            pltpu.SemaphoreType.DMA((3,)),
        ],
        compiler_params=pltpu.CompilerParams(vmem_limit_bytes=32 * 2**20),
        name="layout",
    )(result)


def send_all(workers, own, n_gore, slots):
    states = own[:, :ROWS].reshape(CAP, 3, VOX)
    onehot = (workers[:, None] == jnp.arange(n_gore, dtype=jnp.int32)[None, :]).astype(jnp.int32)
    earlier = jnp.cumsum(onehot, axis=0) - onehot
    slot_index = workers * MOST + jnp.sum(earlier * onehot, axis=1)
    outgoing = jnp.zeros((slots, 3, VOX), F32).at[slot_index].set(states)
    arrived = lax.all_to_all(
        outgoing.reshape(n_gore, MOST, 3, VOX), "gore", split_axis=0, concat_axis=0, tiled=True
    )
    return arrived.reshape(slots, 3, VOX).transpose(1, 0, 2)


def local(displacement, stiffness, pressure, yield_points, route, cell_state, weave):
    n_gore, n_band = lax.axis_size("gore"), lax.axis_size("band")
    slots = n_gore * MOST
    nodes_g, nodes_b = stiffness.shape
    plane_high, plane_low, line, weight = tables()
    vmem, hbm = pl.BlockSpec(memory_space=pltpu.VMEM), pl.BlockSpec(memory_space=pltpu.HBM)
    n = G * CAP
    vm, dma = pltpu.VMEM, pltpu.SemaphoreType.DMA
    workers = route.reshape(-1)
    force, flag, result, own = pl.pallas_call(
        lambda *refs: kernel(n_gore, n_band, *refs),
        out_shape=(
            jax.ShapeDtypeStruct((3, nodes_g, nodes_b), F32),
            jax.ShapeDtypeStruct((8, 128), jnp.int32),
            jax.ShapeDtypeStruct((slots, PACK, 128), F32),
            jax.ShapeDtypeStruct((CAP, PACK, 128), F32),
        ),
        in_specs=[hbm] * 11,
        out_specs=(vmem, vmem, hbm, hbm),
        scratch_shapes=[
            pltpu.SMEM((CAP,), jnp.int32),
            pltpu.SMEM((CAP,), jnp.int32),
            vm((3, nodes_g, nodes_b), F32),
            vm((nodes_g, nodes_b), F32),
            vm((nodes_g, nodes_b), F32),
            vm((3, CAP, VOX), F32),
            vm((VOX // 128, 128), F32),
            vm((PLANE, PLANE), BF16),
            vm((PLANE, PLANE), BF16),
            vm((2 * n, n), BF16),
            vm((G, 1, PLANE), F32),
            vm((4, 8, nodes_b), F32),
            vm((4, 8, nodes_g), F32),
            vm((4, 8, nodes_b), F32),
            vm((4, 8, nodes_g), F32),
            vm((6, nodes_g, nodes_b), F32),
            vm((3, nodes_g, nodes_b), F32),
            vm((3, n, PLANE), F32),
            vm((n, PLANE), F32),
            vm((n + 16, PLANE), F32),
            vm((n, PLANE), F32),
            vm((2 * n, PLANE), BF16),
            vm((n + 16, PLANE), F32),
            vm((PACK * CAP, 128), F32),
            vm((8, 128), jnp.int32),
            vm((n_gore, 8, 128), jnp.int32),
            vm((8, 128), jnp.int32),
            vm((n_band, 8, 128), jnp.int32),
            vm((8, 128), jnp.int32),
            pltpu.SMEM((8, 128), jnp.int32),
            vm((CAP, PACK, 128), F32),
            vm((3 * RING_FIRST, PACK, 128), F32),
            vm((3 * RING_SECOND, PACK, 128), F32),
            vm((FINAL_RING, PACK, 128), F32),
            vm((LINE_FIRST, PACK, 128), F32),
            vm((FINAL, PACK, 128), F32),
            vm((slots, PACK, 128), F32),
            dma((11,)),
            dma((8,)),
            dma((8,)),
            dma((n_gore,)),
            dma((n_gore,)),
            dma((n_band,)),
            dma((n_band,)),
            dma,
            dma((3,)),
            dma((3,)),
            dma((3,)),
            dma((3,)),
            dma((4,)),
            dma((4,)),
            dma((2,)),
            dma((slots // 8,)),
        ],
        compiler_params=pltpu.CompilerParams(
            collective_id=0, has_side_effects=True, vmem_limit_bytes=56 * 2**20
        ),
        name="cells",
    )(
        yield_points,
        workers,
        displacement,
        stiffness,
        pressure,
        cell_state.transpose(1, 0, 2),
        weave.reshape(VOX // 128, 128),
        jnp.asarray(plane_high),
        jnp.asarray(plane_low),
        jnp.asarray(line),
        jnp.asarray(weight),
    )
    cell_strain = lax.cond(
        flag[0, 0] == 0,
        lambda result, own, workers: fast_layout(slots, result),
        lambda result, own, workers: send_all(workers, own, n_gore, slots),
        result, own, workers,
    )
    return force, cell_strain.transpose(1, 0, 2)


def solution(mesh):
    return jax.shard_map(
        local,
        mesh=mesh,
        in_specs=(
            P(None, "gore", "band"),
            P("gore", "band"),
            P("gore", "band"),
            P(("gore", "band")),
            P(("gore", "band"), None),
            P(("gore", "band"), None, None),
            P(),
        ),
        out_specs=(P(None, "gore", "band"), P(("gore", "band"), None, None)),
        check_vma=False,
    )
```

```python
import math

import jax
import jax.numpy as jnp
import numpy as np
from jax import lax
from jax.experimental import pallas as pl
from jax.experimental.pallas import tpu as pltpu
from jax.sharding import PartitionSpec as P

G = 24
PLANE = G * G
VOX = G * G * G
SWEEPS = 2
POISSON = 0.3
CAP = 8
MOST = 2
ROWS = 3 * VOX // 128
PACK = 328
RING, LINE, CORE = 4, 2, 2
GROUP = RING * LINE * CORE
RING_FIRST, LINE_SECOND, LINE_FIRST, RING_SECOND = 5, 10, 8, 6
STEPS = (1, 3, 2)
FINAL_RING = RING * RING_FIRST
FINAL_LINE = FINAL_RING + LINE_SECOND
FINAL = FINAL_LINE + RING * RING_SECOND
MESH = pl.DeviceIdType.MESH
F32 = jnp.float32
BF16 = jnp.bfloat16


def tables():
    n = np.arange(G)
    phase = 2.0 * np.pi * (np.outer(n, n) % G) / G
    hartley = (np.cos(phase) + np.sin(phase)) / math.sqrt(G)
    plane = np.kron(hartley, hartley)
    line = np.kron(hartley, np.eye(CAP))

    def split(a):
        high = a.astype(np.float32).astype(jnp.bfloat16)
        low = (a - high.astype(np.float64)).astype(np.float32).astype(jnp.bfloat16)
        return high, low

    square = np.sin(phase[1]) ** 2
    summed = square[:, None, None] + square[None, :, None] + square[None, None, :]
    level = n % (G // 2) == 0
    silent = level[:, None, None] & level[None, :, None] & level[None, None, :]
    weight = np.where(silent, 0.0, 1.0 / (10.0 * np.where(silent, 1.0, summed)))
    plane_high, plane_low = split(plane)
    line_high, line_low = split(line)
    return (
        plane_high,
        plane_low,
        np.concatenate([line_high, line_low], axis=0),
        weight.reshape(G, 1, PLANE).astype(np.float32),
    )


def shifted(v, k):
    k = k % v.shape[1]
    return jnp.concatenate([v[:, k:], v[:, :k]], axis=1)


def diff_upper(v):
    return shifted(v, G) - shifted(v, -G)


def diff_lower(v, low):
    forward = jnp.where(low == G - 1, shifted(v, 1 - G), shifted(v, 1))
    backward = jnp.where(low == 0, shifted(v, G - 1), shifted(v, -1))
    return forward - backward


def to_row(column):
    n = column.shape[0]
    diagonal = lax.broadcasted_iota(jnp.int32, (n, n), 0) == lax.broadcasted_iota(jnp.int32, (n, n), 1)
    return jnp.sum(jnp.where(diagonal, column, 0.0), axis=0, keepdims=True)


def to_column(row):
    n = row.shape[1]
    diagonal = lax.broadcasted_iota(jnp.int32, (n, n), 0) == lax.broadcasted_iota(jnp.int32, (n, n), 1)
    return jnp.sum(jnp.where(diagonal, row, 0.0), axis=1, keepdims=True)


def gore_diff(v, before, after):
    down = jnp.concatenate([v[1:], after], axis=0)
    up = jnp.concatenate([before, v[:-1]], axis=0)
    return (down - up) * 0.5


def band_diff(v, before, after):
    right = jnp.concatenate([v[:, 1:], after], axis=1)
    left = jnp.concatenate([before, v[:, :-1]], axis=1)
    return (right - left) * 0.5


def rank_of(key, key_column, earlier):
    return jnp.sum(jnp.where((key_column == key) & earlier, 1.0, 0.0), axis=0, keepdims=True)


def routing(worker, g):
    n = GROUP * CAP
    lane = lax.broadcasted_iota(jnp.int32, (1, n), 1)
    to = worker.astype(jnp.int32)
    source = lane >> 3
    to_y, to_z = to >> 2, (to >> 1) & 1
    from_y, from_z, from_c = source >> 2, (source >> 1) & 1, source & 1
    y, z, c = g >> 2, (g >> 1) & 1, g & 1
    crossing, first = to_z != from_z, from_c == 0
    alone = -1 - lane
    earlier = lax.broadcasted_iota(jnp.int32, (n, n), 0) < lax.broadcasted_iota(jnp.int32, (n, n), 1)

    def rank(key):
        key = key.astype(F32)
        return rank_of(key, to_column(key), earlier).astype(jnp.int32)

    own, mine = source == g, from_c == c
    at_ring = c == 0
    cell = lane & 7
    column = lax.broadcasted_iota(jnp.int32, (n, n), 1).astype(F32)

    def listing(place, index):
        place, index = to_column(place.astype(F32)), to_column(index.astype(F32) + 1.0)
        return jnp.sum(jnp.where(place == column, index, 0.0), axis=0, keepdims=True).astype(jnp.int32)

    ring_first = rank(source * RING + to_y)
    line_first = rank(jnp.where(crossing, source, alone))
    place1_ring = jnp.where(own, to_y * RING_FIRST + ring_first, -1)
    place1 = jnp.where(at_ring, place1_ring, jnp.where(own & crossing, line_first, -1))

    def later():
        line_second = rank(jnp.where(first & crossing, from_z * RING + to_y, alone))
        ring_second = rank(jnp.where(first, alone, (from_y * RING + to_y) * LINE + to_z))
        slot = rank(source * GROUP + to)
        over = first & ((ring_first >= RING_FIRST) | (crossing & (line_second >= LINE_SECOND)))
        over = over | (jnp.logical_not(first) & (ring_second >= RING_SECOND))
        place2_ring = jnp.where(mine & crossing & (from_z == z) & (to_y == y), line_second, -1)
        place2_line = jnp.where(mine & (from_y == y) & (to_z == z), to_y * RING_SECOND + ring_second, -1)
        place2 = jnp.where(at_ring, place2_ring, place2_line)
        from_ring = from_y * RING_FIRST + ring_first
        from_line = jnp.where(from_z == z, cell, CAP + line_first)
        index2 = jnp.where(at_ring, from_ring, from_line)
        place3 = jnp.where(to == g, source * MOST + slot, -1)
        index3 = jnp.where(crossing, FINAL_RING + line_second, from_ring)
        index3 = jnp.where(first, index3, FINAL_LINE + from_y * RING_SECOND + ring_second)
        over = jnp.sum(jnp.where(over, 1.0, 0.0), axis=1, keepdims=True)
        return listing(place2, index2), listing(place3, index3), over

    return listing(place1, cell), later


def kernel(
    n_gore, n_band,
    yield_hbm, route_hbm, disp_hbm, stiff_hbm, press_hbm, state_hbm, weave_hbm,
    plane_hi_hbm, plane_lo_hbm, line_hbm, weight_hbm,
    force_ref, flag_ref, table_ref, final, own_ref,
    yield_ref, route_ref, disp_ref, stiff_ref, press_ref, state_ref, weave_ref,
    plane_hi_ref, plane_lo_ref, line_ref, weight_ref,
    halo_g, halo_b, got_g, got_b, slopes, strain_s,
    e_s, w_s, s_pad, d_s, x_s, f_s, cells,
    names, names_got, flag, flag_got, hop1_v, hop1_table, table_v, table,
    own, send1, send2, ring_got, line_got, here_got,
    in_sem, halo_send, halo_recv, name_send, name_recv, flag_send, flag_recv, table_sem,
    hop1_send, hop1_recv, hop2_send, hop2_recv, share_send, share_recv, local_sem,
):
    g, b = lax.axis_index("gore"), lax.axis_index("band")
    y, z, core = lax.div(g, LINE * CORE), lax.rem(lax.div(g, CORE), LINE), lax.rem(g, CORE)
    up, down = lax.rem(g + 1, n_gore), lax.rem(g + n_gore - 1, n_gore)
    right, left = lax.rem(b + 1, n_band), lax.rem(b + n_band - 1, n_band)
    nodes_g, nodes_b = stiff_ref.shape

    barrier = pltpu.get_barrier_semaphore()
    for d in range(1, n_gore):
        pl.semaphore_signal(barrier, inc=1, device_id=(lax.rem(g + d, n_gore), b), device_id_type=MESH)
    for d in range(1, n_band):
        pl.semaphore_signal(barrier, inc=1, device_id=(g, lax.rem(b + d, n_band)), device_id_type=MESH)

    operands = (
        (route_hbm, route_ref), (disp_hbm, disp_ref), (yield_hbm, yield_ref), (state_hbm, state_ref),
        (weave_hbm, weave_ref), (stiff_hbm, stiff_ref), (plane_hi_hbm, plane_hi_ref),
        (plane_lo_hbm, plane_lo_ref), (line_hbm, line_ref), (weight_hbm, weight_ref), (press_hbm, press_ref),
    )
    loads = [pltpu.make_async_copy(p, q, in_sem.at[i]) for i, (p, q) in enumerate(operands)]
    for copy in loads:
        copy.start()

    def halo_copies(k):
        out = []
        for side, target in enumerate(((down, b), (up, b), (g, left), (g, right))):
            source, place = (halo_g, got_g) if side < 2 else (halo_b, got_b)
            out.append(
                pltpu.make_async_remote_copy(
                    src_ref=source.at[2 * k + side % 2],
                    dst_ref=place.at[2 * k + side % 2],
                    send_sem=halo_send.at[4 * k + side],
                    recv_sem=halo_recv.at[4 * k + side],
                    device_id=target,
                    device_id_type=MESH,
                )
            )
        return out

    def name_copy(d):
        return pltpu.make_async_remote_copy(
            src_ref=names, dst_ref=names_got.at[g], send_sem=name_send.at[d], recv_sem=name_recv.at[d],
            device_id=(lax.rem(g + d, n_gore), b), device_id_type=MESH,
        )

    def flag_copy(d):
        return pltpu.make_async_remote_copy(
            src_ref=flag, dst_ref=flag_got.at[b], send_sem=flag_send.at[d], recv_sem=flag_recv.at[d],
            device_id=(g, lax.rem(b + d, n_band)), device_id_type=MESH,
        )

    loads[0].wait()
    place = lax.broadcasted_iota(jnp.int32, (8, 128), 1)
    named = jnp.zeros((8, 128), jnp.int32)
    for r in range(CAP):
        named = jnp.where(place == g * CAP + r, route_ref[r], named)
    names[...] = named
    loads[1].wait()
    for c in range(3):
        v = disp_ref[c]
        halo_g[0, c : c + 1, :] = v[0:1]
        halo_g[1, c : c + 1, :] = v[nodes_g - 1 :]
        halo_b[0, c : c + 1, :] = to_row(v[:, 0:1])
        halo_b[1, c : c + 1, :] = to_row(v[:, nodes_b - 1 :])
    pl.semaphore_wait(barrier, n_gore + n_band - 2)
    first = halo_copies(0)
    for copy in first:
        copy.start()
    for d in range(1, n_gore):
        name_copy(d).start()

    loads[3].wait()
    loads[4].wait()

    def load_states(i, sums):
        at = pl.multiple_of(i * 16, 16)
        out = []
        for c in range(3):
            pair = state_ref[c, :, pl.ds(pl.multiple_of(i * 2 * PLANE, 128), 2 * PLANE)]
            even, odd = pair[:, :PLANE], pair[:, PLANE:]
            e_s[c, pl.ds(at, 16), :] = jnp.concatenate([even, odd], axis=0)
            out.append(sums[c] + even + odd)
        rows = [jnp.broadcast_to(weave_ref[pl.ds(i * 9 + t, 1), :], (CAP, 128)) for t in range(9)]
        pair = jnp.concatenate(rows, axis=1)
        w_s[pl.ds(at, 16), :] = jnp.concatenate([pair[:, :PLANE], pair[:, PLANE:]], axis=0)
        return tuple(out)

    zero = jnp.zeros((CAP, PLANE), F32)
    sums = lax.fori_loop(0, G // 2, load_states, (zero, zero, zero), unroll=2)
    means = [jnp.sum(s, axis=1, keepdims=True) * (1.0 / VOX) for s in sums]

    for d in range(1, n_gore):
        name_copy(d).wait()
    for copy in first:
        copy.wait()

    worker = names[0:1, :]
    for d in range(1, n_gore):
        worker = worker + names_got[lax.rem(g + d, n_gore), 0:1, :]
    hop1_v[...] = jnp.broadcast_to(routing(worker.astype(F32), g)[0], (8, 128))
    hop1_scalars = pltpu.make_async_copy(hop1_v, hop1_table, table_sem.at[0])
    hop1_scalars.start()

    inner_left, inner_right = b > 0, b < n_band - 1
    for c in range(3):
        v = disp_ref[c]
        before = jnp.where(inner_left, to_column(got_b[1, c : c + 1, :]), 0.0)
        after = jnp.where(inner_right, to_column(got_b[0, c : c + 1, :]), 0.0)
        slopes[c] = gore_diff(v, got_g[1, c : c + 1, :], got_g[0, c : c + 1, :])
        slopes[3 + c] = band_diff(v, before, after)
    gz, bz = slopes[2], slopes[5]
    strain_s[0] = slopes[0] + 0.5 * gz * gz
    strain_s[1] = slopes[4] + 0.5 * bz * bz
    strain_s[2] = 0.5 * (slopes[3] + slopes[1]) + 0.5 * gz * bz

    loads[2].wait()
    cell_row = lax.broadcasted_iota(jnp.int32, (CAP, 1), 0)
    lane = lax.broadcasted_iota(jnp.int32, (CAP, nodes_b), 1)
    points = [yield_ref[r] for r in range(CAP)]
    wanted = jnp.zeros((CAP, 1), jnp.int32)
    for r in range(CAP):
        wanted = jnp.where(cell_row == r, lax.rem(points[r], nodes_b), wanted)
    shift = []
    for c in range(3):
        rows = [strain_s[c, pl.ds(lax.div(points[r], nodes_b), 1), :] for r in range(CAP)]
        rows = jnp.concatenate(rows, axis=0)
        drive = jnp.sum(jnp.where(lane == wanted, rows, 0.0), axis=1, keepdims=True)
        drive = drive - means[c]
        shift.append(jnp.concatenate([drive, drive], axis=0))

    low = lax.rem(lax.broadcasted_iota(jnp.int32, (16, PLANE), 1), G)

    def advance(i, sweep):
        at = pl.multiple_of(i * 16, 16)
        e = [e_s[c, pl.ds(at, 16), :] for c in range(3)]
        if sweep == 0:
            e = [e[c] + shift[c] for c in range(3)]
        else:
            middle = f_s[pl.ds(at + 8, 16), :]
            e[0] = e[0] + 0.5 * (f_s[pl.ds(at + 16, 16), :] - f_s[pl.ds(at, 16), :])
            e[1] = e[1] + 0.5 * diff_upper(middle)
            e[2] = e[2] + 0.5 * diff_lower(middle, low)
        size = e[0] * e[0] + e[1] * e[1] + e[2] * e[2]
        factor = w_s[pl.ds(at, 16), :] * (1.5 - 0.5 / (1.0 + size))
        return at, e, [factor * v for v in e]

    def parts(v):
        high = v.astype(BF16)
        return high, (v - high.astype(F32)).astype(BF16)

    def lines(v):
        high, rest = parts(v)
        both = jnp.dot(line_ref[...], high, preferred_element_type=F32)
        n = G * CAP
        return both[:n] + both[n:] + jnp.dot(line_ref[0:n, :], rest, preferred_element_type=F32)

    def planes(both):
        n = G * CAP
        out = jnp.dot(both, plane_hi_ref[...], preferred_element_type=F32)
        return out[:n] + out[n:] + jnp.dot(both[:n], plane_lo_ref[...], preferred_element_type=F32)

    for copy in loads[5:]:
        copy.wait()
    for sweep in range(SWEEPS):

        def law(i, carry, sweep=sweep):
            at, e, s = advance(i, sweep)
            for c in range(3):
                e_s[c, pl.ds(at, 16), :] = e[c]
            s_pad[pl.ds(at + 8, 16), :] = s[0]
            d_s[pl.ds(at, 16), :] = diff_upper(s[1]) + diff_lower(s[2], low)
            return carry

        lax.fori_loop(0, G // 2, law, 0, unroll=6)
        s_pad[0:8, :] = s_pad[G * 8 : G * 8 + 8, :]
        s_pad[G * 8 + 8 :, :] = s_pad[8:16, :]

        def source(i, carry):
            at = pl.multiple_of(i * 16, 16)
            v = 0.5 * (s_pad[pl.ds(at + 16, 16), :] - s_pad[pl.ds(at, 16), :] + d_s[pl.ds(at, 16), :])
            high, rest = parts(v)
            x_s[pl.ds(at, 16), :] = high
            x_s[pl.ds(G * CAP + at, 16), :] = rest
            return carry

        lax.fori_loop(0, G // 2, source, 0, unroll=6)
        spectrum = lines(planes(x_s[...]))
        weight = jnp.broadcast_to(weight_ref[...], (G, CAP, PLANE)).reshape(G * CAP, PLANE)
        back = lines(spectrum * weight)
        high, rest = parts(back)
        x_s[0 : G * CAP, :] = high
        x_s[G * CAP :, :] = rest
        f_s[8 : G * 8 + 8, :] = planes(x_s[...])
        f_s[0:8, :] = f_s[G * 8 : G * 8 + 8, :]
        f_s[G * 8 + 8 :, :] = f_s[8:16, :]

    def finish(i, sums):
        at, e, s = advance(i, SWEEPS)
        out = []
        for c in range(3):
            wide = jnp.concatenate([e[c][0:8], e[c][8:16]], axis=1)
            for t in range(2 * PLANE // 128):
                row = pl.multiple_of((c * (VOX // 128) + i * 9 + t) * CAP, CAP)
                cells[pl.ds(row, CAP), :] = wide[:, 128 * t : 128 * t + 128]
            out.append(sums[c] + s[c][0:8] + s[c][8:16])
        return tuple(out)

    sums = lax.fori_loop(0, G // 2, finish, (zero, zero, zero), unroll=2)
    point_stress = [jnp.sum(s, axis=1, keepdims=True) * (1.0 / VOX) for s in sums]

    cells[ROWS * CAP :, :] = jnp.zeros((PACK * CAP - ROWS * CAP, 128), F32)
    hop1_scalars.wait()

    def at_index(table, row, position, bound):
        return jnp.clip(table[row, position] - 1, 0, bound - 1)

    def tiles_of(cell, m):
        return cells[pl.ds(m * 64 + cell, 8, stride=CAP), :]

    def hop(semaphores, slot, source, place, ring_place, line_place, core_place):
        send, recv = semaphores
        return pltpu.make_async_remote_copy(
            src_ref=source, dst_ref=place, send_sem=send.at[slot], recv_sem=recv.at[slot],
            device_id=((ring_place * LINE + line_place) * CORE + core_place, b), device_id_type=MESH,
        )

    one, two, three = (hop1_send, hop1_recv), (hop2_send, hop2_recv), (share_send, share_recv)

    def ring_first(j):
        to = lax.rem(y + STEPS[j], RING)
        n = RING_FIRST
        return hop(one, j, send1.at[pl.ds(j * n, n)], ring_got.at[pl.ds(y * n, n)], to, z, 0)

    def line_first():
        return hop(one, 0, send1.at[pl.ds(0, LINE_FIRST)], line_got, y, 1 - z, 1)

    half = LINE_SECOND // 2

    def line_second(j):
        span = pl.ds(j * half, half)
        return hop(two, j, send2.at[span], final.at[pl.ds(FINAL_RING + j * half, half)], y, 1 - z, 0)

    def ring_second(j):
        to = lax.rem(y + STEPS[j], RING)
        n = RING_SECOND
        return hop(two, j, send2.at[pl.ds(j * n, n)], final.at[pl.ds(FINAL_LINE + y * n, n)], to, z, 1)

    def share_ring(j):
        if j == 0:
            return hop(three, 0, ring_got, final.at[pl.ds(0, FINAL_RING)], y, z, 1)
        span = final.at[pl.ds(FINAL_RING + (j - 1) * half, half)]
        return hop(three, j, span, span, y, z, 1)

    def share_line(j):
        from_y = y if j == 0 else lax.rem(y + RING - STEPS[j - 1], RING)
        span = final.at[pl.ds(FINAL_LINE + from_y * RING_SECOND, RING_SECOND)]
        return hop(three, j, here_got if j == 0 else span, span, y, z, 0)

    def share_line_in(j):
        from_y = y if j == 0 else lax.rem(y + RING - STEPS[j - 1], RING)
        span = final.at[pl.ds(FINAL_LINE + from_y * RING_SECOND, RING_SECOND)]
        return hop(three, j, span, span, y, z, 1)

    def share_ring_in(j):
        low, n = (0, FINAL_RING) if j == 0 else (FINAL_RING + (j - 1) * half, half)
        span = final.at[pl.ds(low, n)]
        return hop(three, j, span, span, y, z, 0)

    @pl.when(core == 0)
    def _():
        for j in range(RING):
            to = lax.rem(y + (STEPS[j] if j < 3 else 0), RING)

            def fill(p, carry, j=j, to=to):
                cell = at_index(hop1_table, 0, to * RING_FIRST + p, CAP)
                for m in range(PACK // 8):
                    v = tiles_of(cell, m)
                    if j < 3:
                        send1[j * RING_FIRST + p, 8 * m : 8 * m + 8, :] = v
                    else:
                        ring_got[y * RING_FIRST + p, 8 * m : 8 * m + 8, :] = v
                return carry

            lax.fori_loop(0, RING_FIRST, fill, 0)
            if j < 3:
                ring_first(j).start()

    @pl.when(core == 1)
    def _():
        def fill(p, carry):
            cell = at_index(hop1_table, 0, p, CAP)
            for m in range(PACK // 8):
                send1[p, 8 * m : 8 * m + 8, :] = tiles_of(cell, m)
            return carry

        lax.fori_loop(0, LINE_FIRST, fill, 0)
        line_first().start()

    list2, list3, over = routing(worker.astype(F32), g)[1]()
    table_v[0:1, :] = list2
    table_v[1:2, :] = list3
    to_scalars = pltpu.make_async_copy(table_v, table, table_sem.at[1])
    to_scalars.start()
    hand_on = pltpu.make_async_copy(table_v, table_ref, table_sem.at[2])
    hand_on.start()
    flag[...] = jnp.broadcast_to(over, (8, 128)).astype(jnp.int32)
    for d in range(1, n_band):
        flag_copy(d).start()
    for r in range(CAP):

        def gather(m, carry, r=r):
            own[r, pl.ds(pl.multiple_of(m * 8, 8), 8), :] = cells[pl.ds(m * 64 + r, 8, stride=CAP), :]
            return carry

        lax.fori_loop(0, PACK // 8, gather, 0, unroll=True)
    keep = pltpu.make_async_copy(own, own_ref, local_sem.at[0])
    keep.start()

    stiff = stiff_ref[...]
    e11, e22, e12 = strain_s[0], strain_s[1], strain_s[2]
    stress = [
        stiff * (e11 + POISSON * e22),
        stiff * (e22 + POISSON * e11),
        stiff * (1.0 - POISSON) * e12,
    ]
    node = lax.broadcasted_iota(jnp.int32, stiff.shape, 0) * nodes_b + lax.broadcasted_iota(jnp.int32, stiff.shape, 1)
    for r in range(CAP):
        here = node == points[r]
        for c in range(3):
            stress[c] = jnp.where(here, point_stress[c][r : r + 1, :], stress[c])
    s11, s22, s12 = stress
    gz, bz = slopes[2], slopes[5]
    t1 = s11 * gz + s12 * bz
    t2 = s12 * gz + s22 * bz
    over_gore, over_band = [s11, s12, t1], [s12, s22, t2]
    for c in range(3):
        halo_g[2, c : c + 1, :] = over_gore[c][0:1]
        halo_g[3, c : c + 1, :] = over_gore[c][nodes_g - 1 :]
        halo_b[2, c : c + 1, :] = to_row(over_band[c][:, 0:1])
        halo_b[3, c : c + 1, :] = to_row(over_band[c][:, nodes_b - 1 :])
    second = halo_copies(1)
    for copy in second:
        copy.start()
    slopes[0] = s11
    slopes[1] = s12
    slopes[3] = s22
    slopes[4] = t1
    slopes[5] = t2

    to_scalars.wait()

    def stay_here():
        span = pl.ds(FINAL_LINE + y * RING_SECOND, RING_SECOND)
        return pltpu.make_async_copy(here_got, final.at[span], local_sem.at[1])

    def stay():
        return pltpu.make_async_copy(ring_got, final.at[pl.ds(0, FINAL_RING)], local_sem.at[1])

    @pl.when(core == 0)
    def _():
        for j in range(3):
            ring_first(j).wait()
        for j in range(2):

            def fill(p, carry):
                cell = at_index(table, 0, p, FINAL_RING)
                for m in range(PACK // 8):
                    send2[p, 8 * m : 8 * m + 8, :] = ring_got[cell, 8 * m : 8 * m + 8, :]
                return carry

            lax.fori_loop(j * half, (j + 1) * half, fill, 0)
            line_second(j).start()
        share_ring(0).start()
        stay().start()

    @pl.when(core == 1)
    def _():
        line_first().wait()
        for j in range(4):
            to = lax.rem(y + (STEPS[j] if j < 3 else 0), RING)

            def fill(p, carry, j=j, to=to):
                index = at_index(table, 0, to * RING_SECOND + p, 2 * CAP)
                mine = index < CAP
                here, there = jnp.minimum(index, CAP - 1), jnp.maximum(index - CAP, 0)
                for m in range(PACK // 8):
                    v = jnp.where(mine, own[here, 8 * m : 8 * m + 8, :], line_got[there, 8 * m : 8 * m + 8, :])
                    if j < 3:
                        send2[j * RING_SECOND + p, 8 * m : 8 * m + 8, :] = v
                    else:
                        here_got[p, 8 * m : 8 * m + 8, :] = v
                return carry

            lax.fori_loop(0, RING_SECOND, fill, 0)
            if j < 3:
                ring_second(j).start()
        share_line(0).start()
        stay_here().start()

    for copy in second:
        copy.wait()
    edge = []
    for c in range(3):
        before = jnp.where(inner_left, to_column(got_b[3, c : c + 1, :]), 0.0)
        after = jnp.where(inner_right, to_column(got_b[2, c : c + 1, :]), 0.0)
        edge.append((before, after))
    pairs = ((0, 1), (1, 3), (4, 5))
    for c, (p, q) in enumerate(pairs):
        value = gore_diff(slopes[p], got_g[3, c : c + 1, :], got_g[2, c : c + 1, :])
        value = value + band_diff(slopes[q], *edge[c])
        if c == 2:
            value = value + press_ref[...]
        force_ref[c] = value
    @pl.when(core == 0)
    def _():
        for j in range(2):
            line_second(j).wait()
            share_ring(1 + j).start()
        stay().wait()
        for j in range(3):
            share_ring(j).wait_send()
        for j in range(4):
            share_line_in(j).wait_recv()

    @pl.when(core == 1)
    def _():
        for j in range(3):
            ring_second(j).wait()
            share_line(1 + j).start()
        stay_here().wait()
        for j in range(4):
            share_line(j).wait_send()
        for j in range(3):
            share_ring_in(j).wait_recv()

    for d in range(1, n_band):
        flag_copy(d).wait()
    total = flag[...]
    for d in range(1, n_band):
        total = total + flag_got[lax.rem(b + d, n_band)]
    flag_ref[0] = jnp.sum(total[0:1, :].astype(F32)).astype(jnp.int32)

    keep.wait()
    hand_on.wait()


def place_kernel(table, final, result, got, made, in_sem, out_sem):
    tiles, groups = VOX // 128, GROUP * MOST // 8

    def load(p):
        cell = jnp.clip(table[1, p] - 1, 0, FINAL - 1)
        return pltpu.make_async_copy(final.at[cell], got.at[p], in_sem.at[p])

    for p in range(GROUP * MOST):

        @pl.when(table[1, p] > 0)
        def _(p=p):
            load(p).start()

    def clear(i, carry):
        made[pl.ds(pl.multiple_of(i * 216, 216), 216), :] = jnp.zeros((216, 128), F32)
        return carry

    lax.fori_loop(0, 3 * groups * tiles * 8 // 216, clear, 0)

    def one(p, carry):
        @pl.when(table[1, p] > 0)
        def _():
            load(p).wait()
            for m in range(PACK // 8):
                v = got[p, 8 * m : 8 * m + 8, :]
                row = 8 * m
                while row < min(8 * m + 8, ROWS):
                    c, tile = row // tiles, row % tiles
                    count = min(8 * m + 8, (c + 1) * tiles) - row
                    start = ((c * groups + p // 8) * tiles + tile) * 8 + p % 8
                    made[pl.ds(start, count, stride=8), :] = v[row - 8 * m : row - 8 * m + count]
                    row = row + count

        return carry

    stores = []
    for t in range(groups):
        lax.fori_loop(8 * t, 8 * t + 8, one, 0)
        for c in range(3):
            span = pl.ds((c * groups + t) * tiles * 8, tiles * 8)
            stores.append(pltpu.make_async_copy(made.at[span], result.at[span], out_sem.at[3 * t + c]))
            stores[-1].start()
    for copy in stores:
        copy.wait()


def place(table, final):
    hbm = pl.BlockSpec(memory_space=pltpu.HBM)
    slots = GROUP * MOST
    result = pl.pallas_call(
        place_kernel,
        out_shape=jax.ShapeDtypeStruct((3 * slots * VOX // 128, 128), F32),
        in_specs=[pl.BlockSpec(memory_space=pltpu.SMEM), hbm],
        out_specs=hbm,
        scratch_shapes=[
            pltpu.VMEM((slots, PACK, 128), F32),
            pltpu.VMEM((3 * slots * VOX // 128, 128), F32),
            pltpu.SemaphoreType.DMA((slots,)),
            pltpu.SemaphoreType.DMA((3 * slots // 8,)),
        ],
        compiler_params=pltpu.CompilerParams(vmem_limit_bytes=60 * 2**20),
        name="place",
    )(table, final)
    return in_place(slots, result)


def in_place(slots, result):
    tiles = result.reshape(3, slots // 8, VOX // 128, 8, 128)
    return tiles.transpose(0, 1, 3, 2, 4).reshape(3, slots, VOX)


def send_all(workers, own, n_gore, slots):
    states = own[:, :ROWS].reshape(CAP, 3, VOX)
    onehot = (workers[:, None] == jnp.arange(n_gore, dtype=jnp.int32)[None, :]).astype(jnp.int32)
    earlier = jnp.cumsum(onehot, axis=0) - onehot
    slot_index = workers * MOST + jnp.sum(earlier * onehot, axis=1)
    outgoing = jnp.zeros((slots, 3, VOX), F32).at[slot_index].set(states)
    arrived = lax.all_to_all(
        outgoing.reshape(n_gore, MOST, 3, VOX), "gore", split_axis=0, concat_axis=0, tiled=True
    )
    return arrived.reshape(slots, 3, VOX).transpose(1, 0, 2)


def local(displacement, stiffness, pressure, yield_points, route, cell_state, weave):
    n_gore, n_band = lax.axis_size("gore"), lax.axis_size("band")
    slots = n_gore * MOST
    nodes_g, nodes_b = stiffness.shape
    plane_high, plane_low, line, weight = tables()
    vmem, hbm = pl.BlockSpec(memory_space=pltpu.VMEM), pl.BlockSpec(memory_space=pltpu.HBM)
    n = G * CAP
    vm, dma = pltpu.VMEM, pltpu.SemaphoreType.DMA
    workers = route.reshape(-1)
    force, flag, table, final, own = pl.pallas_call(
        lambda *refs: kernel(n_gore, n_band, *refs),
        out_shape=(
            jax.ShapeDtypeStruct((3, nodes_g, nodes_b), F32),
            jax.ShapeDtypeStruct((1,), jnp.int32),
            jax.ShapeDtypeStruct((8, 128), jnp.int32),
            jax.ShapeDtypeStruct((FINAL, PACK, 128), F32),
            jax.ShapeDtypeStruct((CAP, PACK, 128), F32),
        ),
        in_specs=[hbm] * 11,
        out_specs=(vmem, pl.BlockSpec(memory_space=pltpu.SMEM), hbm, hbm, hbm),
        scratch_shapes=[
            pltpu.SMEM((CAP,), jnp.int32),
            pltpu.SMEM((CAP,), jnp.int32),
            vm((3, nodes_g, nodes_b), F32),
            vm((nodes_g, nodes_b), F32),
            vm((nodes_g, nodes_b), F32),
            vm((3, CAP, VOX), F32),
            vm((VOX // 128, 128), F32),
            vm((PLANE, PLANE), BF16),
            vm((PLANE, PLANE), BF16),
            vm((2 * n, n), BF16),
            vm((G, 1, PLANE), F32),
            vm((4, 8, nodes_b), F32),
            vm((4, 8, nodes_g), F32),
            vm((4, 8, nodes_b), F32),
            vm((4, 8, nodes_g), F32),
            vm((6, nodes_g, nodes_b), F32),
            vm((3, nodes_g, nodes_b), F32),
            vm((3, n, PLANE), F32),
            vm((n, PLANE), F32),
            vm((n + 16, PLANE), F32),
            vm((n, PLANE), F32),
            vm((2 * n, PLANE), BF16),
            vm((n + 16, PLANE), F32),
            vm((PACK * CAP, 128), F32),
            vm((8, 128), jnp.int32),
            vm((n_gore, 8, 128), jnp.int32),
            vm((8, 128), jnp.int32),
            vm((n_band, 8, 128), jnp.int32),
            vm((8, 128), jnp.int32),
            pltpu.SMEM((8, 128), jnp.int32),
            vm((8, 128), jnp.int32),
            pltpu.SMEM((8, 128), jnp.int32),
            vm((CAP, PACK, 128), F32),
            vm((3 * RING_FIRST, PACK, 128), F32),
            vm((3 * RING_SECOND, PACK, 128), F32),
            vm((FINAL_RING, PACK, 128), F32),
            vm((LINE_FIRST, PACK, 128), F32),
            vm((RING_SECOND, PACK, 128), F32),
            dma((11,)),
            dma((8,)),
            dma((8,)),
            dma((n_gore,)),
            dma((n_gore,)),
            dma((n_band,)),
            dma((n_band,)),
            dma((3,)),
            dma((3,)),
            dma((3,)),
            dma((3,)),
            dma((3,)),
            dma((4,)),
            dma((4,)),
            dma((2,)),
        ],
        compiler_params=pltpu.CompilerParams(
            collective_id=0, has_side_effects=True, vmem_limit_bytes=60 * 2**20
        ),
        name="cells",
    )(
        yield_points,
        workers,
        displacement,
        stiffness,
        pressure,
        cell_state.transpose(1, 0, 2),
        weave.reshape(VOX // 128, 128),
        jnp.asarray(plane_high),
        jnp.asarray(plane_low),
        jnp.asarray(line),
        jnp.asarray(weight),
    )
    cell_strain = lax.cond(
        flag[0] == 0,
        lambda table, final, own, workers: place(table, final),
        lambda table, final, own, workers: send_all(workers, own, n_gore, slots),
        table, final, own, workers,
    )
    return force, cell_strain.transpose(1, 0, 2)


def solution(mesh):
    return jax.shard_map(
        local,
        mesh=mesh,
        in_specs=(
            P(None, "gore", "band"),
            P("gore", "band"),
            P("gore", "band"),
            P(("gore", "band")),
            P(("gore", "band"), None),
            P(("gore", "band"), None, None),
            P(),
        ),
        out_specs=(P(None, "gore", "band"), P(("gore", "band"), None, None)),
        check_vma=False,
    )
```

```python
import math

import jax
import jax.numpy as jnp
import numpy as np
from jax import lax
from jax.experimental import pallas as pl
from jax.experimental.pallas import tpu as pltpu
from jax.sharding import PartitionSpec as P

G = 24
PLANE = G * G
VOX = G * G * G
SWEEPS = 2
POISSON = 0.3
CAP = 8
MOST = 2
ROWS = 3 * VOX // 128
PACK = 328
RING, LINE, CORE = 4, 2, 2
GROUP = RING * LINE * CORE
RING_FIRST, LINE_NEAR, LINE_FAR, LINE_FIRST, RING_SECOND = 5, 9, 3, 8, 6
STEPS = (1, 3, 2)
FINAL_RING = RING * RING_FIRST
FINAL_LINE = FINAL_RING + LINE_NEAR + LINE_FAR
NEAR = (RING - 1) * RING_FIRST
FINAL = FINAL_LINE + RING * RING_SECOND
MESH = pl.DeviceIdType.MESH
F32 = jnp.float32
BF16 = jnp.bfloat16


def tables():
    n = np.arange(G)
    phase = 2.0 * np.pi * (np.outer(n, n) % G) / G
    hartley = (np.cos(phase) + np.sin(phase)) / math.sqrt(G)
    plane = np.kron(hartley, hartley)
    line = np.kron(hartley, np.eye(CAP))

    def split(a):
        high = a.astype(np.float32).astype(jnp.bfloat16)
        low = (a - high.astype(np.float64)).astype(np.float32).astype(jnp.bfloat16)
        return high, low

    square = np.sin(phase[1]) ** 2
    summed = square[:, None, None] + square[None, :, None] + square[None, None, :]
    level = n % (G // 2) == 0
    silent = level[:, None, None] & level[None, :, None] & level[None, None, :]
    weight = np.where(silent, 0.0, 1.0 / (10.0 * np.where(silent, 1.0, summed)))
    plane_high, plane_low = split(plane)
    line_high, line_low = split(line)
    return (
        plane_high,
        plane_low,
        np.concatenate([line_high, line_low], axis=0),
        weight.reshape(G, 1, PLANE).astype(np.float32),
    )


def shifted(v, k):
    k = k % v.shape[1]
    return jnp.concatenate([v[:, k:], v[:, :k]], axis=1)


def diff_upper(v):
    return shifted(v, G) - shifted(v, -G)


def diff_lower(v, low):
    forward = jnp.where(low == G - 1, shifted(v, 1 - G), shifted(v, 1))
    backward = jnp.where(low == 0, shifted(v, G - 1), shifted(v, -1))
    return forward - backward


def to_row(column):
    n = column.shape[0]
    diagonal = lax.broadcasted_iota(jnp.int32, (n, n), 0) == lax.broadcasted_iota(jnp.int32, (n, n), 1)
    return jnp.sum(jnp.where(diagonal, column, 0.0), axis=0, keepdims=True)


def to_column(row):
    n = row.shape[1]
    diagonal = lax.broadcasted_iota(jnp.int32, (n, n), 0) == lax.broadcasted_iota(jnp.int32, (n, n), 1)
    return jnp.sum(jnp.where(diagonal, row, 0.0), axis=1, keepdims=True)


def gore_diff(v, before, after):
    down = jnp.concatenate([v[1:], after], axis=0)
    up = jnp.concatenate([before, v[:-1]], axis=0)
    return (down - up) * 0.5


def band_diff(v, before, after):
    right = jnp.concatenate([v[:, 1:], after], axis=1)
    left = jnp.concatenate([before, v[:, :-1]], axis=1)
    return (right - left) * 0.5


def rank_of(key, key_column, earlier):
    return jnp.sum(jnp.where((key_column == key) & earlier, 1.0, 0.0), axis=0, keepdims=True)


def routing(worker, g):
    n = GROUP * CAP
    lane = lax.broadcasted_iota(jnp.int32, (1, n), 1)
    to = worker.astype(jnp.int32)
    source = lane >> 3
    to_y, to_z = to >> 2, (to >> 1) & 1
    from_y, from_z, from_c = source >> 2, (source >> 1) & 1, source & 1
    y, z, c = g >> 2, (g >> 1) & 1, g & 1
    crossing, first = to_z != from_z, from_c == 0
    alone = -1 - lane
    earlier = lax.broadcasted_iota(jnp.int32, (n, n), 0) < lax.broadcasted_iota(jnp.int32, (n, n), 1)

    def rank(key):
        key = key.astype(F32)
        return rank_of(key, to_column(key), earlier).astype(jnp.int32)

    own, mine = source == g, from_c == c
    at_ring = c == 0
    cell = lane & 7
    column = lax.broadcasted_iota(jnp.int32, (n, n), 1).astype(F32)

    def listing(place, index):
        place, index = to_column(place.astype(F32)), to_column(index.astype(F32) + 1.0)
        return jnp.sum(jnp.where(place == column, index, 0.0), axis=0, keepdims=True).astype(jnp.int32)

    ahead = (from_y + RING - to_y) & (RING - 1)
    block = jnp.where(ahead == 3, 1, jnp.where(ahead == 1, 2, jnp.where(ahead == 2, 3, 0)))
    far = jnp.where(ahead == 2, 1, 0)
    ring_first = rank(source * RING + to_y)
    line_first = rank(jnp.where(crossing, source, alone))
    place1_ring = jnp.where(own, to_y * RING_FIRST + ring_first, -1)
    place1 = jnp.where(at_ring, place1_ring, jnp.where(own & crossing, line_first, -1))

    def later():
        line_second = rank(jnp.where(first & crossing, (from_z * RING + to_y) * 2 + far, alone))
        line_over = line_second >= LINE_NEAR + far * (LINE_FAR - LINE_NEAR)
        line_second = line_second + far * LINE_NEAR
        ring_second = rank(jnp.where(first, alone, (from_y * RING + to_y) * LINE + to_z))
        slot = rank(source * GROUP + to)
        over = first & ((ring_first >= RING_FIRST) | (crossing & line_over))
        over = over | (jnp.logical_not(first) & (ring_second >= RING_SECOND))
        place2_ring = jnp.where(mine & crossing & (from_z == z) & (to_y == y), line_second, -1)
        place2_line = jnp.where(mine & (from_y == y) & (to_z == z), to_y * RING_SECOND + ring_second, -1)
        place2 = jnp.where(at_ring, place2_ring, place2_line)
        from_ring = block * RING_FIRST + ring_first
        from_line = jnp.where(from_z == z, cell, CAP + line_first)
        index2 = jnp.where(at_ring, from_ring, from_line)
        place3 = jnp.where(to == g, source * MOST + slot, -1)
        index3 = jnp.where(crossing, FINAL_RING + line_second, from_ring)
        index3 = jnp.where(first, index3, FINAL_LINE + from_y * RING_SECOND + ring_second)
        over = jnp.sum(jnp.where(over, 1.0, 0.0), axis=1, keepdims=True)
        return listing(place2, index2), listing(place3, index3), over

    return listing(place1, cell), later


def kernel(
    n_gore, n_band,
    yield_hbm, route_hbm, disp_hbm, stiff_hbm, press_hbm, state_hbm, weave_hbm,
    plane_hi_hbm, plane_lo_hbm, line_hbm, weight_hbm,
    force_ref, flag_ref, table_ref, final, own_ref,
    yield_ref, route_ref, disp_ref, stiff_ref, press_ref, state_ref, weave_ref,
    plane_hi_ref, plane_lo_ref, line_ref, weight_ref,
    halo_g, halo_b, got_g, got_b, slopes, strain_s,
    e_s, w_s, s_pad, d_s, x_s, f_s, cells,
    names, names_got, flag, flag_got, hop1_v, hop1_table, table_v, table,
    own, send1, send2, ring_got, ring_far, line_got, here_got,
    in_sem, halo_send, halo_recv, name_send, name_recv, flag_send, flag_recv, table_sem,
    hop1_send, hop1_recv, hop2_send, hop2_recv, share_send, share_recv, local_sem,
):
    g, b = lax.axis_index("gore"), lax.axis_index("band")
    y, z, core = lax.div(g, LINE * CORE), lax.rem(lax.div(g, CORE), LINE), lax.rem(g, CORE)
    up, down = lax.rem(g + 1, n_gore), lax.rem(g + n_gore - 1, n_gore)
    right, left = lax.rem(b + 1, n_band), lax.rem(b + n_band - 1, n_band)
    nodes_g, nodes_b = stiff_ref.shape

    barrier = pltpu.get_barrier_semaphore()
    for d in range(1, n_gore):
        pl.semaphore_signal(barrier, inc=1, device_id=(lax.rem(g + d, n_gore), b), device_id_type=MESH)
    for d in range(1, n_band):
        pl.semaphore_signal(barrier, inc=1, device_id=(g, lax.rem(b + d, n_band)), device_id_type=MESH)

    operands = (
        (route_hbm, route_ref), (disp_hbm, disp_ref), (yield_hbm, yield_ref), (state_hbm, state_ref),
        (weave_hbm, weave_ref), (stiff_hbm, stiff_ref), (plane_hi_hbm, plane_hi_ref),
        (plane_lo_hbm, plane_lo_ref), (line_hbm, line_ref), (weight_hbm, weight_ref), (press_hbm, press_ref),
    )
    loads = [pltpu.make_async_copy(p, q, in_sem.at[i]) for i, (p, q) in enumerate(operands)]
    for copy in loads:
        copy.start()

    def halo_copies(k):
        out = []
        for side, target in enumerate(((down, b), (up, b), (g, left), (g, right))):
            source, place = (halo_g, got_g) if side < 2 else (halo_b, got_b)
            out.append(
                pltpu.make_async_remote_copy(
                    src_ref=source.at[2 * k + side % 2],
                    dst_ref=place.at[2 * k + side % 2],
                    send_sem=halo_send.at[4 * k + side],
                    recv_sem=halo_recv.at[4 * k + side],
                    device_id=target,
                    device_id_type=MESH,
                )
            )
        return out

    def name_copy(d):
        return pltpu.make_async_remote_copy(
            src_ref=names, dst_ref=names_got.at[g], send_sem=name_send.at[d], recv_sem=name_recv.at[d],
            device_id=(lax.rem(g + d, n_gore), b), device_id_type=MESH,
        )

    def flag_copy(d):
        return pltpu.make_async_remote_copy(
            src_ref=flag, dst_ref=flag_got.at[b], send_sem=flag_send.at[d], recv_sem=flag_recv.at[d],
            device_id=(g, lax.rem(b + d, n_band)), device_id_type=MESH,
        )

    loads[0].wait()
    place = lax.broadcasted_iota(jnp.int32, (8, 128), 1)
    named = jnp.zeros((8, 128), jnp.int32)
    for r in range(CAP):
        named = jnp.where(place == g * CAP + r, route_ref[r], named)
    names[...] = named
    loads[1].wait()
    for c in range(3):
        v = disp_ref[c]
        halo_g[0, c : c + 1, :] = v[0:1]
        halo_g[1, c : c + 1, :] = v[nodes_g - 1 :]
        halo_b[0, c : c + 1, :] = to_row(v[:, 0:1])
        halo_b[1, c : c + 1, :] = to_row(v[:, nodes_b - 1 :])
    pl.semaphore_wait(barrier, n_gore + n_band - 2)
    first = halo_copies(0)
    for copy in first:
        copy.start()
    for d in range(1, n_gore):
        name_copy(d).start()

    loads[3].wait()
    loads[4].wait()

    def load_states(i, sums):
        at = pl.multiple_of(i * 16, 16)
        out = []
        for c in range(3):
            pair = state_ref[c, :, pl.ds(pl.multiple_of(i * 2 * PLANE, 128), 2 * PLANE)]
            even, odd = pair[:, :PLANE], pair[:, PLANE:]
            e_s[c, pl.ds(at, 16), :] = jnp.concatenate([even, odd], axis=0)
            out.append(sums[c] + even + odd)
        rows = [jnp.broadcast_to(weave_ref[pl.ds(i * 9 + t, 1), :], (CAP, 128)) for t in range(9)]
        pair = jnp.concatenate(rows, axis=1)
        w_s[pl.ds(at, 16), :] = jnp.concatenate([pair[:, :PLANE], pair[:, PLANE:]], axis=0)
        return tuple(out)

    zero = jnp.zeros((CAP, PLANE), F32)
    sums = lax.fori_loop(0, G // 2, load_states, (zero, zero, zero), unroll=2)
    means = [jnp.sum(s, axis=1, keepdims=True) * (1.0 / VOX) for s in sums]

    for d in range(1, n_gore):
        name_copy(d).wait()
    for copy in first:
        copy.wait()

    worker = names[0:1, :]
    for d in range(1, n_gore):
        worker = worker + names_got[lax.rem(g + d, n_gore), 0:1, :]
    hop1_v[...] = jnp.broadcast_to(routing(worker.astype(F32), g)[0], (8, 128))
    hop1_scalars = pltpu.make_async_copy(hop1_v, hop1_table, table_sem.at[0])
    hop1_scalars.start()

    inner_left, inner_right = b > 0, b < n_band - 1
    for c in range(3):
        v = disp_ref[c]
        before = jnp.where(inner_left, to_column(got_b[1, c : c + 1, :]), 0.0)
        after = jnp.where(inner_right, to_column(got_b[0, c : c + 1, :]), 0.0)
        slopes[c] = gore_diff(v, got_g[1, c : c + 1, :], got_g[0, c : c + 1, :])
        slopes[3 + c] = band_diff(v, before, after)
    gz, bz = slopes[2], slopes[5]
    strain_s[0] = slopes[0] + 0.5 * gz * gz
    strain_s[1] = slopes[4] + 0.5 * bz * bz
    strain_s[2] = 0.5 * (slopes[3] + slopes[1]) + 0.5 * gz * bz

    loads[2].wait()
    cell_row = lax.broadcasted_iota(jnp.int32, (CAP, 1), 0)
    lane = lax.broadcasted_iota(jnp.int32, (CAP, nodes_b), 1)
    points = [yield_ref[r] for r in range(CAP)]
    wanted = jnp.zeros((CAP, 1), jnp.int32)
    for r in range(CAP):
        wanted = jnp.where(cell_row == r, lax.rem(points[r], nodes_b), wanted)
    shift = []
    for c in range(3):
        rows = [strain_s[c, pl.ds(lax.div(points[r], nodes_b), 1), :] for r in range(CAP)]
        rows = jnp.concatenate(rows, axis=0)
        drive = jnp.sum(jnp.where(lane == wanted, rows, 0.0), axis=1, keepdims=True)
        drive = drive - means[c]
        shift.append(jnp.concatenate([drive, drive], axis=0))

    low = lax.rem(lax.broadcasted_iota(jnp.int32, (16, PLANE), 1), G)

    def advance(i, sweep):
        at = pl.multiple_of(i * 16, 16)
        e = [e_s[c, pl.ds(at, 16), :] for c in range(3)]
        if sweep == 0:
            e = [e[c] + shift[c] for c in range(3)]
        else:
            middle = f_s[pl.ds(at + 8, 16), :]
            e[0] = e[0] + 0.5 * (f_s[pl.ds(at + 16, 16), :] - f_s[pl.ds(at, 16), :])
            e[1] = e[1] + 0.5 * diff_upper(middle)
            e[2] = e[2] + 0.5 * diff_lower(middle, low)
        size = e[0] * e[0] + e[1] * e[1] + e[2] * e[2]
        factor = w_s[pl.ds(at, 16), :] * (1.5 - 0.5 / (1.0 + size))
        return at, e, [factor * v for v in e]

    def parts(v):
        high = v.astype(BF16)
        return high, (v - high.astype(F32)).astype(BF16)

    def lines(v):
        high, rest = parts(v)
        both = jnp.dot(line_ref[...], high, preferred_element_type=F32)
        n = G * CAP
        return both[:n] + both[n:] + jnp.dot(line_ref[0:n, :], rest, preferred_element_type=F32)

    def planes(both):
        n = G * CAP
        out = jnp.dot(both, plane_hi_ref[...], preferred_element_type=F32)
        return out[:n] + out[n:] + jnp.dot(both[:n], plane_lo_ref[...], preferred_element_type=F32)

    for copy in loads[5:]:
        copy.wait()
    for sweep in range(SWEEPS):

        def law(i, carry, sweep=sweep):
            at, e, s = advance(i, sweep)
            for c in range(3):
                e_s[c, pl.ds(at, 16), :] = e[c]
            s_pad[pl.ds(at + 8, 16), :] = s[0]
            d_s[pl.ds(at, 16), :] = diff_upper(s[1]) + diff_lower(s[2], low)
            return carry

        lax.fori_loop(0, G // 2, law, 0, unroll=6)
        s_pad[0:8, :] = s_pad[G * 8 : G * 8 + 8, :]
        s_pad[G * 8 + 8 :, :] = s_pad[8:16, :]

        def source(i, carry):
            at = pl.multiple_of(i * 16, 16)
            v = 0.5 * (s_pad[pl.ds(at + 16, 16), :] - s_pad[pl.ds(at, 16), :] + d_s[pl.ds(at, 16), :])
            high, rest = parts(v)
            x_s[pl.ds(at, 16), :] = high
            x_s[pl.ds(G * CAP + at, 16), :] = rest
            return carry

        lax.fori_loop(0, G // 2, source, 0, unroll=6)
        spectrum = lines(planes(x_s[...]))
        weight = jnp.broadcast_to(weight_ref[...], (G, CAP, PLANE)).reshape(G * CAP, PLANE)
        back = lines(spectrum * weight)
        high, rest = parts(back)
        x_s[0 : G * CAP, :] = high
        x_s[G * CAP :, :] = rest
        f_s[8 : G * 8 + 8, :] = planes(x_s[...])
        f_s[0:8, :] = f_s[G * 8 : G * 8 + 8, :]
        f_s[G * 8 + 8 :, :] = f_s[8:16, :]

    def finish(i, sums):
        at, e, s = advance(i, SWEEPS)
        out = []
        for c in range(3):
            wide = jnp.concatenate([e[c][0:8], e[c][8:16]], axis=1)
            for t in range(2 * PLANE // 128):
                row = pl.multiple_of((c * (VOX // 128) + i * 9 + t) * CAP, CAP)
                cells[pl.ds(row, CAP), :] = wide[:, 128 * t : 128 * t + 128]
            out.append(sums[c] + s[c][0:8] + s[c][8:16])
        return tuple(out)

    sums = lax.fori_loop(0, G // 2, finish, (zero, zero, zero), unroll=2)
    point_stress = [jnp.sum(s, axis=1, keepdims=True) * (1.0 / VOX) for s in sums]

    cells[ROWS * CAP :, :] = jnp.zeros((PACK * CAP - ROWS * CAP, 128), F32)
    hop1_scalars.wait()

    def at_index(table, row, position, bound):
        return jnp.clip(table[row, position] - 1, 0, bound - 1)

    def tiles_of(cell, m):
        return cells[pl.ds(m * 64 + cell, 8, stride=CAP), :]

    def hop(semaphores, slot, source, place, ring_place, line_place, core_place):
        send, recv = semaphores
        return pltpu.make_async_remote_copy(
            src_ref=source, dst_ref=place, send_sem=send.at[slot], recv_sem=recv.at[slot],
            device_id=((ring_place * LINE + line_place) * CORE + core_place, b), device_id_type=MESH,
        )

    one, two, three = (hop1_send, hop1_recv), (hop2_send, hop2_recv), (share_send, share_recv)

    def ring_first(j):
        to = lax.rem(y + STEPS[j], RING)
        n = RING_FIRST
        place = ring_got.at[pl.ds((j + 1) * n, n)] if j < 2 else ring_far
        return hop(one, j, send1.at[pl.ds(j * n, n)], place, to, z, 0)

    def line_first():
        return hop(one, 0, send1.at[pl.ds(0, LINE_FIRST)], line_got, y, 1 - z, 1)

    line_spans = ((0, LINE_NEAR), (LINE_NEAR, LINE_FAR))

    def line_second(j):
        low, n = line_spans[j]
        return hop(two, j, send2.at[pl.ds(low, n)], final.at[pl.ds(FINAL_RING + low, n)], y, 1 - z, 0)

    def ring_second(j):
        to = lax.rem(y + STEPS[j], RING)
        n = RING_SECOND
        return hop(two, j, send2.at[pl.ds(j * n, n)], final.at[pl.ds(FINAL_LINE + y * n, n)], to, z, 1)

    ring_spans = ((0, NEAR), (NEAR, RING_FIRST)) + tuple((FINAL_RING + low, n) for low, n in line_spans)

    def share_ring(j, to=1):
        low, n = ring_spans[j]
        span = final.at[pl.ds(low, n)]
        return hop(three, j, (ring_got, ring_far, span, span)[j], span, y, z, to)

    def share_line(j):
        from_y = y if j == 0 else lax.rem(y + RING - STEPS[j - 1], RING)
        span = final.at[pl.ds(FINAL_LINE + from_y * RING_SECOND, RING_SECOND)]
        return hop(three, j, here_got if j == 0 else span, span, y, z, 0)

    def share_line_in(j):
        from_y = y if j == 0 else lax.rem(y + RING - STEPS[j - 1], RING)
        span = final.at[pl.ds(FINAL_LINE + from_y * RING_SECOND, RING_SECOND)]
        return hop(three, j, span, span, y, z, 1)

    def share_ring_in(j):
        return share_ring(j, 0)

    @pl.when(core == 0)
    def _():
        for j in range(RING):
            to = lax.rem(y + (STEPS[j] if j < 3 else 0), RING)

            def fill(p, carry, j=j, to=to):
                cell = at_index(hop1_table, 0, to * RING_FIRST + p, CAP)
                for m in range(PACK // 8):
                    v = tiles_of(cell, m)
                    if j < 3:
                        send1[j * RING_FIRST + p, 8 * m : 8 * m + 8, :] = v
                    else:
                        ring_got[p, 8 * m : 8 * m + 8, :] = v
                return carry

            lax.fori_loop(0, RING_FIRST, fill, 0)
            if j < 3:
                ring_first(j).start()

    @pl.when(core == 1)
    def _():
        def fill(p, carry):
            cell = at_index(hop1_table, 0, p, CAP)
            for m in range(PACK // 8):
                send1[p, 8 * m : 8 * m + 8, :] = tiles_of(cell, m)
            return carry

        lax.fori_loop(0, LINE_FIRST, fill, 0)
        line_first().start()

    list2, list3, over = routing(worker.astype(F32), g)[1]()
    table_v[0:1, :] = list2
    table_v[1:2, :] = list3
    to_scalars = pltpu.make_async_copy(table_v, table, table_sem.at[1])
    to_scalars.start()
    hand_on = pltpu.make_async_copy(table_v, table_ref, table_sem.at[2])
    hand_on.start()
    flag[...] = jnp.broadcast_to(over, (8, 128)).astype(jnp.int32)
    for d in range(1, n_band):
        flag_copy(d).start()
    for r in range(CAP):

        def gather(m, carry, r=r):
            own[r, pl.ds(pl.multiple_of(m * 8, 8), 8), :] = cells[pl.ds(m * 64 + r, 8, stride=CAP), :]
            return carry

        lax.fori_loop(0, PACK // 8, gather, 0, unroll=True)
    keep = pltpu.make_async_copy(own, own_ref, local_sem.at[0])
    keep.start()

    stiff = stiff_ref[...]
    e11, e22, e12 = strain_s[0], strain_s[1], strain_s[2]
    stress = [
        stiff * (e11 + POISSON * e22),
        stiff * (e22 + POISSON * e11),
        stiff * (1.0 - POISSON) * e12,
    ]
    node = lax.broadcasted_iota(jnp.int32, stiff.shape, 0) * nodes_b + lax.broadcasted_iota(jnp.int32, stiff.shape, 1)
    for r in range(CAP):
        here = node == points[r]
        for c in range(3):
            stress[c] = jnp.where(here, point_stress[c][r : r + 1, :], stress[c])
    s11, s22, s12 = stress
    gz, bz = slopes[2], slopes[5]
    t1 = s11 * gz + s12 * bz
    t2 = s12 * gz + s22 * bz
    over_gore, over_band = [s11, s12, t1], [s12, s22, t2]
    for c in range(3):
        halo_g[2, c : c + 1, :] = over_gore[c][0:1]
        halo_g[3, c : c + 1, :] = over_gore[c][nodes_g - 1 :]
        halo_b[2, c : c + 1, :] = to_row(over_band[c][:, 0:1])
        halo_b[3, c : c + 1, :] = to_row(over_band[c][:, nodes_b - 1 :])
    second = halo_copies(1)
    for copy in second:
        copy.start()
    slopes[0] = s11
    slopes[1] = s12
    slopes[3] = s22
    slopes[4] = t1
    slopes[5] = t2

    to_scalars.wait()

    def stay_here():
        span = pl.ds(FINAL_LINE + y * RING_SECOND, RING_SECOND)
        return pltpu.make_async_copy(here_got, final.at[span], local_sem.at[1])

    def stay(j):
        low, n = ring_spans[j]
        return pltpu.make_async_copy((ring_got, ring_far)[j], final.at[pl.ds(low, n)], local_sem.at[1 + j])

    @pl.when(core == 0)
    def _():
        for j in range(2):
            for i in ((0, 1), (2,))[j]:
                ring_first(i).wait()

            def fill(p, carry, j=j):
                cell = at_index(table, 0, p, FINAL_RING)
                held = ring_got if j == 0 else ring_far
                cell = jnp.clip(cell - j * NEAR, 0, held.shape[0] - 1)
                for m in range(PACK // 8):
                    send2[p, 8 * m : 8 * m + 8, :] = held[cell, 8 * m : 8 * m + 8, :]
                return carry

            low, n = line_spans[j]
            lax.fori_loop(low, low + n, fill, 0)
            line_second(j).start()
            share_ring(j).start()
            stay(j).start()

    @pl.when(core == 1)
    def _():
        line_first().wait()
        for j in range(4):
            to = lax.rem(y + (STEPS[j] if j < 3 else 0), RING)

            def fill(p, carry, j=j, to=to):
                index = at_index(table, 0, to * RING_SECOND + p, 2 * CAP)
                mine = index < CAP
                here, there = jnp.minimum(index, CAP - 1), jnp.maximum(index - CAP, 0)
                for m in range(PACK // 8):
                    v = jnp.where(mine, own[here, 8 * m : 8 * m + 8, :], line_got[there, 8 * m : 8 * m + 8, :])
                    if j < 3:
                        send2[j * RING_SECOND + p, 8 * m : 8 * m + 8, :] = v
                    else:
                        here_got[p, 8 * m : 8 * m + 8, :] = v
                return carry

            lax.fori_loop(0, RING_SECOND, fill, 0)
            if j < 3:
                ring_second(j).start()
        share_line(0).start()
        stay_here().start()

    for copy in second:
        copy.wait()
    edge = []
    for c in range(3):
        before = jnp.where(inner_left, to_column(got_b[3, c : c + 1, :]), 0.0)
        after = jnp.where(inner_right, to_column(got_b[2, c : c + 1, :]), 0.0)
        edge.append((before, after))
    pairs = ((0, 1), (1, 3), (4, 5))
    for c, (p, q) in enumerate(pairs):
        value = gore_diff(slopes[p], got_g[3, c : c + 1, :], got_g[2, c : c + 1, :])
        value = value + band_diff(slopes[q], *edge[c])
        if c == 2:
            value = value + press_ref[...]
        force_ref[c] = value
    @pl.when(core == 0)
    def _():
        for j in range(2):
            line_second(j).wait()
            share_ring(2 + j).start()
        for j in range(2):
            stay(j).wait()
        for j in range(4):
            share_ring(j).wait_send()
        for j in range(4):
            share_line_in(j).wait_recv()

    @pl.when(core == 1)
    def _():
        for j in range(3):
            ring_second(j).wait()
            share_line(1 + j).start()
        stay_here().wait()
        for j in range(4):
            share_line(j).wait_send()
        for j in range(4):
            share_ring_in(j).wait_recv()

    for d in range(1, n_band):
        flag_copy(d).wait()
    total = flag[...]
    for d in range(1, n_band):
        total = total + flag_got[lax.rem(b + d, n_band)]
    flag_ref[0] = jnp.sum(total[0:1, :].astype(F32)).astype(jnp.int32)

    keep.wait()
    hand_on.wait()


def place_kernel(table, final, result, got, made, in_sem, out_sem):
    tiles, groups = VOX // 128, GROUP * MOST // 8

    def load(p):
        cell = jnp.clip(table[1, p] - 1, 0, FINAL - 1)
        return pltpu.make_async_copy(final.at[cell], got.at[p], in_sem.at[p])

    for p in range(GROUP * MOST):

        @pl.when(table[1, p] > 0)
        def _(p=p):
            load(p).start()

    def clear(i, carry):
        made[pl.ds(pl.multiple_of(i * 216, 216), 216), :] = jnp.zeros((216, 128), F32)
        return carry

    lax.fori_loop(0, 3 * groups * tiles * 8 // 216, clear, 0)

    def one(p, carry):
        @pl.when(table[1, p] > 0)
        def _():
            load(p).wait()
            for m in range(PACK // 8):
                v = got[p, 8 * m : 8 * m + 8, :]
                row = 8 * m
                while row < min(8 * m + 8, ROWS):
                    c, tile = row // tiles, row % tiles
                    count = min(8 * m + 8, (c + 1) * tiles) - row
                    start = ((c * groups + p // 8) * tiles + tile) * 8 + p % 8
                    made[pl.ds(start, count, stride=8), :] = v[row - 8 * m : row - 8 * m + count]
                    row = row + count

        return carry

    stores = []
    for t in range(groups):
        lax.fori_loop(8 * t, 8 * t + 8, one, 0)
        for c in range(3):
            span = pl.ds((c * groups + t) * tiles * 8, tiles * 8)
            stores.append(pltpu.make_async_copy(made.at[span], result.at[span], out_sem.at[3 * t + c]))
            stores[-1].start()
    for copy in stores:
        copy.wait()


def place(table, final):
    hbm = pl.BlockSpec(memory_space=pltpu.HBM)
    slots = GROUP * MOST
    result = pl.pallas_call(
        place_kernel,
        out_shape=jax.ShapeDtypeStruct((3 * slots * VOX // 128, 128), F32),
        in_specs=[pl.BlockSpec(memory_space=pltpu.SMEM), hbm],
        out_specs=hbm,
        scratch_shapes=[
            pltpu.VMEM((slots, PACK, 128), F32),
            pltpu.VMEM((3 * slots * VOX // 128, 128), F32),
            pltpu.SemaphoreType.DMA((slots,)),
            pltpu.SemaphoreType.DMA((3 * slots // 8,)),
        ],
        compiler_params=pltpu.CompilerParams(vmem_limit_bytes=60 * 2**20),
        name="place",
    )(table, final)
    return in_place(slots, result)


def in_place(slots, result):
    tiles = result.reshape(3, slots // 8, VOX // 128, 8, 128)
    return tiles.transpose(0, 1, 3, 2, 4).reshape(3, slots, VOX)


def send_all(workers, own, n_gore, slots):
    states = own[:, :ROWS].reshape(CAP, 3, VOX)
    onehot = (workers[:, None] == jnp.arange(n_gore, dtype=jnp.int32)[None, :]).astype(jnp.int32)
    earlier = jnp.cumsum(onehot, axis=0) - onehot
    slot_index = workers * MOST + jnp.sum(earlier * onehot, axis=1)
    outgoing = jnp.zeros((slots, 3, VOX), F32).at[slot_index].set(states)
    arrived = lax.all_to_all(
        outgoing.reshape(n_gore, MOST, 3, VOX), "gore", split_axis=0, concat_axis=0, tiled=True
    )
    return arrived.reshape(slots, 3, VOX).transpose(1, 0, 2)


def local(displacement, stiffness, pressure, yield_points, route, cell_state, weave):
    n_gore, n_band = lax.axis_size("gore"), lax.axis_size("band")
    slots = n_gore * MOST
    nodes_g, nodes_b = stiffness.shape
    plane_high, plane_low, line, weight = tables()
    vmem, hbm = pl.BlockSpec(memory_space=pltpu.VMEM), pl.BlockSpec(memory_space=pltpu.HBM)
    n = G * CAP
    vm, dma = pltpu.VMEM, pltpu.SemaphoreType.DMA
    workers = route.reshape(-1)
    force, flag, table, final, own = pl.pallas_call(
        lambda *refs: kernel(n_gore, n_band, *refs),
        out_shape=(
            jax.ShapeDtypeStruct((3, nodes_g, nodes_b), F32),
            jax.ShapeDtypeStruct((1,), jnp.int32),
            jax.ShapeDtypeStruct((8, 128), jnp.int32),
            jax.ShapeDtypeStruct((FINAL, PACK, 128), F32),
            jax.ShapeDtypeStruct((CAP, PACK, 128), F32),
        ),
        in_specs=[hbm] * 11,
        out_specs=(vmem, pl.BlockSpec(memory_space=pltpu.SMEM), hbm, hbm, hbm),
        scratch_shapes=[
            pltpu.SMEM((CAP,), jnp.int32),
            pltpu.SMEM((CAP,), jnp.int32),
            vm((3, nodes_g, nodes_b), F32),
            vm((nodes_g, nodes_b), F32),
            vm((nodes_g, nodes_b), F32),
            vm((3, CAP, VOX), F32),
            vm((VOX // 128, 128), F32),
            vm((PLANE, PLANE), BF16),
            vm((PLANE, PLANE), BF16),
            vm((2 * n, n), BF16),
            vm((G, 1, PLANE), F32),
            vm((4, 8, nodes_b), F32),
            vm((4, 8, nodes_g), F32),
            vm((4, 8, nodes_b), F32),
            vm((4, 8, nodes_g), F32),
            vm((6, nodes_g, nodes_b), F32),
            vm((3, nodes_g, nodes_b), F32),
            vm((3, n, PLANE), F32),
            vm((n, PLANE), F32),
            vm((n + 16, PLANE), F32),
            vm((n, PLANE), F32),
            vm((2 * n, PLANE), BF16),
            vm((n + 16, PLANE), F32),
            vm((PACK * CAP, 128), F32),
            vm((8, 128), jnp.int32),
            vm((n_gore, 8, 128), jnp.int32),
            vm((8, 128), jnp.int32),
            vm((n_band, 8, 128), jnp.int32),
            vm((8, 128), jnp.int32),
            pltpu.SMEM((8, 128), jnp.int32),
            vm((8, 128), jnp.int32),
            pltpu.SMEM((8, 128), jnp.int32),
            vm((CAP, PACK, 128), F32),
            vm((3 * RING_FIRST, PACK, 128), F32),
            vm((3 * RING_SECOND, PACK, 128), F32),
            vm((NEAR, PACK, 128), F32),
            vm((RING_FIRST, PACK, 128), F32),
            vm((LINE_FIRST, PACK, 128), F32),
            vm((RING_SECOND, PACK, 128), F32),
            dma((11,)),
            dma((8,)),
            dma((8,)),
            dma((n_gore,)),
            dma((n_gore,)),
            dma((n_band,)),
            dma((n_band,)),
            dma((3,)),
            dma((3,)),
            dma((3,)),
            dma((3,)),
            dma((3,)),
            dma((4,)),
            dma((4,)),
            dma((3,)),
        ],
        compiler_params=pltpu.CompilerParams(
            collective_id=0, has_side_effects=True, vmem_limit_bytes=60 * 2**20
        ),
        name="cells",
    )(
        yield_points,
        workers,
        displacement,
        stiffness,
        pressure,
        cell_state.transpose(1, 0, 2),
        weave.reshape(VOX // 128, 128),
        jnp.asarray(plane_high),
        jnp.asarray(plane_low),
        jnp.asarray(line),
        jnp.asarray(weight),
    )
    cell_strain = lax.cond(
        flag[0] == 0,
        lambda table, final, own, workers: place(table, final),
        lambda table, final, own, workers: send_all(workers, own, n_gore, slots),
        table, final, own, workers,
    )
    return force, cell_strain.transpose(1, 0, 2)


def solution(mesh):
    return jax.shard_map(
        local,
        mesh=mesh,
        in_specs=(
            P(None, "gore", "band"),
            P("gore", "band"),
            P("gore", "band"),
            P(("gore", "band")),
            P(("gore", "band"), None),
            P(("gore", "band"), None, None),
            P(),
        ),
        out_specs=(P(None, "gore", "band"), P(("gore", "band"), None, None)),
        check_vma=False,
    )
```

```python
import math

import jax
import jax.numpy as jnp
import numpy as np
from jax import lax
from jax.experimental import pallas as pl
from jax.experimental.pallas import tpu as pltpu
from jax.sharding import PartitionSpec as P

G = 24
PLANE = G * G
VOX = G * G * G
SWEEPS = 2
POISSON = 0.3
CAP = 8
MOST = 2
ROWS = 3 * VOX // 128
PACK = 328
RING, LINE, CORE = 4, 2, 2
GROUP = RING * LINE * CORE
RING_FIRST, LINE_NEAR, LINE_FAR, LINE_FIRST, RING_SECOND = 5, 9, 3, 8, 6
STEPS = (1, 3, 2)
FINAL_RING = RING * RING_FIRST
FINAL_LINE = FINAL_RING + LINE_NEAR + LINE_FAR
NEAR = (RING - 1) * RING_FIRST
FINAL = FINAL_LINE + RING * RING_SECOND
MESH = pl.DeviceIdType.MESH
F32 = jnp.float32
BF16 = jnp.bfloat16


def tables():
    n = np.arange(G)
    phase = 2.0 * np.pi * (np.outer(n, n) % G) / G
    hartley = (np.cos(phase) + np.sin(phase)) / math.sqrt(G)
    plane = np.kron(hartley, hartley)
    line = np.kron(hartley, np.eye(CAP))

    def split(a):
        high = a.astype(np.float32).astype(jnp.bfloat16)
        low = (a - high.astype(np.float64)).astype(np.float32).astype(jnp.bfloat16)
        return high, low

    square = np.sin(phase[1]) ** 2
    summed = square[:, None, None] + square[None, :, None] + square[None, None, :]
    level = n % (G // 2) == 0
    silent = level[:, None, None] & level[None, :, None] & level[None, None, :]
    weight = np.where(silent, 0.0, 1.0 / (10.0 * np.where(silent, 1.0, summed)))
    plane_high, plane_low = split(plane)
    line_high, line_low = split(line)
    return (
        plane_high,
        plane_low,
        np.concatenate([line_high, line_low], axis=0),
        weight.reshape(G, 1, PLANE).astype(np.float32),
    )


def shifted(v, k):
    k = k % v.shape[1]
    return jnp.concatenate([v[:, k:], v[:, :k]], axis=1)


def diff_upper(v):
    return shifted(v, G) - shifted(v, -G)


def diff_lower(v, low):
    forward = jnp.where(low == G - 1, shifted(v, 1 - G), shifted(v, 1))
    backward = jnp.where(low == 0, shifted(v, G - 1), shifted(v, -1))
    return forward - backward


def to_row(column):
    n = column.shape[0]
    diagonal = lax.broadcasted_iota(jnp.int32, (n, n), 0) == lax.broadcasted_iota(jnp.int32, (n, n), 1)
    return jnp.sum(jnp.where(diagonal, column, 0.0), axis=0, keepdims=True)


def to_column(row):
    n = row.shape[1]
    diagonal = lax.broadcasted_iota(jnp.int32, (n, n), 0) == lax.broadcasted_iota(jnp.int32, (n, n), 1)
    return jnp.sum(jnp.where(diagonal, row, 0.0), axis=1, keepdims=True)


def gore_diff(v, before, after):
    down = jnp.concatenate([v[1:], after], axis=0)
    up = jnp.concatenate([before, v[:-1]], axis=0)
    return (down - up) * 0.5


def band_diff(v, before, after):
    right = jnp.concatenate([v[:, 1:], after], axis=1)
    left = jnp.concatenate([before, v[:, :-1]], axis=1)
    return (right - left) * 0.5


def rank_of(key, key_column, earlier):
    return jnp.sum(jnp.where((key_column == key) & earlier, 1.0, 0.0), axis=0, keepdims=True)


def routing(worker, g):
    n = GROUP * CAP
    lane = lax.broadcasted_iota(jnp.int32, (1, n), 1)
    to = worker.astype(jnp.int32)
    source = lane >> 3
    to_y, to_z = to >> 2, (to >> 1) & 1
    from_y, from_z, from_c = source >> 2, (source >> 1) & 1, source & 1
    y, z, c = g >> 2, (g >> 1) & 1, g & 1
    crossing, first = to_z != from_z, from_c == 0
    alone = -1 - lane
    earlier = lax.broadcasted_iota(jnp.int32, (n, n), 0) < lax.broadcasted_iota(jnp.int32, (n, n), 1)

    def rank(key):
        key = key.astype(F32)
        return rank_of(key, to_column(key), earlier).astype(jnp.int32)

    own, mine = source == g, from_c == c
    at_ring = c == 0
    cell = lane & 7
    column = lax.broadcasted_iota(jnp.int32, (n, n), 1).astype(F32)

    def listing(place, index):
        place, index = to_column(place.astype(F32)), to_column(index.astype(F32) + 1.0)
        return jnp.sum(jnp.where(place == column, index, 0.0), axis=0, keepdims=True).astype(jnp.int32)

    ahead = (from_y + RING - to_y) & (RING - 1)
    block = jnp.where(ahead == 3, 1, jnp.where(ahead == 1, 2, jnp.where(ahead == 2, 3, 0)))
    far = jnp.where(ahead == 2, 1, 0)
    ring_first = rank(source * RING + to_y)
    line_first = rank(jnp.where(crossing, source, alone))
    place1_ring = jnp.where(own, to_y * RING_FIRST + ring_first, -1)
    place1 = jnp.where(at_ring, place1_ring, jnp.where(own & crossing, line_first, -1))

    def later():
        line_second = rank(jnp.where(first & crossing, (from_z * RING + to_y) * 2 + far, alone))
        line_over = line_second >= LINE_NEAR + far * (LINE_FAR - LINE_NEAR)
        line_second = line_second + far * LINE_NEAR
        ring_second = rank(jnp.where(first, alone, (from_y * RING + to_y) * LINE + to_z))
        slot = rank(source * GROUP + to)
        over = first & ((ring_first >= RING_FIRST) | (crossing & line_over))
        over = over | (jnp.logical_not(first) & (ring_second >= RING_SECOND))
        place2_ring = jnp.where(mine & crossing & (from_z == z) & (to_y == y), line_second, -1)
        place2_line = jnp.where(mine & (from_y == y) & (to_z == z), to_y * RING_SECOND + ring_second, -1)
        place2 = jnp.where(at_ring, place2_ring, place2_line)
        from_ring = block * RING_FIRST + ring_first
        from_line = jnp.where(from_z == z, cell, CAP + line_first)
        index2 = jnp.where(at_ring, from_ring, from_line)
        place3 = jnp.where(to == g, source * MOST + slot, -1)
        index3 = jnp.where(crossing, FINAL_RING + line_second, from_ring)
        index3 = jnp.where(first, index3, FINAL_LINE + from_y * RING_SECOND + ring_second)
        over = jnp.sum(jnp.where(over, 1.0, 0.0), axis=1, keepdims=True)
        return listing(place2, index2), listing(place3, index3), over

    return listing(place1, cell), later


def kernel(
    n_gore, n_band,
    yield_hbm, route_hbm, disp_hbm, stiff_hbm, press_hbm, state_hbm, weave_hbm,
    plane_hi_hbm, plane_lo_hbm, line_hbm, weight_hbm,
    force_ref, flag_ref, table_ref, final, own_ref,
    yield_ref, route_ref, disp_ref, stiff_ref, press_ref, state_ref, weave_ref,
    plane_hi_ref, plane_lo_ref, line_ref, weight_ref,
    halo_g, halo_b, got_g, got_b, slopes, strain_s,
    e_s, w_s, s_pad, d_s, x_s, f_s, cells,
    names, names_got, flag, flag_got, hop1_v, hop1_table, table_v, table,
    own, send1, send2, ring_got, ring_far, line_got, here_got,
    in_sem, halo_send, halo_recv, name_send, name_recv, flag_send, flag_recv, table_sem,
    hop1_send, hop1_recv, hop2_send, hop2_recv, share_send, share_recv, local_sem,
):
    g, b = lax.axis_index("gore"), lax.axis_index("band")
    y, z, core = lax.div(g, LINE * CORE), lax.rem(lax.div(g, CORE), LINE), lax.rem(g, CORE)
    up, down = lax.rem(g + 1, n_gore), lax.rem(g + n_gore - 1, n_gore)
    right, left = lax.rem(b + 1, n_band), lax.rem(b + n_band - 1, n_band)
    nodes_g, nodes_b = stiff_ref.shape

    barrier = pltpu.get_barrier_semaphore()
    for d in range(1, n_gore):
        pl.semaphore_signal(barrier, inc=1, device_id=(lax.rem(g + d, n_gore), b), device_id_type=MESH)
    for d in range(1, n_band):
        pl.semaphore_signal(barrier, inc=1, device_id=(g, lax.rem(b + d, n_band)), device_id_type=MESH)

    operands = (
        (route_hbm, route_ref), (disp_hbm, disp_ref), (yield_hbm, yield_ref), (state_hbm, state_ref),
        (weave_hbm, weave_ref), (stiff_hbm, stiff_ref), (plane_hi_hbm, plane_hi_ref),
        (plane_lo_hbm, plane_lo_ref), (line_hbm, line_ref), (weight_hbm, weight_ref), (press_hbm, press_ref),
    )
    loads = [pltpu.make_async_copy(p, q, in_sem.at[i]) for i, (p, q) in enumerate(operands)]
    for copy in loads:
        copy.start()

    def halo_copies(k):
        out = []
        for side, target in enumerate(((down, b), (up, b), (g, left), (g, right))):
            source, place = (halo_g, got_g) if side < 2 else (halo_b, got_b)
            out.append(
                pltpu.make_async_remote_copy(
                    src_ref=source.at[2 * k + side % 2],
                    dst_ref=place.at[2 * k + side % 2],
                    send_sem=halo_send.at[4 * k + side],
                    recv_sem=halo_recv.at[4 * k + side],
                    device_id=target,
                    device_id_type=MESH,
                )
            )
        return out

    def name_copy(d):
        return pltpu.make_async_remote_copy(
            src_ref=names, dst_ref=names_got.at[g], send_sem=name_send.at[d], recv_sem=name_recv.at[d],
            device_id=(lax.rem(g + d, n_gore), b), device_id_type=MESH,
        )

    def flag_copy(d):
        return pltpu.make_async_remote_copy(
            src_ref=flag, dst_ref=flag_got.at[b], send_sem=flag_send.at[d], recv_sem=flag_recv.at[d],
            device_id=(g, lax.rem(b + d, n_band)), device_id_type=MESH,
        )

    loads[0].wait()
    place = lax.broadcasted_iota(jnp.int32, (8, 128), 1)
    named = jnp.zeros((8, 128), jnp.int32)
    for r in range(CAP):
        named = jnp.where(place == g * CAP + r, route_ref[r], named)
    names[...] = named
    loads[1].wait()
    for c in range(3):
        v = disp_ref[c]
        halo_g[0, c : c + 1, :] = v[0:1]
        halo_g[1, c : c + 1, :] = v[nodes_g - 1 :]
        halo_b[0, c : c + 1, :] = to_row(v[:, 0:1])
        halo_b[1, c : c + 1, :] = to_row(v[:, nodes_b - 1 :])
    pl.semaphore_wait(barrier, n_gore + n_band - 2)
    first = halo_copies(0)
    for copy in first:
        copy.start()
    for d in range(1, n_gore):
        name_copy(d).start()

    loads[3].wait()
    loads[4].wait()

    def load_states(i, sums):
        at = pl.multiple_of(i * 16, 16)
        out = []
        for c in range(3):
            pair = state_ref[c, :, pl.ds(pl.multiple_of(i * 2 * PLANE, 128), 2 * PLANE)]
            even, odd = pair[:, :PLANE], pair[:, PLANE:]
            e_s[c, pl.ds(at, 16), :] = jnp.concatenate([even, odd], axis=0)
            out.append(sums[c] + even + odd)
        rows = [jnp.broadcast_to(weave_ref[pl.ds(i * 9 + t, 1), :], (CAP, 128)) for t in range(9)]
        pair = jnp.concatenate(rows, axis=1)
        w_s[pl.ds(at, 16), :] = jnp.concatenate([pair[:, :PLANE], pair[:, PLANE:]], axis=0)
        return tuple(out)

    zero = jnp.zeros((CAP, PLANE), F32)
    sums = lax.fori_loop(0, G // 2, load_states, (zero, zero, zero), unroll=True)
    means = [jnp.sum(s, axis=1, keepdims=True) * (1.0 / VOX) for s in sums]

    for d in range(1, n_gore):
        name_copy(d).wait()
    for copy in first:
        copy.wait()

    worker = names[0:1, :]
    for d in range(1, n_gore):
        worker = worker + names_got[lax.rem(g + d, n_gore), 0:1, :]
    hop1_v[...] = jnp.broadcast_to(routing(worker.astype(F32), g)[0], (8, 128))
    hop1_scalars = pltpu.make_async_copy(hop1_v, hop1_table, table_sem.at[0])
    hop1_scalars.start()

    inner_left, inner_right = b > 0, b < n_band - 1
    for c in range(3):
        v = disp_ref[c]
        before = jnp.where(inner_left, to_column(got_b[1, c : c + 1, :]), 0.0)
        after = jnp.where(inner_right, to_column(got_b[0, c : c + 1, :]), 0.0)
        slopes[c] = gore_diff(v, got_g[1, c : c + 1, :], got_g[0, c : c + 1, :])
        slopes[3 + c] = band_diff(v, before, after)
    gz, bz = slopes[2], slopes[5]
    strain_s[0] = slopes[0] + 0.5 * gz * gz
    strain_s[1] = slopes[4] + 0.5 * bz * bz
    strain_s[2] = 0.5 * (slopes[3] + slopes[1]) + 0.5 * gz * bz

    loads[2].wait()
    cell_row = lax.broadcasted_iota(jnp.int32, (CAP, 1), 0)
    lane = lax.broadcasted_iota(jnp.int32, (CAP, nodes_b), 1)
    points = [yield_ref[r] for r in range(CAP)]
    wanted = jnp.zeros((CAP, 1), jnp.int32)
    for r in range(CAP):
        wanted = jnp.where(cell_row == r, lax.rem(points[r], nodes_b), wanted)
    shift = []
    for c in range(3):
        rows = [strain_s[c, pl.ds(lax.div(points[r], nodes_b), 1), :] for r in range(CAP)]
        rows = jnp.concatenate(rows, axis=0)
        drive = jnp.sum(jnp.where(lane == wanted, rows, 0.0), axis=1, keepdims=True)
        drive = drive - means[c]
        shift.append(jnp.concatenate([drive, drive], axis=0))

    low = lax.rem(lax.broadcasted_iota(jnp.int32, (16, PLANE), 1), G)

    def advance(i, sweep):
        at = pl.multiple_of(i * 16, 16)
        e = [e_s[c, pl.ds(at, 16), :] for c in range(3)]
        if sweep == 0:
            e = [e[c] + shift[c] for c in range(3)]
        else:
            middle = f_s[pl.ds(at + 8, 16), :]
            e[0] = e[0] + 0.5 * (f_s[pl.ds(at + 16, 16), :] - f_s[pl.ds(at, 16), :])
            e[1] = e[1] + 0.5 * diff_upper(middle)
            e[2] = e[2] + 0.5 * diff_lower(middle, low)
        size = e[0] * e[0] + e[1] * e[1] + e[2] * e[2]
        factor = w_s[pl.ds(at, 16), :] * (1.5 - 0.5 / (1.0 + size))
        return at, e, [factor * v for v in e]

    def parts(v):
        high = v.astype(BF16)
        return high, (v - high.astype(F32)).astype(BF16)

    def lines(v):
        high, rest = parts(v)
        both = jnp.dot(line_ref[...], high, preferred_element_type=F32)
        n = G * CAP
        return both[:n] + both[n:] + jnp.dot(line_ref[0:n, :], rest, preferred_element_type=F32)

    def planes(both):
        n = G * CAP
        out = jnp.dot(both, plane_hi_ref[...], preferred_element_type=F32)
        return out[:n] + out[n:] + jnp.dot(both[:n], plane_lo_ref[...], preferred_element_type=F32)

    for copy in loads[5:]:
        copy.wait()
    for sweep in range(SWEEPS):

        def law(i, carry, sweep=sweep):
            at, e, s = advance(i, sweep)
            for c in range(3):
                e_s[c, pl.ds(at, 16), :] = e[c]
            s_pad[pl.ds(at + 8, 16), :] = s[0]
            d_s[pl.ds(at, 16), :] = diff_upper(s[1]) + diff_lower(s[2], low)
            return carry

        lax.fori_loop(0, G // 2, law, 0, unroll=True)
        s_pad[0:8, :] = s_pad[G * 8 : G * 8 + 8, :]
        s_pad[G * 8 + 8 :, :] = s_pad[8:16, :]

        def source(i, carry):
            at = pl.multiple_of(i * 16, 16)
            v = 0.5 * (s_pad[pl.ds(at + 16, 16), :] - s_pad[pl.ds(at, 16), :] + d_s[pl.ds(at, 16), :])
            high, rest = parts(v)
            x_s[pl.ds(at, 16), :] = high
            x_s[pl.ds(G * CAP + at, 16), :] = rest
            return carry

        lax.fori_loop(0, G // 2, source, 0, unroll=True)
        spectrum = lines(planes(x_s[...]))
        weight = jnp.broadcast_to(weight_ref[...], (G, CAP, PLANE)).reshape(G * CAP, PLANE)
        back = lines(spectrum * weight)
        high, rest = parts(back)
        x_s[0 : G * CAP, :] = high
        x_s[G * CAP :, :] = rest
        f_s[8 : G * 8 + 8, :] = planes(x_s[...])
        f_s[0:8, :] = f_s[G * 8 : G * 8 + 8, :]
        f_s[G * 8 + 8 :, :] = f_s[8:16, :]

    def finish(i, sums):
        at, e, s = advance(i, SWEEPS)
        out = []
        for c in range(3):
            wide = jnp.concatenate([e[c][0:8], e[c][8:16]], axis=1)
            for t in range(2 * PLANE // 128):
                row = pl.multiple_of((c * (VOX // 128) + i * 9 + t) * CAP, CAP)
                cells[pl.ds(row, CAP), :] = wide[:, 128 * t : 128 * t + 128]
            out.append(sums[c] + s[c][0:8] + s[c][8:16])
        return tuple(out)

    sums = lax.fori_loop(0, G // 2, finish, (zero, zero, zero), unroll=True)
    point_stress = [jnp.sum(s, axis=1, keepdims=True) * (1.0 / VOX) for s in sums]

    cells[ROWS * CAP :, :] = jnp.zeros((PACK * CAP - ROWS * CAP, 128), F32)
    hop1_scalars.wait()

    def at_index(table, row, position, bound):
        return jnp.clip(table[row, position] - 1, 0, bound - 1)

    def tiles_of(cell, m):
        return cells[pl.ds(m * 64 + cell, 8, stride=CAP), :]

    def hop(semaphores, slot, source, place, ring_place, line_place, core_place):
        send, recv = semaphores
        return pltpu.make_async_remote_copy(
            src_ref=source, dst_ref=place, send_sem=send.at[slot], recv_sem=recv.at[slot],
            device_id=((ring_place * LINE + line_place) * CORE + core_place, b), device_id_type=MESH,
        )

    one, two, three = (hop1_send, hop1_recv), (hop2_send, hop2_recv), (share_send, share_recv)

    def ring_first(j):
        to = lax.rem(y + STEPS[j], RING)
        n = RING_FIRST
        place = ring_got.at[pl.ds((j + 1) * n, n)] if j < 2 else ring_far
        return hop(one, j, send1.at[pl.ds(j * n, n)], place, to, z, 0)

    def line_first():
        return hop(one, 0, send1.at[pl.ds(0, LINE_FIRST)], line_got, y, 1 - z, 1)

    line_spans = ((0, 5), (5, LINE_NEAR - 5), (LINE_NEAR, LINE_FAR))

    def line_second(j):
        low, n = line_spans[j]
        return hop(two, j, send2.at[pl.ds(low, n)], final.at[pl.ds(FINAL_RING + low, n)], y, 1 - z, 0)

    half = RING_SECOND // 3
    pieces = tuple((j, h) for h in range(3) for j in range(3))

    def ring_second(i):
        j, h = pieces[i]
        to = lax.rem(y + STEPS[j], RING)
        source = send2.at[pl.ds(j * RING_SECOND + h * half, half)]
        return hop(two, i, source, final.at[pl.ds(FINAL_LINE + y * RING_SECOND + h * half, half)], to, z, 1)

    ring_spans = ((0, NEAR), (NEAR, RING_FIRST)) + tuple((FINAL_RING + low, n) for low, n in line_spans)

    def share_ring(j, to=1):
        low, n = ring_spans[j]
        span = final.at[pl.ds(low, n)]
        return hop(three, j, (ring_got, ring_far, span, span, span)[j], span, y, z, to)

    def share_line(i, to=0):
        if i == 0:
            span, source = pl.ds(FINAL_LINE + y * RING_SECOND, RING_SECOND), here_got
        else:
            j, h = pieces[i - 1]
            from_y = lax.rem(y + RING - STEPS[j], RING)
            span = pl.ds(FINAL_LINE + from_y * RING_SECOND + h * half, half)
            source = final.at[span]
        return hop(three, i, source, final.at[span], y, z, to)

    def share_line_in(i):
        return share_line(i, 1)

    def share_ring_in(j):
        return share_ring(j, 0)

    @pl.when(core == 0)
    def _():
        for j in range(RING):
            to = lax.rem(y + (STEPS[j] if j < 3 else 0), RING)

            def fill(p, carry, j=j, to=to):
                cell = at_index(hop1_table, 0, to * RING_FIRST + p, CAP)
                for m in range(PACK // 8):
                    v = tiles_of(cell, m)
                    if j < 3:
                        send1[j * RING_FIRST + p, 8 * m : 8 * m + 8, :] = v
                    else:
                        ring_got[p, 8 * m : 8 * m + 8, :] = v
                return carry

            lax.fori_loop(0, RING_FIRST, fill, 0)
            if j < 3:
                ring_first(j).start()

    @pl.when(core == 1)
    def _():
        def fill(p, carry):
            cell = at_index(hop1_table, 0, p, CAP)
            for m in range(PACK // 8):
                send1[p, 8 * m : 8 * m + 8, :] = tiles_of(cell, m)
            return carry

        lax.fori_loop(0, LINE_FIRST, fill, 0)
        line_first().start()

    list2, list3, over = routing(worker.astype(F32), g)[1]()
    table_v[0:1, :] = list2
    table_v[1:2, :] = list3
    to_scalars = pltpu.make_async_copy(table_v, table, table_sem.at[1])
    to_scalars.start()
    hand_on = pltpu.make_async_copy(table_v, table_ref, table_sem.at[2])
    hand_on.start()
    flag[...] = jnp.broadcast_to(over, (8, 128)).astype(jnp.int32)
    for d in range(1, n_band):
        flag_copy(d).start()
    for r in range(CAP):

        def gather(m, carry, r=r):
            own[r, pl.ds(pl.multiple_of(m * 8, 8), 8), :] = cells[pl.ds(m * 64 + r, 8, stride=CAP), :]
            return carry

        lax.fori_loop(0, PACK // 8, gather, 0, unroll=True)
    keep = pltpu.make_async_copy(own, own_ref, local_sem.at[0])
    keep.start()

    stiff = stiff_ref[...]
    e11, e22, e12 = strain_s[0], strain_s[1], strain_s[2]
    stress = [
        stiff * (e11 + POISSON * e22),
        stiff * (e22 + POISSON * e11),
        stiff * (1.0 - POISSON) * e12,
    ]
    node = lax.broadcasted_iota(jnp.int32, stiff.shape, 0) * nodes_b + lax.broadcasted_iota(jnp.int32, stiff.shape, 1)
    for r in range(CAP):
        here = node == points[r]
        for c in range(3):
            stress[c] = jnp.where(here, point_stress[c][r : r + 1, :], stress[c])
    s11, s22, s12 = stress
    gz, bz = slopes[2], slopes[5]
    t1 = s11 * gz + s12 * bz
    t2 = s12 * gz + s22 * bz
    over_gore, over_band = [s11, s12, t1], [s12, s22, t2]
    for c in range(3):
        halo_g[2, c : c + 1, :] = over_gore[c][0:1]
        halo_g[3, c : c + 1, :] = over_gore[c][nodes_g - 1 :]
        halo_b[2, c : c + 1, :] = to_row(over_band[c][:, 0:1])
        halo_b[3, c : c + 1, :] = to_row(over_band[c][:, nodes_b - 1 :])
    second = halo_copies(1)
    for copy in second:
        copy.start()
    slopes[0] = s11
    slopes[1] = s12
    slopes[3] = s22
    slopes[4] = t1
    slopes[5] = t2

    to_scalars.wait()

    def stay_here():
        span = pl.ds(FINAL_LINE + y * RING_SECOND, RING_SECOND)
        return pltpu.make_async_copy(here_got, final.at[span], local_sem.at[1])

    def stay(j):
        low, n = ring_spans[j]
        return pltpu.make_async_copy((ring_got, ring_far)[j], final.at[pl.ds(low, n)], local_sem.at[1 + j])

    @pl.when(core == 0)
    def _():
        for j in range(2):
            for i in ((0, 1), (2,))[j]:
                ring_first(i).wait()

            def fill(p, carry, j=j):
                cell = at_index(table, 0, p, FINAL_RING)
                held = ring_got if j == 0 else ring_far
                cell = jnp.clip(cell - j * NEAR, 0, held.shape[0] - 1)
                for m in range(PACK // 8):
                    send2[p, 8 * m : 8 * m + 8, :] = held[cell, 8 * m : 8 * m + 8, :]
                return carry

            for k in ((0, 1), (2,))[j]:
                low, n = line_spans[k]
                lax.fori_loop(low, low + n, fill, 0)
                line_second(k).start()
            share_ring(j).start()
            stay(j).start()

    @pl.when(core == 1)
    def _():
        line_first().wait()
        for i in range(12):
            j, h = pieces[i] if i < 9 else (3, i - 9)
            to = lax.rem(y + (STEPS[j] if j < 3 else 0), RING)

            def fill(p, carry, j=j, to=to):
                index = at_index(table, 0, to * RING_SECOND + p, 2 * CAP)
                mine = index < CAP
                here, there = jnp.minimum(index, CAP - 1), jnp.maximum(index - CAP, 0)
                for m in range(PACK // 8):
                    v = jnp.where(mine, own[here, 8 * m : 8 * m + 8, :], line_got[there, 8 * m : 8 * m + 8, :])
                    if j < 3:
                        send2[j * RING_SECOND + p, 8 * m : 8 * m + 8, :] = v
                    else:
                        here_got[p, 8 * m : 8 * m + 8, :] = v
                return carry

            lax.fori_loop(h * half, (h + 1) * half, fill, 0)
            if j < 3:
                ring_second(i).start()
        share_line(0).start()
        stay_here().start()

    for copy in second:
        copy.wait()
    edge = []
    for c in range(3):
        before = jnp.where(inner_left, to_column(got_b[3, c : c + 1, :]), 0.0)
        after = jnp.where(inner_right, to_column(got_b[2, c : c + 1, :]), 0.0)
        edge.append((before, after))
    pairs = ((0, 1), (1, 3), (4, 5))
    for c, (p, q) in enumerate(pairs):
        value = gore_diff(slopes[p], got_g[3, c : c + 1, :], got_g[2, c : c + 1, :])
        value = value + band_diff(slopes[q], *edge[c])
        if c == 2:
            value = value + press_ref[...]
        force_ref[c] = value
    @pl.when(core == 0)
    def _():
        for j in range(3):
            line_second(j).wait()
            share_ring(2 + j).start()
        for j in range(2):
            stay(j).wait()
        for j in range(5):
            share_ring(j).wait_send()
        for i in range(10):
            share_line_in(i).wait_recv()

    @pl.when(core == 1)
    def _():
        for i in range(9):
            ring_second(i).wait()
            share_line(1 + i).start()
        stay_here().wait()
        for i in range(10):
            share_line(i).wait_send()
        for j in range(5):
            share_ring_in(j).wait_recv()

    for d in range(1, n_band):
        flag_copy(d).wait()
    total = flag[...]
    for d in range(1, n_band):
        total = total + flag_got[lax.rem(b + d, n_band)]
    flag_ref[0] = jnp.sum(total[0:1, :].astype(F32)).astype(jnp.int32)

    keep.wait()
    hand_on.wait()


def place_kernel(table, final, result, got, made, in_sem, out_sem):
    tiles, groups = VOX // 128, GROUP * MOST // 8

    def load(p):
        cell = jnp.clip(table[1, p] - 1, 0, FINAL - 1)
        return pltpu.make_async_copy(final.at[cell], got.at[p], in_sem.at[p])

    for p in range(GROUP * MOST):

        @pl.when(table[1, p] > 0)
        def _(p=p):
            load(p).start()

    def clear(i, carry):
        made[pl.ds(pl.multiple_of(i * 216, 216), 216), :] = jnp.zeros((216, 128), F32)
        return carry

    lax.fori_loop(0, 3 * groups * tiles * 8 // 216, clear, 0)

    def one(p, carry):
        @pl.when(table[1, p] > 0)
        def _():
            load(p).wait()
            for m in range(PACK // 8):
                v = got[p, 8 * m : 8 * m + 8, :]
                row = 8 * m
                while row < min(8 * m + 8, ROWS):
                    c, tile = row // tiles, row % tiles
                    count = min(8 * m + 8, (c + 1) * tiles) - row
                    start = ((c * groups + p // 8) * tiles + tile) * 8 + p % 8
                    made[pl.ds(start, count, stride=8), :] = v[row - 8 * m : row - 8 * m + count]
                    row = row + count

        return carry

    stores = []
    for t in range(groups):
        lax.fori_loop(8 * t, 8 * t + 8, one, 0)
        for c in range(3):
            span = pl.ds((c * groups + t) * tiles * 8, tiles * 8)
            stores.append(pltpu.make_async_copy(made.at[span], result.at[span], out_sem.at[3 * t + c]))
            stores[-1].start()
    for copy in stores:
        copy.wait()


def place(table, final):
    hbm = pl.BlockSpec(memory_space=pltpu.HBM)
    slots = GROUP * MOST
    result = pl.pallas_call(
        place_kernel,
        out_shape=jax.ShapeDtypeStruct((3 * slots * VOX // 128, 128), F32),
        in_specs=[pl.BlockSpec(memory_space=pltpu.SMEM), hbm],
        out_specs=hbm,
        scratch_shapes=[
            pltpu.VMEM((slots, PACK, 128), F32),
            pltpu.VMEM((3 * slots * VOX // 128, 128), F32),
            pltpu.SemaphoreType.DMA((slots,)),
            pltpu.SemaphoreType.DMA((3 * slots // 8,)),
        ],
        compiler_params=pltpu.CompilerParams(vmem_limit_bytes=60 * 2**20),
        name="place",
    )(table, final)
    return in_place(slots, result)


def in_place(slots, result):
    tiles = result.reshape(3, slots // 8, VOX // 128, 8, 128)
    return tiles.transpose(0, 1, 3, 2, 4).reshape(3, slots, VOX)


def send_all(workers, own, n_gore, slots):
    states = own[:, :ROWS].reshape(CAP, 3, VOX)
    onehot = (workers[:, None] == jnp.arange(n_gore, dtype=jnp.int32)[None, :]).astype(jnp.int32)
    earlier = jnp.cumsum(onehot, axis=0) - onehot
    slot_index = workers * MOST + jnp.sum(earlier * onehot, axis=1)
    outgoing = jnp.zeros((slots, 3, VOX), F32).at[slot_index].set(states)
    arrived = lax.all_to_all(
        outgoing.reshape(n_gore, MOST, 3, VOX), "gore", split_axis=0, concat_axis=0, tiled=True
    )
    return arrived.reshape(slots, 3, VOX).transpose(1, 0, 2)


def local(displacement, stiffness, pressure, yield_points, route, cell_state, weave):
    n_gore, n_band = lax.axis_size("gore"), lax.axis_size("band")
    slots = n_gore * MOST
    nodes_g, nodes_b = stiffness.shape
    plane_high, plane_low, line, weight = tables()
    vmem, hbm = pl.BlockSpec(memory_space=pltpu.VMEM), pl.BlockSpec(memory_space=pltpu.HBM)
    n = G * CAP
    vm, dma = pltpu.VMEM, pltpu.SemaphoreType.DMA
    workers = route.reshape(-1)
    force, flag, table, final, own = pl.pallas_call(
        lambda *refs: kernel(n_gore, n_band, *refs),
        out_shape=(
            jax.ShapeDtypeStruct((3, nodes_g, nodes_b), F32),
            jax.ShapeDtypeStruct((1,), jnp.int32),
            jax.ShapeDtypeStruct((8, 128), jnp.int32),
            jax.ShapeDtypeStruct((FINAL, PACK, 128), F32),
            jax.ShapeDtypeStruct((CAP, PACK, 128), F32),
        ),
        in_specs=[hbm] * 11,
        out_specs=(vmem, pl.BlockSpec(memory_space=pltpu.SMEM), hbm, hbm, hbm),
        scratch_shapes=[
            pltpu.SMEM((CAP,), jnp.int32),
            pltpu.SMEM((CAP,), jnp.int32),
            vm((3, nodes_g, nodes_b), F32),
            vm((nodes_g, nodes_b), F32),
            vm((nodes_g, nodes_b), F32),
            vm((3, CAP, VOX), F32),
            vm((VOX // 128, 128), F32),
            vm((PLANE, PLANE), BF16),
            vm((PLANE, PLANE), BF16),
            vm((2 * n, n), BF16),
            vm((G, 1, PLANE), F32),
            vm((4, 8, nodes_b), F32),
            vm((4, 8, nodes_g), F32),
            vm((4, 8, nodes_b), F32),
            vm((4, 8, nodes_g), F32),
            vm((6, nodes_g, nodes_b), F32),
            vm((3, nodes_g, nodes_b), F32),
            vm((3, n, PLANE), F32),
            vm((n, PLANE), F32),
            vm((n + 16, PLANE), F32),
            vm((n, PLANE), F32),
            vm((2 * n, PLANE), BF16),
            vm((n + 16, PLANE), F32),
            vm((PACK * CAP, 128), F32),
            vm((8, 128), jnp.int32),
            vm((n_gore, 8, 128), jnp.int32),
            vm((8, 128), jnp.int32),
            vm((n_band, 8, 128), jnp.int32),
            vm((8, 128), jnp.int32),
            pltpu.SMEM((8, 128), jnp.int32),
            vm((8, 128), jnp.int32),
            pltpu.SMEM((8, 128), jnp.int32),
            vm((CAP, PACK, 128), F32),
            vm((3 * RING_FIRST, PACK, 128), F32),
            vm((3 * RING_SECOND, PACK, 128), F32),
            vm((NEAR, PACK, 128), F32),
            vm((RING_FIRST, PACK, 128), F32),
            vm((LINE_FIRST, PACK, 128), F32),
            vm((RING_SECOND, PACK, 128), F32),
            dma((11,)),
            dma((8,)),
            dma((8,)),
            dma((n_gore,)),
            dma((n_gore,)),
            dma((n_band,)),
            dma((n_band,)),
            dma((3,)),
            dma((3,)),
            dma((3,)),
            dma((9,)),
            dma((9,)),
            dma((10,)),
            dma((10,)),
            dma((3,)),
        ],
        compiler_params=pltpu.CompilerParams(
            collective_id=0, has_side_effects=True, vmem_limit_bytes=60 * 2**20
        ),
        name="cells",
    )(
        yield_points,
        workers,
        displacement,
        stiffness,
        pressure,
        cell_state.transpose(1, 0, 2),
        weave.reshape(VOX // 128, 128),
        jnp.asarray(plane_high),
        jnp.asarray(plane_low),
        jnp.asarray(line),
        jnp.asarray(weight),
    )
    cell_strain = lax.cond(
        flag[0] == 0,
        lambda table, final, own, workers: place(table, final),
        lambda table, final, own, workers: send_all(workers, own, n_gore, slots),
        table, final, own, workers,
    )
    return force, cell_strain.transpose(1, 0, 2)


def solution(mesh):
    return jax.shard_map(
        local,
        mesh=mesh,
        in_specs=(
            P(None, "gore", "band"),
            P("gore", "band"),
            P("gore", "band"),
            P(("gore", "band")),
            P(("gore", "band"), None),
            P(("gore", "band"), None, None),
            P(),
        ),
        out_specs=(P(None, "gore", "band"), P(("gore", "band"), None, None)),
        check_vma=False,
    )
```

```python
import math

import jax
import jax.numpy as jnp
import numpy as np
from jax import lax
from jax.experimental import pallas as pl
from jax.experimental.pallas import tpu as pltpu
from jax.sharding import PartitionSpec as P

G = 24
PLANE = G * G
VOX = G * G * G
SWEEPS = 2
POISSON = 0.3
CAP = 8
MOST = 2
ROWS = 3 * VOX // 128
PACK = 328
RING, LINE, CORE = 4, 2, 2
GROUP = RING * LINE * CORE
RING_FIRST, LINE_NEAR, LINE_FAR, LINE_FIRST, RING_SECOND = 5, 9, 3, 8, 6
STEPS = (1, 3, 2)
FINAL_RING = RING * RING_FIRST
FINAL_LINE = FINAL_RING + LINE_NEAR + LINE_FAR
NEAR = (RING - 1) * RING_FIRST
FINAL = FINAL_LINE + RING * RING_SECOND
MESH = pl.DeviceIdType.MESH
F32 = jnp.float32
BF16 = jnp.bfloat16


def tables():
    n = np.arange(G)
    phase = 2.0 * np.pi * (np.outer(n, n) % G) / G
    hartley = (np.cos(phase) + np.sin(phase)) / math.sqrt(G)
    plane = np.kron(hartley, hartley)
    line = np.kron(hartley, np.eye(CAP))

    def split(a):
        high = a.astype(np.float32).astype(jnp.bfloat16)
        low = (a - high.astype(np.float64)).astype(np.float32).astype(jnp.bfloat16)
        return high, low

    square = np.sin(phase[1]) ** 2
    summed = square[:, None, None] + square[None, :, None] + square[None, None, :]
    level = n % (G // 2) == 0
    silent = level[:, None, None] & level[None, :, None] & level[None, None, :]
    weight = np.where(silent, 0.0, 1.0 / (10.0 * np.where(silent, 1.0, summed)))
    plane_high, plane_low = split(plane)
    line_high, line_low = split(line)
    return (
        plane_high,
        plane_low,
        np.concatenate([line_high, line_low], axis=0),
        weight.reshape(G, 1, PLANE).astype(np.float32),
    )


def shifted(v, k):
    k = k % v.shape[1]
    return jnp.concatenate([v[:, k:], v[:, :k]], axis=1)


def diff_upper(v):
    return shifted(v, G) - shifted(v, -G)


def diff_lower(v, low):
    forward = jnp.where(low == G - 1, shifted(v, 1 - G), shifted(v, 1))
    backward = jnp.where(low == 0, shifted(v, G - 1), shifted(v, -1))
    return forward - backward


def to_row(column):
    n = column.shape[0]
    diagonal = lax.broadcasted_iota(jnp.int32, (n, n), 0) == lax.broadcasted_iota(jnp.int32, (n, n), 1)
    return jnp.sum(jnp.where(diagonal, column, 0.0), axis=0, keepdims=True)


def to_column(row):
    n = row.shape[1]
    diagonal = lax.broadcasted_iota(jnp.int32, (n, n), 0) == lax.broadcasted_iota(jnp.int32, (n, n), 1)
    return jnp.sum(jnp.where(diagonal, row, 0.0), axis=1, keepdims=True)


def gore_diff(v, before, after):
    down = jnp.concatenate([v[1:], after], axis=0)
    up = jnp.concatenate([before, v[:-1]], axis=0)
    return (down - up) * 0.5


def band_diff(v, before, after):
    right = jnp.concatenate([v[:, 1:], after], axis=1)
    left = jnp.concatenate([before, v[:, :-1]], axis=1)
    return (right - left) * 0.5


def rank_of(key, key_column, earlier):
    return jnp.sum(jnp.where((key_column == key) & earlier, 1.0, 0.0), axis=0, keepdims=True)


def routing(worker, g):
    n = GROUP * CAP
    lane = lax.broadcasted_iota(jnp.int32, (1, n), 1)
    to = worker.astype(jnp.int32)
    source = lane >> 3
    to_y, to_z = to >> 2, (to >> 1) & 1
    from_y, from_z, from_c = source >> 2, (source >> 1) & 1, source & 1
    y, z, c = g >> 2, (g >> 1) & 1, g & 1
    crossing, first = to_z != from_z, from_c == 0
    alone = -1 - lane
    earlier = lax.broadcasted_iota(jnp.int32, (n, n), 0) < lax.broadcasted_iota(jnp.int32, (n, n), 1)

    def rank(key):
        key = key.astype(F32)
        return rank_of(key, to_column(key), earlier).astype(jnp.int32)

    own, mine = source == g, from_c == c
    at_ring = c == 0
    cell = lane & 7
    column = lax.broadcasted_iota(jnp.int32, (n, n), 1).astype(F32)

    def listing(place, index):
        place, index = to_column(place.astype(F32)), to_column(index.astype(F32) + 1.0)
        return jnp.sum(jnp.where(place == column, index, 0.0), axis=0, keepdims=True).astype(jnp.int32)

    ahead = (from_y + RING - to_y) & (RING - 1)
    block = jnp.where(ahead == 3, 1, jnp.where(ahead == 1, 2, jnp.where(ahead == 2, 3, 0)))
    far = jnp.where(ahead == 2, 1, 0)
    ring_first = rank(source * RING + to_y)
    line_first = rank(jnp.where(crossing, source, alone))
    place1_ring = jnp.where(own, to_y * RING_FIRST + ring_first, -1)
    place1 = jnp.where(at_ring, place1_ring, jnp.where(own & crossing, line_first, -1))

    def later():
        line_second = rank(jnp.where(first & crossing, (from_z * RING + to_y) * 2 + far, alone))
        line_over = line_second >= LINE_NEAR + far * (LINE_FAR - LINE_NEAR)
        line_second = line_second + far * LINE_NEAR
        ring_second = rank(jnp.where(first, alone, (from_y * RING + to_y) * LINE + to_z))
        slot = rank(source * GROUP + to)
        over = first & ((ring_first >= RING_FIRST) | (crossing & line_over))
        over = over | (jnp.logical_not(first) & (ring_second >= RING_SECOND))
        place2_ring = jnp.where(mine & crossing & (from_z == z) & (to_y == y), line_second, -1)
        place2_line = jnp.where(mine & (from_y == y) & (to_z == z), to_y * RING_SECOND + ring_second, -1)
        place2 = jnp.where(at_ring, place2_ring, place2_line)
        from_ring = block * RING_FIRST + ring_first
        from_line = jnp.where(from_z == z, cell, CAP + line_first)
        index2 = jnp.where(at_ring, from_ring, from_line)
        place3 = jnp.where(to == g, source * MOST + slot, -1)
        index3 = jnp.where(crossing, FINAL_RING + line_second, from_ring)
        index3 = jnp.where(first, index3, FINAL_LINE + from_y * RING_SECOND + ring_second)
        over = jnp.sum(jnp.where(over, 1.0, 0.0), axis=1, keepdims=True)
        return listing(place2, index2), listing(place3, index3), over

    return listing(place1, cell), later


def kernel(
    n_gore, n_band,
    yield_hbm, route_hbm, disp_hbm, stiff_hbm, press_hbm, state_hbm, weave_hbm,
    plane_hi_hbm, plane_lo_hbm, line_hbm, weight_hbm,
    force_ref, flag_ref, table_ref, final, own_ref,
    yield_ref, route_ref, disp_ref, stiff_ref, press_ref, state_ref, weave_ref,
    plane_hi_ref, plane_lo_ref, line_ref, weight_ref,
    halo_g, halo_b, got_g, got_b, slopes, strain_s,
    e_s, w_s, s_pad, d_s, x_s, f_s, cells,
    names, names_got, flag, flag_got, hop1_v, hop1_table, table_v, table,
    own, send1, send2, ring_got, ring_far, line_got, here_got,
    in_sem, halo_send, halo_recv, name_send, name_recv, flag_send, flag_recv, table_sem,
    hop1_send, hop1_recv, hop2_send, hop2_recv, share_send, share_recv, local_sem,
):
    g, b = lax.axis_index("gore"), lax.axis_index("band")
    y, z, core = lax.div(g, LINE * CORE), lax.rem(lax.div(g, CORE), LINE), lax.rem(g, CORE)
    up, down = lax.rem(g + 1, n_gore), lax.rem(g + n_gore - 1, n_gore)
    right, left = lax.rem(b + 1, n_band), lax.rem(b + n_band - 1, n_band)
    nodes_g, nodes_b = stiff_ref.shape

    barrier = pltpu.get_barrier_semaphore()
    for d in range(1, n_gore):
        pl.semaphore_signal(barrier, inc=1, device_id=(lax.rem(g + d, n_gore), b), device_id_type=MESH)
    for d in range(1, n_band):
        pl.semaphore_signal(barrier, inc=1, device_id=(g, lax.rem(b + d, n_band)), device_id_type=MESH)

    operands = (
        (route_hbm, route_ref), (disp_hbm, disp_ref), (yield_hbm, yield_ref), (state_hbm, state_ref),
        (weave_hbm, weave_ref), (stiff_hbm, stiff_ref), (plane_hi_hbm, plane_hi_ref),
        (plane_lo_hbm, plane_lo_ref), (line_hbm, line_ref), (weight_hbm, weight_ref), (press_hbm, press_ref),
    )
    loads = [pltpu.make_async_copy(p, q, in_sem.at[i]) for i, (p, q) in enumerate(operands)]
    for copy in loads:
        copy.start()

    def halo_copies(k):
        out = []
        for side, target in enumerate(((down, b), (up, b), (g, left), (g, right))):
            source, place = (halo_g, got_g) if side < 2 else (halo_b, got_b)
            out.append(
                pltpu.make_async_remote_copy(
                    src_ref=source.at[2 * k + side % 2],
                    dst_ref=place.at[2 * k + side % 2],
                    send_sem=halo_send.at[4 * k + side],
                    recv_sem=halo_recv.at[4 * k + side],
                    device_id=target,
                    device_id_type=MESH,
                )
            )
        return out

    def name_copy(d):
        return pltpu.make_async_remote_copy(
            src_ref=names, dst_ref=names_got.at[g], send_sem=name_send.at[d], recv_sem=name_recv.at[d],
            device_id=(lax.rem(g + d, n_gore), b), device_id_type=MESH,
        )

    def flag_copy(d):
        return pltpu.make_async_remote_copy(
            src_ref=flag, dst_ref=flag_got.at[b], send_sem=flag_send.at[d], recv_sem=flag_recv.at[d],
            device_id=(g, lax.rem(b + d, n_band)), device_id_type=MESH,
        )

    loads[0].wait()
    place = lax.broadcasted_iota(jnp.int32, (8, 128), 1)
    named = jnp.zeros((8, 128), jnp.int32)
    for r in range(CAP):
        named = jnp.where(place == g * CAP + r, route_ref[r], named)
    names[...] = named
    loads[1].wait()
    for c in range(3):
        v = disp_ref[c]
        halo_g[0, c : c + 1, :] = v[0:1]
        halo_g[1, c : c + 1, :] = v[nodes_g - 1 :]
        halo_b[0, c : c + 1, :] = to_row(v[:, 0:1])
        halo_b[1, c : c + 1, :] = to_row(v[:, nodes_b - 1 :])
    pl.semaphore_wait(barrier, n_gore + n_band - 2)
    first = halo_copies(0)
    for copy in first:
        copy.start()
    for d in range(1, n_gore):
        name_copy(d).start()

    loads[3].wait()
    loads[4].wait()

    def load_states(i, sums):
        at = pl.multiple_of(i * 16, 16)
        out = []
        for c in range(3):
            pair = state_ref[c, :, pl.ds(pl.multiple_of(i * 2 * PLANE, 128), 2 * PLANE)]
            even, odd = pair[:, :PLANE], pair[:, PLANE:]
            e_s[c, pl.ds(at, 16), :] = jnp.concatenate([even, odd], axis=0)
            out.append(sums[c] + even + odd)
        rows = [jnp.broadcast_to(weave_ref[pl.ds(i * 9 + t, 1), :], (CAP, 128)) for t in range(9)]
        pair = jnp.concatenate(rows, axis=1)
        w_s[pl.ds(at, 16), :] = jnp.concatenate([pair[:, :PLANE], pair[:, PLANE:]], axis=0)
        return tuple(out)

    zero = jnp.zeros((CAP, PLANE), F32)
    sums = lax.fori_loop(0, G // 2, load_states, (zero, zero, zero), unroll=True)
    means = [jnp.sum(s, axis=1, keepdims=True) * (1.0 / VOX) for s in sums]

    for d in range(1, n_gore):
        name_copy(d).wait()
    for copy in first:
        copy.wait()

    worker = names[0:1, :]
    for d in range(1, n_gore):
        worker = worker + names_got[lax.rem(g + d, n_gore), 0:1, :]
    hop1_v[...] = jnp.broadcast_to(routing(worker.astype(F32), g)[0], (8, 128))
    hop1_scalars = pltpu.make_async_copy(hop1_v, hop1_table, table_sem.at[0])
    hop1_scalars.start()

    inner_left, inner_right = b > 0, b < n_band - 1
    for c in range(3):
        v = disp_ref[c]
        before = jnp.where(inner_left, to_column(got_b[1, c : c + 1, :]), 0.0)
        after = jnp.where(inner_right, to_column(got_b[0, c : c + 1, :]), 0.0)
        slopes[c] = gore_diff(v, got_g[1, c : c + 1, :], got_g[0, c : c + 1, :])
        slopes[3 + c] = band_diff(v, before, after)
    gz, bz = slopes[2], slopes[5]
    strain_s[0] = slopes[0] + 0.5 * gz * gz
    strain_s[1] = slopes[4] + 0.5 * bz * bz
    strain_s[2] = 0.5 * (slopes[3] + slopes[1]) + 0.5 * gz * bz

    loads[2].wait()
    cell_row = lax.broadcasted_iota(jnp.int32, (CAP, 1), 0)
    lane = lax.broadcasted_iota(jnp.int32, (CAP, nodes_b), 1)
    points = [yield_ref[r] for r in range(CAP)]
    wanted = jnp.zeros((CAP, 1), jnp.int32)
    for r in range(CAP):
        wanted = jnp.where(cell_row == r, lax.rem(points[r], nodes_b), wanted)
    shift = []
    for c in range(3):
        rows = [strain_s[c, pl.ds(lax.div(points[r], nodes_b), 1), :] for r in range(CAP)]
        rows = jnp.concatenate(rows, axis=0)
        drive = jnp.sum(jnp.where(lane == wanted, rows, 0.0), axis=1, keepdims=True)
        drive = drive - means[c]
        shift.append(jnp.concatenate([drive, drive], axis=0))

    low = lax.rem(lax.broadcasted_iota(jnp.int32, (16, PLANE), 1), G)

    def advance(i, sweep):
        at = pl.multiple_of(i * 16, 16)
        e = [e_s[c, pl.ds(at, 16), :] for c in range(3)]
        if sweep == 0:
            e = [e[c] + shift[c] for c in range(3)]
        else:
            middle = f_s[pl.ds(at + 8, 16), :]
            e[0] = e[0] + 0.5 * (f_s[pl.ds(at + 16, 16), :] - f_s[pl.ds(at, 16), :])
            after, before = shifted(middle, G), shifted(middle, -G)
            e[1] = e[1] + 0.5 * (after - before)
            forward = shifted(jnp.where(low == 0, before, middle), 1)
            backward = shifted(jnp.where(low == G - 1, after, middle), -1)
            e[2] = e[2] + 0.5 * (forward - backward)
        size = e[0] * e[0] + e[1] * e[1] + e[2] * e[2]
        factor = w_s[pl.ds(at, 16), :] * (1.5 - 0.5 / (1.0 + size))
        return at, e, [factor * v for v in e]

    def parts(v):
        high = v.astype(BF16)
        return high, (v - high.astype(F32)).astype(BF16)

    def lines(v):
        high, rest = parts(v)
        both = jnp.dot(line_ref[...], high, preferred_element_type=F32)
        n = G * CAP
        return both[:n] + both[n:] + jnp.dot(line_ref[0:n, :], rest, preferred_element_type=F32)

    def planes(both):
        n = G * CAP
        out = jnp.dot(both, plane_hi_ref[...], preferred_element_type=F32)
        return out[:n] + out[n:] + jnp.dot(both[:n], plane_lo_ref[...], preferred_element_type=F32)

    for copy in loads[5:]:
        copy.wait()
    for sweep in range(SWEEPS):

        def law(i, carry, sweep=sweep):
            at, e, s = advance(i, sweep)
            for c in range(3):
                e_s[c, pl.ds(at, 16), :] = e[c]
            s_pad[pl.ds(at + 8, 16), :] = s[0]
            d_s[pl.ds(at, 16), :] = diff_upper(s[1]) + diff_lower(s[2], low)
            return carry

        lax.fori_loop(0, G // 2, law, 0, unroll=True)
        s_pad[0:8, :] = s_pad[G * 8 : G * 8 + 8, :]
        s_pad[G * 8 + 8 :, :] = s_pad[8:16, :]

        def source(i, carry):
            at = pl.multiple_of(i * 16, 16)
            v = 0.5 * (s_pad[pl.ds(at + 16, 16), :] - s_pad[pl.ds(at, 16), :] + d_s[pl.ds(at, 16), :])
            high, rest = parts(v)
            x_s[pl.ds(at, 16), :] = high
            x_s[pl.ds(G * CAP + at, 16), :] = rest
            return carry

        lax.fori_loop(0, G // 2, source, 0, unroll=True)
        spectrum = lines(planes(x_s[...]))
        weight = jnp.broadcast_to(weight_ref[...], (G, CAP, PLANE)).reshape(G * CAP, PLANE)
        back = lines(spectrum * weight)
        high, rest = parts(back)
        x_s[0 : G * CAP, :] = high
        x_s[G * CAP :, :] = rest
        f_s[8 : G * 8 + 8, :] = planes(x_s[...])
        f_s[0:8, :] = f_s[G * 8 : G * 8 + 8, :]
        f_s[G * 8 + 8 :, :] = f_s[8:16, :]

    def finish(i, sums):
        at, e, s = advance(i, SWEEPS)
        out = []
        for c in range(3):
            wide = jnp.concatenate([e[c][0:8], e[c][8:16]], axis=1)
            for t in range(2 * PLANE // 128):
                row = pl.multiple_of((c * (VOX // 128) + i * 9 + t) * CAP, CAP)
                cells[pl.ds(row, CAP), :] = wide[:, 128 * t : 128 * t + 128]
            out.append(sums[c] + s[c][0:8] + s[c][8:16])
        return tuple(out)

    sums = lax.fori_loop(0, G // 2, finish, (zero, zero, zero), unroll=True)
    point_stress = [jnp.sum(s, axis=1, keepdims=True) * (1.0 / VOX) for s in sums]

    cells[ROWS * CAP :, :] = jnp.zeros((PACK * CAP - ROWS * CAP, 128), F32)
    hop1_scalars.wait()

    def at_index(table, row, position, bound):
        return jnp.clip(table[row, position] - 1, 0, bound - 1)

    def tiles_of(cell, m):
        return cells[pl.ds(m * 64 + cell, 8, stride=CAP), :]

    def hop(semaphores, slot, source, place, ring_place, line_place, core_place):
        send, recv = semaphores
        return pltpu.make_async_remote_copy(
            src_ref=source, dst_ref=place, send_sem=send.at[slot], recv_sem=recv.at[slot],
            device_id=((ring_place * LINE + line_place) * CORE + core_place, b), device_id_type=MESH,
        )

    one, two, three = (hop1_send, hop1_recv), (hop2_send, hop2_recv), (share_send, share_recv)

    def ring_first(j):
        to = lax.rem(y + STEPS[j], RING)
        n = RING_FIRST
        place = ring_got.at[pl.ds((j + 1) * n, n)] if j < 2 else ring_far
        return hop(one, j, send1.at[pl.ds(j * n, n)], place, to, z, 0)

    def line_first():
        return hop(one, 0, send1.at[pl.ds(0, LINE_FIRST)], line_got, y, 1 - z, 1)

    line_spans = ((0, 5), (5, LINE_NEAR - 5), (LINE_NEAR, LINE_FAR))

    def line_second(j):
        low, n = line_spans[j]
        return hop(two, j, send2.at[pl.ds(low, n)], final.at[pl.ds(FINAL_RING + low, n)], y, 1 - z, 0)

    half = RING_SECOND // 3
    pieces = tuple((j, h) for h in range(3) for j in range(3))

    def ring_second(i):
        j, h = pieces[i]
        to = lax.rem(y + STEPS[j], RING)
        source = send2.at[pl.ds(j * RING_SECOND + h * half, half)]
        return hop(two, i, source, final.at[pl.ds(FINAL_LINE + y * RING_SECOND + h * half, half)], to, z, 1)

    ring_spans = ((0, NEAR), (NEAR, RING_FIRST)) + tuple((FINAL_RING + low, n) for low, n in line_spans)

    def share_ring(j, to=1):
        low, n = ring_spans[j]
        span = final.at[pl.ds(low, n)]
        return hop(three, j, (ring_got, ring_far, span, span, span)[j], span, y, z, to)

    def share_line(i, to=0):
        if i == 0:
            span, source = pl.ds(FINAL_LINE + y * RING_SECOND, RING_SECOND), here_got
        else:
            j, h = pieces[i - 1]
            from_y = lax.rem(y + RING - STEPS[j], RING)
            span = pl.ds(FINAL_LINE + from_y * RING_SECOND + h * half, half)
            source = final.at[span]
        return hop(three, i, source, final.at[span], y, z, to)

    def share_line_in(i):
        return share_line(i, 1)

    def share_ring_in(j):
        return share_ring(j, 0)

    @pl.when(core == 0)
    def _():
        for j in range(RING):
            to = lax.rem(y + (STEPS[j] if j < 3 else 0), RING)

            def fill(p, carry, j=j, to=to):
                cell = at_index(hop1_table, 0, to * RING_FIRST + p, CAP)
                for m in range(PACK // 8):
                    v = tiles_of(cell, m)
                    if j < 3:
                        send1[j * RING_FIRST + p, 8 * m : 8 * m + 8, :] = v
                    else:
                        ring_got[p, 8 * m : 8 * m + 8, :] = v
                return carry

            lax.fori_loop(0, RING_FIRST, fill, 0)
            if j < 3:
                ring_first(j).start()

    @pl.when(core == 1)
    def _():
        def fill(p, carry):
            cell = at_index(hop1_table, 0, p, CAP)
            for m in range(PACK // 8):
                send1[p, 8 * m : 8 * m + 8, :] = tiles_of(cell, m)
            return carry

        lax.fori_loop(0, LINE_FIRST, fill, 0)
        line_first().start()

    list2, list3, over = routing(worker.astype(F32), g)[1]()
    table_v[0:1, :] = list2
    table_v[1:2, :] = list3
    to_scalars = pltpu.make_async_copy(table_v, table, table_sem.at[1])
    to_scalars.start()
    hand_on = pltpu.make_async_copy(table_v, table_ref, table_sem.at[2])
    hand_on.start()
    flag[...] = jnp.broadcast_to(over, (8, 128)).astype(jnp.int32)
    for d in range(1, n_band):
        flag_copy(d).start()
    for r in range(CAP):

        def gather(m, carry, r=r):
            own[r, pl.ds(pl.multiple_of(m * 8, 8), 8), :] = cells[pl.ds(m * 64 + r, 8, stride=CAP), :]
            return carry

        lax.fori_loop(0, PACK // 8, gather, 0, unroll=True)
    keep = pltpu.make_async_copy(own, own_ref, local_sem.at[0])
    keep.start()

    stiff = stiff_ref[...]
    e11, e22, e12 = strain_s[0], strain_s[1], strain_s[2]
    stress = [
        stiff * (e11 + POISSON * e22),
        stiff * (e22 + POISSON * e11),
        stiff * (1.0 - POISSON) * e12,
    ]
    node = lax.broadcasted_iota(jnp.int32, stiff.shape, 0) * nodes_b + lax.broadcasted_iota(jnp.int32, stiff.shape, 1)
    for r in range(CAP):
        here = node == points[r]
        for c in range(3):
            stress[c] = jnp.where(here, point_stress[c][r : r + 1, :], stress[c])
    s11, s22, s12 = stress
    gz, bz = slopes[2], slopes[5]
    t1 = s11 * gz + s12 * bz
    t2 = s12 * gz + s22 * bz
    over_gore, over_band = [s11, s12, t1], [s12, s22, t2]
    for c in range(3):
        halo_g[2, c : c + 1, :] = over_gore[c][0:1]
        halo_g[3, c : c + 1, :] = over_gore[c][nodes_g - 1 :]
        halo_b[2, c : c + 1, :] = to_row(over_band[c][:, 0:1])
        halo_b[3, c : c + 1, :] = to_row(over_band[c][:, nodes_b - 1 :])
    second = halo_copies(1)
    for copy in second:
        copy.start()
    slopes[0] = s11
    slopes[1] = s12
    slopes[3] = s22
    slopes[4] = t1
    slopes[5] = t2

    to_scalars.wait()

    def stay_here():
        span = pl.ds(FINAL_LINE + y * RING_SECOND, RING_SECOND)
        return pltpu.make_async_copy(here_got, final.at[span], local_sem.at[1])

    def stay(j):
        low, n = ring_spans[j]
        return pltpu.make_async_copy((ring_got, ring_far)[j], final.at[pl.ds(low, n)], local_sem.at[1 + j])

    @pl.when(core == 0)
    def _():
        for j in range(2):
            for i in ((0, 1), (2,))[j]:
                ring_first(i).wait()

            def fill(p, carry, j=j):
                cell = at_index(table, 0, p, FINAL_RING)
                held = ring_got if j == 0 else ring_far
                cell = jnp.clip(cell - j * NEAR, 0, held.shape[0] - 1)
                for m in range(PACK // 8):
                    send2[p, 8 * m : 8 * m + 8, :] = held[cell, 8 * m : 8 * m + 8, :]
                return carry

            for k in ((0, 1), (2,))[j]:
                low, n = line_spans[k]
                lax.fori_loop(low, low + n, fill, 0)
                line_second(k).start()
            share_ring(j).start()
            stay(j).start()

    @pl.when(core == 1)
    def _():
        line_first().wait()
        for i in range(12):
            j, h = pieces[i] if i < 9 else (3, i - 9)
            to = lax.rem(y + (STEPS[j] if j < 3 else 0), RING)

            def fill(p, carry, j=j, to=to):
                index = at_index(table, 0, to * RING_SECOND + p, 2 * CAP)
                mine = index < CAP
                here, there = jnp.minimum(index, CAP - 1), jnp.maximum(index - CAP, 0)
                for m in range(PACK // 8):
                    v = jnp.where(mine, own[here, 8 * m : 8 * m + 8, :], line_got[there, 8 * m : 8 * m + 8, :])
                    if j < 3:
                        send2[j * RING_SECOND + p, 8 * m : 8 * m + 8, :] = v
                    else:
                        here_got[p, 8 * m : 8 * m + 8, :] = v
                return carry

            lax.fori_loop(h * half, (h + 1) * half, fill, 0)
            if j < 3:
                ring_second(i).start()
        share_line(0).start()
        stay_here().start()

    for copy in second:
        copy.wait()
    edge = []
    for c in range(3):
        before = jnp.where(inner_left, to_column(got_b[3, c : c + 1, :]), 0.0)
        after = jnp.where(inner_right, to_column(got_b[2, c : c + 1, :]), 0.0)
        edge.append((before, after))
    pairs = ((0, 1), (1, 3), (4, 5))
    for c, (p, q) in enumerate(pairs):
        value = gore_diff(slopes[p], got_g[3, c : c + 1, :], got_g[2, c : c + 1, :])
        value = value + band_diff(slopes[q], *edge[c])
        if c == 2:
            value = value + press_ref[...]
        force_ref[c] = value
    @pl.when(core == 0)
    def _():
        for j in range(3):
            line_second(j).wait()
            share_ring(2 + j).start()
        for j in range(2):
            stay(j).wait()
        for j in range(5):
            share_ring(j).wait_send()
        for i in range(10):
            share_line_in(i).wait_recv()

    @pl.when(core == 1)
    def _():
        for i in range(9):
            ring_second(i).wait()
            share_line(1 + i).start()
        stay_here().wait()
        for i in range(10):
            share_line(i).wait_send()
        for j in range(5):
            share_ring_in(j).wait_recv()

    for d in range(1, n_band):
        flag_copy(d).wait()
    total = flag[...]
    for d in range(1, n_band):
        total = total + flag_got[lax.rem(b + d, n_band)]
    flag_ref[0] = jnp.sum(total[0:1, :].astype(F32)).astype(jnp.int32)

    keep.wait()
    hand_on.wait()


def place_kernel(table, final, result, got, made, in_sem, out_sem):
    tiles, groups = VOX // 128, GROUP * MOST // 8

    def load(p):
        cell = jnp.clip(table[1, p] - 1, 0, FINAL - 1)
        return pltpu.make_async_copy(final.at[cell], got.at[p], in_sem.at[p])

    for p in range(GROUP * MOST):

        @pl.when(table[1, p] > 0)
        def _(p=p):
            load(p).start()

    def clear(i, carry):
        made[pl.ds(pl.multiple_of(i * 216, 216), 216), :] = jnp.zeros((216, 128), F32)
        return carry

    lax.fori_loop(0, 3 * groups * tiles * 8 // 216, clear, 0)

    def one(p, carry):
        @pl.when(table[1, p] > 0)
        def _():
            load(p).wait()
            for m in range(PACK // 8):
                v = got[p, 8 * m : 8 * m + 8, :]
                row = 8 * m
                while row < min(8 * m + 8, ROWS):
                    c, tile = row // tiles, row % tiles
                    count = min(8 * m + 8, (c + 1) * tiles) - row
                    start = ((c * groups + p // 8) * tiles + tile) * 8 + p % 8
                    made[pl.ds(start, count, stride=8), :] = v[row - 8 * m : row - 8 * m + count]
                    row = row + count

        return carry

    stores = []
    for t in range(groups):
        lax.fori_loop(8 * t, 8 * t + 8, one, 0)
        for c in range(3):
            span = pl.ds((c * groups + t) * tiles * 8, tiles * 8)
            stores.append(pltpu.make_async_copy(made.at[span], result.at[span], out_sem.at[3 * t + c]))
            stores[-1].start()
    for copy in stores:
        copy.wait()


def place(table, final):
    hbm = pl.BlockSpec(memory_space=pltpu.HBM)
    slots = GROUP * MOST
    result = pl.pallas_call(
        place_kernel,
        out_shape=jax.ShapeDtypeStruct((3 * slots * VOX // 128, 128), F32),
        in_specs=[pl.BlockSpec(memory_space=pltpu.SMEM), hbm],
        out_specs=hbm,
        scratch_shapes=[
            pltpu.VMEM((slots, PACK, 128), F32),
            pltpu.VMEM((3 * slots * VOX // 128, 128), F32),
            pltpu.SemaphoreType.DMA((slots,)),
            pltpu.SemaphoreType.DMA((3 * slots // 8,)),
        ],
        compiler_params=pltpu.CompilerParams(vmem_limit_bytes=60 * 2**20),
        name="place",
    )(table, final)
    return in_place(slots, result)


def in_place(slots, result):
    tiles = result.reshape(3, slots // 8, VOX // 128, 8, 128)
    return tiles.transpose(0, 1, 3, 2, 4).reshape(3, slots, VOX)


def send_all(workers, own, n_gore, slots):
    states = own[:, :ROWS].reshape(CAP, 3, VOX)
    onehot = (workers[:, None] == jnp.arange(n_gore, dtype=jnp.int32)[None, :]).astype(jnp.int32)
    earlier = jnp.cumsum(onehot, axis=0) - onehot
    slot_index = workers * MOST + jnp.sum(earlier * onehot, axis=1)
    outgoing = jnp.zeros((slots, 3, VOX), F32).at[slot_index].set(states)
    arrived = lax.all_to_all(
        outgoing.reshape(n_gore, MOST, 3, VOX), "gore", split_axis=0, concat_axis=0, tiled=True
    )
    return arrived.reshape(slots, 3, VOX).transpose(1, 0, 2)


def local(displacement, stiffness, pressure, yield_points, route, cell_state, weave):
    n_gore, n_band = lax.axis_size("gore"), lax.axis_size("band")
    slots = n_gore * MOST
    nodes_g, nodes_b = stiffness.shape
    plane_high, plane_low, line, weight = tables()
    vmem, hbm = pl.BlockSpec(memory_space=pltpu.VMEM), pl.BlockSpec(memory_space=pltpu.HBM)
    n = G * CAP
    vm, dma = pltpu.VMEM, pltpu.SemaphoreType.DMA
    workers = route.reshape(-1)
    force, flag, table, final, own = pl.pallas_call(
        lambda *refs: kernel(n_gore, n_band, *refs),
        out_shape=(
            jax.ShapeDtypeStruct((3, nodes_g, nodes_b), F32),
            jax.ShapeDtypeStruct((1,), jnp.int32),
            jax.ShapeDtypeStruct((8, 128), jnp.int32),
            jax.ShapeDtypeStruct((FINAL, PACK, 128), F32),
            jax.ShapeDtypeStruct((CAP, PACK, 128), F32),
        ),
        in_specs=[hbm] * 11,
        out_specs=(vmem, pl.BlockSpec(memory_space=pltpu.SMEM), hbm, hbm, hbm),
        scratch_shapes=[
            pltpu.SMEM((CAP,), jnp.int32),
            pltpu.SMEM((CAP,), jnp.int32),
            vm((3, nodes_g, nodes_b), F32),
            vm((nodes_g, nodes_b), F32),
            vm((nodes_g, nodes_b), F32),
            vm((3, CAP, VOX), F32),
            vm((VOX // 128, 128), F32),
            vm((PLANE, PLANE), BF16),
            vm((PLANE, PLANE), BF16),
            vm((2 * n, n), BF16),
            vm((G, 1, PLANE), F32),
            vm((4, 8, nodes_b), F32),
            vm((4, 8, nodes_g), F32),
            vm((4, 8, nodes_b), F32),
            vm((4, 8, nodes_g), F32),
            vm((6, nodes_g, nodes_b), F32),
            vm((3, nodes_g, nodes_b), F32),
            vm((3, n, PLANE), F32),
            vm((n, PLANE), F32),
            vm((n + 16, PLANE), F32),
            vm((n, PLANE), F32),
            vm((2 * n, PLANE), BF16),
            vm((n + 16, PLANE), F32),
            vm((PACK * CAP, 128), F32),
            vm((8, 128), jnp.int32),
            vm((n_gore, 8, 128), jnp.int32),
            vm((8, 128), jnp.int32),
            vm((n_band, 8, 128), jnp.int32),
            vm((8, 128), jnp.int32),
            pltpu.SMEM((8, 128), jnp.int32),
            vm((8, 128), jnp.int32),
            pltpu.SMEM((8, 128), jnp.int32),
            vm((CAP, PACK, 128), F32),
            vm((3 * RING_FIRST, PACK, 128), F32),
            vm((3 * RING_SECOND, PACK, 128), F32),
            vm((NEAR, PACK, 128), F32),
            vm((RING_FIRST, PACK, 128), F32),
            vm((LINE_FIRST, PACK, 128), F32),
            vm((RING_SECOND, PACK, 128), F32),
            dma((11,)),
            dma((8,)),
            dma((8,)),
            dma((n_gore,)),
            dma((n_gore,)),
            dma((n_band,)),
            dma((n_band,)),
            dma((3,)),
            dma((3,)),
            dma((3,)),
            dma((9,)),
            dma((9,)),
            dma((10,)),
            dma((10,)),
            dma((3,)),
        ],
        compiler_params=pltpu.CompilerParams(
            collective_id=0, has_side_effects=True, vmem_limit_bytes=60 * 2**20
        ),
        name="cells",
    )(
        yield_points,
        workers,
        displacement,
        stiffness,
        pressure,
        cell_state.transpose(1, 0, 2),
        weave.reshape(VOX // 128, 128),
        jnp.asarray(plane_high),
        jnp.asarray(plane_low),
        jnp.asarray(line),
        jnp.asarray(weight),
    )
    cell_strain = lax.cond(
        flag[0] == 0,
        lambda table, final, own, workers: place(table, final),
        lambda table, final, own, workers: send_all(workers, own, n_gore, slots),
        table, final, own, workers,
    )
    return force, cell_strain.transpose(1, 0, 2)


def solution(mesh):
    return jax.shard_map(
        local,
        mesh=mesh,
        in_specs=(
            P(None, "gore", "band"),
            P("gore", "band"),
            P("gore", "band"),
            P(("gore", "band")),
            P(("gore", "band"), None),
            P(("gore", "band"), None, None),
            P(),
        ),
        out_specs=(P(None, "gore", "band"), P(("gore", "band"), None, None)),
        check_vma=False,
    )
```

```python
import math

import jax
import jax.numpy as jnp
import numpy as np
from jax import lax
from jax.experimental import pallas as pl
from jax.experimental.pallas import tpu as pltpu
from jax.sharding import PartitionSpec as P

G = 24
PLANE = G * G
VOX = G * G * G
SWEEPS = 2
POISSON = 0.3
CAP = 8
MOST = 2
ROWS = 3 * VOX // 128
PACK = 328
RING, LINE, CORE = 4, 2, 2
GROUP = RING * LINE * CORE
RING_FIRST, LINE_NEAR, LINE_FAR, LINE_FIRST, RING_SECOND = 5, 9, 3, 8, 6
STEPS = (1, 3, 2)
FINAL_RING = RING * RING_FIRST
FINAL_LINE = FINAL_RING + LINE_NEAR + LINE_FAR
NEAR = (RING - 1) * RING_FIRST
FINAL = FINAL_LINE + RING * RING_SECOND
MESH = pl.DeviceIdType.MESH
F32 = jnp.float32
BF16 = jnp.bfloat16


def tables():
    n = np.arange(G)
    phase = 2.0 * np.pi * (np.outer(n, n) % G) / G
    hartley = (np.cos(phase) + np.sin(phase)) / math.sqrt(G)
    plane = np.kron(hartley, hartley)
    line = np.kron(hartley, np.eye(CAP))

    def split(a):
        high = a.astype(np.float32).astype(jnp.bfloat16)
        low = (a - high.astype(np.float64)).astype(np.float32).astype(jnp.bfloat16)
        return high, low

    square = np.sin(phase[1]) ** 2
    summed = square[:, None, None] + square[None, :, None] + square[None, None, :]
    level = n % (G // 2) == 0
    silent = level[:, None, None] & level[None, :, None] & level[None, None, :]
    weight = np.where(silent, 0.0, 1.0 / (10.0 * np.where(silent, 1.0, summed)))
    plane_high, plane_low = split(plane)
    line_high, line_low = split(line)
    return (
        plane_high,
        plane_low,
        np.concatenate([line_high, line_low], axis=0),
        weight.reshape(G, 1, PLANE).astype(np.float32),
    )


def shifted(v, k):
    k = k % v.shape[1]
    return jnp.concatenate([v[:, k:], v[:, :k]], axis=1)


def diff_upper(v):
    return shifted(v, G) - shifted(v, -G)


def diff_lower(v, low):
    forward = jnp.where(low == G - 1, shifted(v, 1 - G), shifted(v, 1))
    backward = jnp.where(low == 0, shifted(v, G - 1), shifted(v, -1))
    return forward - backward


def to_row(column):
    n = column.shape[0]
    diagonal = lax.broadcasted_iota(jnp.int32, (n, n), 0) == lax.broadcasted_iota(jnp.int32, (n, n), 1)
    return jnp.sum(jnp.where(diagonal, column, 0.0), axis=0, keepdims=True)


def to_column(row):
    n = row.shape[1]
    diagonal = lax.broadcasted_iota(jnp.int32, (n, n), 0) == lax.broadcasted_iota(jnp.int32, (n, n), 1)
    return jnp.sum(jnp.where(diagonal, row, 0.0), axis=1, keepdims=True)


def gore_diff(v, before, after):
    down = jnp.concatenate([v[1:], after], axis=0)
    up = jnp.concatenate([before, v[:-1]], axis=0)
    return (down - up) * 0.5


def band_diff(v, before, after):
    right = jnp.concatenate([v[:, 1:], after], axis=1)
    left = jnp.concatenate([before, v[:, :-1]], axis=1)
    return (right - left) * 0.5


def rank_of(key, key_column, earlier):
    return jnp.sum(jnp.where((key_column == key) & earlier, 1.0, 0.0), axis=0, keepdims=True)


def routing(worker, g):
    n = GROUP * CAP
    lane = lax.broadcasted_iota(jnp.int32, (1, n), 1)
    to = worker.astype(jnp.int32)
    source = lane >> 3
    to_y, to_z = to >> 2, (to >> 1) & 1
    from_y, from_z, from_c = source >> 2, (source >> 1) & 1, source & 1
    y, z, c = g >> 2, (g >> 1) & 1, g & 1
    crossing, first = to_z != from_z, from_c == 0
    alone = -1 - lane
    earlier = lax.broadcasted_iota(jnp.int32, (n, n), 0) < lax.broadcasted_iota(jnp.int32, (n, n), 1)

    def rank(key):
        key = key.astype(F32)
        return rank_of(key, to_column(key), earlier).astype(jnp.int32)

    own, mine = source == g, from_c == c
    at_ring = c == 0
    cell = lane & 7
    column = lax.broadcasted_iota(jnp.int32, (n, n), 1).astype(F32)

    def listing(place, index):
        place, index = to_column(place.astype(F32)), to_column(index.astype(F32) + 1.0)
        return jnp.sum(jnp.where(place == column, index, 0.0), axis=0, keepdims=True).astype(jnp.int32)

    ahead = (from_y + RING - to_y) & (RING - 1)
    block = jnp.where(ahead == 3, 1, jnp.where(ahead == 1, 2, jnp.where(ahead == 2, 3, 0)))
    far = jnp.where(ahead == 2, 1, 0)
    ring_first = rank(source * RING + to_y)
    line_first = rank(jnp.where(crossing, source, alone))
    place1_ring = jnp.where(own, to_y * RING_FIRST + ring_first, -1)
    place1 = jnp.where(at_ring, place1_ring, jnp.where(own & crossing, line_first, -1))

    def later():
        line_second = rank(jnp.where(first & crossing, (from_z * RING + to_y) * 2 + far, alone))
        line_over = line_second >= LINE_NEAR + far * (LINE_FAR - LINE_NEAR)
        line_second = line_second + far * LINE_NEAR
        ring_second = rank(jnp.where(first, alone, (from_y * RING + to_y) * LINE + to_z))
        slot = rank(source * GROUP + to)
        over = first & ((ring_first >= RING_FIRST) | (crossing & line_over))
        over = over | (jnp.logical_not(first) & (ring_second >= RING_SECOND))
        place2_ring = jnp.where(mine & crossing & (from_z == z) & (to_y == y), line_second, -1)
        place2_line = jnp.where(mine & (from_y == y) & (to_z == z), to_y * RING_SECOND + ring_second, -1)
        place2 = jnp.where(at_ring, place2_ring, place2_line)
        from_ring = block * RING_FIRST + ring_first
        from_line = jnp.where(from_z == z, cell, CAP + line_first)
        index2 = jnp.where(at_ring, from_ring, from_line)
        place3 = jnp.where(to == g, source * MOST + slot, -1)
        index3 = jnp.where(crossing, FINAL_RING + line_second, from_ring)
        index3 = jnp.where(first, index3, FINAL_LINE + from_y * RING_SECOND + ring_second)
        over = jnp.sum(jnp.where(over, 1.0, 0.0), axis=1, keepdims=True)
        return listing(place2, index2), listing(place3, index3), over

    return listing(place1, cell), later


def kernel(
    n_gore, n_band,
    yield_hbm, route_hbm, disp_hbm, stiff_hbm, press_hbm, state_hbm, weave_hbm,
    plane_hi_hbm, plane_lo_hbm, line_hbm, weight_hbm,
    force_ref, flag_ref, table_ref, final, own_ref,
    yield_ref, route_ref, disp_ref, stiff_ref, press_ref, state_ref, weave_ref,
    plane_hi_ref, plane_lo_ref, line_ref, weight_ref,
    halo_g, halo_b, got_g, got_b, slopes, strain_s,
    e_s, w_s, s_pad, d_s, x_s, f_s, cells,
    names, names_got, flag, flag_got, hop1_v, hop1_table, table_v, table,
    own, send1, send2, ring_got, ring_far, line_got, here_got,
    in_sem, halo_send, halo_recv, name_send, name_recv, flag_send, flag_recv, table_sem,
    hop1_send, hop1_recv, hop2_send, hop2_recv, share_send, share_recv, local_sem,
):
    g, b = lax.axis_index("gore"), lax.axis_index("band")
    y, z, core = lax.div(g, LINE * CORE), lax.rem(lax.div(g, CORE), LINE), lax.rem(g, CORE)
    up, down = lax.rem(g + 1, n_gore), lax.rem(g + n_gore - 1, n_gore)
    right, left = lax.rem(b + 1, n_band), lax.rem(b + n_band - 1, n_band)
    nodes_g, nodes_b = stiff_ref.shape

    barrier = pltpu.get_barrier_semaphore()
    for d in range(1, n_gore):
        pl.semaphore_signal(barrier, inc=1, device_id=(lax.rem(g + d, n_gore), b), device_id_type=MESH)
    for d in range(1, n_band):
        pl.semaphore_signal(barrier, inc=1, device_id=(g, lax.rem(b + d, n_band)), device_id_type=MESH)

    operands = (
        (route_hbm, route_ref), (disp_hbm, disp_ref), (yield_hbm, yield_ref), (state_hbm, state_ref),
        (weave_hbm, weave_ref), (stiff_hbm, stiff_ref), (plane_hi_hbm, plane_hi_ref),
        (plane_lo_hbm, plane_lo_ref), (line_hbm, line_ref), (weight_hbm, weight_ref), (press_hbm, press_ref),
    )
    loads = [pltpu.make_async_copy(p, q, in_sem.at[i]) for i, (p, q) in enumerate(operands)]
    for copy in loads:
        copy.start()

    def halo_copies(k):
        out = []
        for side, target in enumerate(((down, b), (up, b), (g, left), (g, right))):
            source, place = (halo_g, got_g) if side < 2 else (halo_b, got_b)
            out.append(
                pltpu.make_async_remote_copy(
                    src_ref=source.at[2 * k + side % 2],
                    dst_ref=place.at[2 * k + side % 2],
                    send_sem=halo_send.at[4 * k + side],
                    recv_sem=halo_recv.at[4 * k + side],
                    device_id=target,
                    device_id_type=MESH,
                )
            )
        return out

    def name_copy(d):
        return pltpu.make_async_remote_copy(
            src_ref=names, dst_ref=names_got.at[g], send_sem=name_send.at[d], recv_sem=name_recv.at[d],
            device_id=(lax.rem(g + d, n_gore), b), device_id_type=MESH,
        )

    def flag_copy(d):
        return pltpu.make_async_remote_copy(
            src_ref=flag, dst_ref=flag_got.at[b], send_sem=flag_send.at[d], recv_sem=flag_recv.at[d],
            device_id=(g, lax.rem(b + d, n_band)), device_id_type=MESH,
        )

    loads[0].wait()
    place = lax.broadcasted_iota(jnp.int32, (8, 128), 1)
    named = jnp.zeros((8, 128), jnp.int32)
    for r in range(CAP):
        named = jnp.where(place == g * CAP + r, route_ref[r], named)
    names[...] = named
    loads[1].wait()
    for c in range(3):
        v = disp_ref[c]
        halo_g[0, c : c + 1, :] = v[0:1]
        halo_g[1, c : c + 1, :] = v[nodes_g - 1 :]
        halo_b[0, c : c + 1, :] = to_row(v[:, 0:1])
        halo_b[1, c : c + 1, :] = to_row(v[:, nodes_b - 1 :])
    pl.semaphore_wait(barrier, n_gore + n_band - 2)
    first = halo_copies(0)
    for copy in first:
        copy.start()
    for d in range(1, n_gore):
        name_copy(d).start()

    loads[3].wait()
    loads[4].wait()

    def load_states(i, sums):
        at = pl.multiple_of(i * 16, 16)
        out = []
        for c in range(3):
            pair = state_ref[c, :, pl.ds(pl.multiple_of(i * 2 * PLANE, 128), 2 * PLANE)]
            even, odd = pair[:, :PLANE], pair[:, PLANE:]
            e_s[c, pl.ds(at, 16), :] = jnp.concatenate([even, odd], axis=0)
            out.append(sums[c] + even + odd)
        rows = [jnp.broadcast_to(weave_ref[pl.ds(i * 9 + t, 1), :], (CAP, 128)) for t in range(9)]
        pair = jnp.concatenate(rows, axis=1)
        w_s[pl.ds(at, 16), :] = jnp.concatenate([pair[:, :PLANE], pair[:, PLANE:]], axis=0)
        return tuple(out)

    zero = jnp.zeros((CAP, PLANE), F32)
    sums = lax.fori_loop(0, G // 2, load_states, (zero, zero, zero), unroll=True)
    means = [jnp.sum(s, axis=1, keepdims=True) * (1.0 / VOX) for s in sums]

    for d in range(1, n_gore):
        name_copy(d).wait()
    for copy in first:
        copy.wait()

    worker = names[0:1, :]
    for d in range(1, n_gore):
        worker = worker + names_got[lax.rem(g + d, n_gore), 0:1, :]
    hop1_v[...] = jnp.broadcast_to(routing(worker.astype(F32), g)[0], (8, 128))
    hop1_scalars = pltpu.make_async_copy(hop1_v, hop1_table, table_sem.at[0])
    hop1_scalars.start()

    inner_left, inner_right = b > 0, b < n_band - 1
    for c in range(3):
        v = disp_ref[c]
        before = jnp.where(inner_left, to_column(got_b[1, c : c + 1, :]), 0.0)
        after = jnp.where(inner_right, to_column(got_b[0, c : c + 1, :]), 0.0)
        slopes[c] = gore_diff(v, got_g[1, c : c + 1, :], got_g[0, c : c + 1, :])
        slopes[3 + c] = band_diff(v, before, after)
    gz, bz = slopes[2], slopes[5]
    strain_s[0] = slopes[0] + 0.5 * gz * gz
    strain_s[1] = slopes[4] + 0.5 * bz * bz
    strain_s[2] = 0.5 * (slopes[3] + slopes[1]) + 0.5 * gz * bz

    loads[2].wait()
    cell_row = lax.broadcasted_iota(jnp.int32, (CAP, 1), 0)
    lane = lax.broadcasted_iota(jnp.int32, (CAP, nodes_b), 1)
    points = [yield_ref[r] for r in range(CAP)]
    wanted = jnp.zeros((CAP, 1), jnp.int32)
    for r in range(CAP):
        wanted = jnp.where(cell_row == r, lax.rem(points[r], nodes_b), wanted)
    shift = []
    for c in range(3):
        rows = [strain_s[c, pl.ds(lax.div(points[r], nodes_b), 1), :] for r in range(CAP)]
        rows = jnp.concatenate(rows, axis=0)
        drive = jnp.sum(jnp.where(lane == wanted, rows, 0.0), axis=1, keepdims=True)
        drive = drive - means[c]
        shift.append(jnp.concatenate([drive, drive], axis=0))

    low = lax.rem(lax.broadcasted_iota(jnp.int32, (16, PLANE), 1), G)

    def advance(i, sweep):
        at = pl.multiple_of(i * 16, 16)
        e = [e_s[c, pl.ds(at, 16), :] for c in range(3)]
        if sweep == 0:
            e = [e[c] + shift[c] for c in range(3)]
        else:
            middle = f_s[pl.ds(at + 8, 16), :]
            e[0] = e[0] + 0.5 * (f_s[pl.ds(at + 16, 16), :] - f_s[pl.ds(at, 16), :])
            after, before = shifted(middle, G), shifted(middle, -G)
            e[1] = e[1] + 0.5 * (after - before)
            forward = shifted(jnp.where(low == 0, before, middle), 1)
            backward = shifted(jnp.where(low == G - 1, after, middle), -1)
            e[2] = e[2] + 0.5 * (forward - backward)
        size = e[0] * e[0] + e[1] * e[1] + e[2] * e[2]
        factor = w_s[pl.ds(at, 16), :] * (1.5 - 0.5 / (1.0 + size))
        return at, e, [factor * v for v in e]

    def parts(v):
        high = v.astype(BF16)
        return high, (v - high.astype(F32)).astype(BF16)

    def lines(v):
        high, rest = parts(v)
        both = jnp.dot(line_ref[...], high, preferred_element_type=F32)
        n = G * CAP
        return both[:n] + both[n:] + jnp.dot(line_ref[0:n, :], rest, preferred_element_type=F32)

    def planes(both):
        n = G * CAP
        out = jnp.dot(both, plane_hi_ref[...], preferred_element_type=F32)
        return out[:n] + out[n:] + jnp.dot(both[:n], plane_lo_ref[...], preferred_element_type=F32)

    for copy in loads[5:]:
        copy.wait()
    for sweep in range(SWEEPS):

        def law(i, carry, sweep=sweep):
            at, e, s = advance(i, sweep)
            for c in range(3):
                e_s[c, pl.ds(at, 16), :] = e[c]
            s_pad[pl.ds(at + 8, 16), :] = s[0]
            d_s[pl.ds(at, 16), :] = diff_upper(s[1]) + diff_lower(s[2], low)
            return carry

        lax.fori_loop(0, G // 2, law, 0, unroll=True)
        s_pad[0:8, :] = s_pad[G * 8 : G * 8 + 8, :]
        s_pad[G * 8 + 8 :, :] = s_pad[8:16, :]

        def source(i, carry):
            at = pl.multiple_of(i * 16, 16)
            v = 0.5 * (s_pad[pl.ds(at + 16, 16), :] - s_pad[pl.ds(at, 16), :] + d_s[pl.ds(at, 16), :])
            high, rest = parts(v)
            x_s[pl.ds(at, 16), :] = high
            x_s[pl.ds(G * CAP + at, 16), :] = rest
            return carry

        lax.fori_loop(0, G // 2, source, 0, unroll=True)
        spectrum = lines(planes(x_s[...]))
        weight = jnp.broadcast_to(weight_ref[...], (G, CAP, PLANE)).reshape(G * CAP, PLANE)
        back = lines(spectrum * weight)
        high, rest = parts(back)
        x_s[0 : G * CAP, :] = high
        x_s[G * CAP :, :] = rest
        f_s[8 : G * 8 + 8, :] = planes(x_s[...])
        f_s[0:8, :] = f_s[G * 8 : G * 8 + 8, :]
        f_s[G * 8 + 8 :, :] = f_s[8:16, :]

    def finish(i, sums):
        at, e, s = advance(i, SWEEPS)
        out = []
        for c in range(3):
            wide = jnp.concatenate([e[c][0:8], e[c][8:16]], axis=1)
            for t in range(2 * PLANE // 128):
                row = pl.multiple_of((c * (VOX // 128) + i * 9 + t) * CAP, CAP)
                cells[pl.ds(row, CAP), :] = wide[:, 128 * t : 128 * t + 128]
            out.append(sums[c] + s[c][0:8] + s[c][8:16])
        return tuple(out)

    sums = lax.fori_loop(0, G // 2, finish, (zero, zero, zero), unroll=True)
    point_stress = [jnp.sum(s, axis=1, keepdims=True) * (1.0 / VOX) for s in sums]

    cells[ROWS * CAP :, :] = jnp.zeros((PACK * CAP - ROWS * CAP, 128), F32)
    hop1_scalars.wait()

    def at_index(table, row, position, bound):
        return jnp.clip(table[row, position] - 1, 0, bound - 1)

    def tiles_of(cell, m):
        return cells[pl.ds(m * 64 + cell, 8, stride=CAP), :]

    def hop(semaphores, slot, source, place, ring_place, line_place, core_place):
        send, recv = semaphores
        return pltpu.make_async_remote_copy(
            src_ref=source, dst_ref=place, send_sem=send.at[slot], recv_sem=recv.at[slot],
            device_id=((ring_place * LINE + line_place) * CORE + core_place, b), device_id_type=MESH,
        )

    one, two, three = (hop1_send, hop1_recv), (hop2_send, hop2_recv), (share_send, share_recv)

    def ring_first(j):
        to = lax.rem(y + STEPS[j], RING)
        n = RING_FIRST
        place = ring_got.at[pl.ds((j + 1) * n, n)] if j < 2 else ring_far
        return hop(one, j, send1.at[pl.ds(j * n, n)], place, to, z, 0)

    def line_first():
        return hop(one, 0, send1.at[pl.ds(0, LINE_FIRST)], line_got, y, 1 - z, 1)

    line_spans = ((0, 5), (5, LINE_NEAR - 5), (LINE_NEAR, LINE_FAR))

    def line_second(j):
        low, n = line_spans[j]
        return hop(two, j, send2.at[pl.ds(low, n)], final.at[pl.ds(FINAL_RING + low, n)], y, 1 - z, 0)

    half = RING_SECOND // 3
    pieces = tuple((j, h) for h in range(3) for j in (2, 0, 1))

    def ring_second(i):
        j, h = pieces[i]
        to = lax.rem(y + STEPS[j], RING)
        source = send2.at[pl.ds(j * RING_SECOND + h * half, half)]
        return hop(two, i, source, final.at[pl.ds(FINAL_LINE + y * RING_SECOND + h * half, half)], to, z, 1)

    ring_spans = ((0, NEAR), (NEAR, RING_FIRST)) + tuple((FINAL_RING + low, n) for low, n in line_spans)

    def share_ring(j, to=1):
        low, n = ring_spans[j]
        span = final.at[pl.ds(low, n)]
        return hop(three, j, (ring_got, ring_far, span, span, span)[j], span, y, z, to)

    def share_line(i, to=0):
        if i == 0:
            span, source = pl.ds(FINAL_LINE + y * RING_SECOND, RING_SECOND), here_got
        else:
            j, h = pieces[i - 1]
            from_y = lax.rem(y + RING - STEPS[j], RING)
            span = pl.ds(FINAL_LINE + from_y * RING_SECOND + h * half, half)
            source = final.at[span]
        return hop(three, i, source, final.at[span], y, z, to)

    def share_line_in(i):
        return share_line(i, 1)

    def share_ring_in(j):
        return share_ring(j, 0)

    @pl.when(core == 0)
    def _():
        for j in range(RING):
            to = lax.rem(y + (STEPS[j] if j < 3 else 0), RING)

            def fill(p, carry, j=j, to=to):
                cell = at_index(hop1_table, 0, to * RING_FIRST + p, CAP)
                for m in range(PACK // 8):
                    v = tiles_of(cell, m)
                    if j < 3:
                        send1[j * RING_FIRST + p, 8 * m : 8 * m + 8, :] = v
                    else:
                        ring_got[p, 8 * m : 8 * m + 8, :] = v
                return carry

            lax.fori_loop(0, RING_FIRST, fill, 0)
            if j < 3:
                ring_first(j).start()

    @pl.when(core == 1)
    def _():
        def fill(p, carry):
            cell = at_index(hop1_table, 0, p, CAP)
            for m in range(PACK // 8):
                send1[p, 8 * m : 8 * m + 8, :] = tiles_of(cell, m)
            return carry

        lax.fori_loop(0, LINE_FIRST, fill, 0)
        line_first().start()

    list2, list3, over = routing(worker.astype(F32), g)[1]()
    table_v[0:1, :] = list2
    table_v[1:2, :] = list3
    to_scalars = pltpu.make_async_copy(table_v, table, table_sem.at[1])
    to_scalars.start()
    hand_on = pltpu.make_async_copy(table_v, table_ref, table_sem.at[2])
    hand_on.start()
    flag[...] = jnp.broadcast_to(over, (8, 128)).astype(jnp.int32)
    for d in range(1, n_band):
        flag_copy(d).start()
    for r in range(CAP):

        def gather(m, carry, r=r):
            own[r, pl.ds(pl.multiple_of(m * 8, 8), 8), :] = cells[pl.ds(m * 64 + r, 8, stride=CAP), :]
            return carry

        lax.fori_loop(0, PACK // 8, gather, 0, unroll=True)
    keep = pltpu.make_async_copy(own, own_ref, local_sem.at[0])
    keep.start()

    stiff = stiff_ref[...]
    e11, e22, e12 = strain_s[0], strain_s[1], strain_s[2]
    stress = [
        stiff * (e11 + POISSON * e22),
        stiff * (e22 + POISSON * e11),
        stiff * (1.0 - POISSON) * e12,
    ]
    node = lax.broadcasted_iota(jnp.int32, stiff.shape, 0) * nodes_b + lax.broadcasted_iota(jnp.int32, stiff.shape, 1)
    for r in range(CAP):
        here = node == points[r]
        for c in range(3):
            stress[c] = jnp.where(here, point_stress[c][r : r + 1, :], stress[c])
    s11, s22, s12 = stress
    gz, bz = slopes[2], slopes[5]
    t1 = s11 * gz + s12 * bz
    t2 = s12 * gz + s22 * bz
    over_gore, over_band = [s11, s12, t1], [s12, s22, t2]
    for c in range(3):
        halo_g[2, c : c + 1, :] = over_gore[c][0:1]
        halo_g[3, c : c + 1, :] = over_gore[c][nodes_g - 1 :]
        halo_b[2, c : c + 1, :] = to_row(over_band[c][:, 0:1])
        halo_b[3, c : c + 1, :] = to_row(over_band[c][:, nodes_b - 1 :])
    second = halo_copies(1)
    for copy in second:
        copy.start()
    slopes[0] = s11
    slopes[1] = s12
    slopes[3] = s22
    slopes[4] = t1
    slopes[5] = t2

    to_scalars.wait()

    def stay_here():
        span = pl.ds(FINAL_LINE + y * RING_SECOND, RING_SECOND)
        return pltpu.make_async_copy(here_got, final.at[span], local_sem.at[1])

    def stay(j):
        low, n = ring_spans[j]
        return pltpu.make_async_copy((ring_got, ring_far)[j], final.at[pl.ds(low, n)], local_sem.at[1 + j])

    @pl.when(core == 0)
    def _():
        for j in range(2):
            for i in ((0, 1), (2,))[j]:
                ring_first(i).wait()

            def fill(p, carry, j=j):
                cell = at_index(table, 0, p, FINAL_RING)
                held = ring_got if j == 0 else ring_far
                cell = jnp.clip(cell - j * NEAR, 0, held.shape[0] - 1)
                for m in range(PACK // 8):
                    send2[p, 8 * m : 8 * m + 8, :] = held[cell, 8 * m : 8 * m + 8, :]
                return carry

            for k in ((0, 1), (2,))[j]:
                low, n = line_spans[k]
                lax.fori_loop(low, low + n, fill, 0)
                line_second(k).start()
            share_ring(j).start()
            stay(j).start()

    @pl.when(core == 1)
    def _():
        line_first().wait()
        for i in range(12):
            j, h = pieces[i] if i < 9 else (3, i - 9)
            to = lax.rem(y + (STEPS[j] if j < 3 else 0), RING)

            def fill(p, carry, j=j, to=to):
                index = at_index(table, 0, to * RING_SECOND + p, 2 * CAP)
                mine = index < CAP
                here, there = jnp.minimum(index, CAP - 1), jnp.maximum(index - CAP, 0)
                for m in range(PACK // 8):
                    v = jnp.where(mine, own[here, 8 * m : 8 * m + 8, :], line_got[there, 8 * m : 8 * m + 8, :])
                    if j < 3:
                        send2[j * RING_SECOND + p, 8 * m : 8 * m + 8, :] = v
                    else:
                        here_got[p, 8 * m : 8 * m + 8, :] = v
                return carry

            lax.fori_loop(h * half, (h + 1) * half, fill, 0)
            if j < 3:
                ring_second(i).start()
        share_line(0).start()
        stay_here().start()

    for copy in second:
        copy.wait()
    edge = []
    for c in range(3):
        before = jnp.where(inner_left, to_column(got_b[3, c : c + 1, :]), 0.0)
        after = jnp.where(inner_right, to_column(got_b[2, c : c + 1, :]), 0.0)
        edge.append((before, after))
    pairs = ((0, 1), (1, 3), (4, 5))
    for c, (p, q) in enumerate(pairs):
        value = gore_diff(slopes[p], got_g[3, c : c + 1, :], got_g[2, c : c + 1, :])
        value = value + band_diff(slopes[q], *edge[c])
        if c == 2:
            value = value + press_ref[...]
        force_ref[c] = value
    @pl.when(core == 0)
    def _():
        for j in range(3):
            line_second(j).wait()
            share_ring(2 + j).start()
        for j in range(2):
            stay(j).wait()
        for j in range(5):
            share_ring(j).wait_send()
        for i in range(10):
            share_line_in(i).wait_recv()

    @pl.when(core == 1)
    def _():
        for i in range(9):
            ring_second(i).wait()
            share_line(1 + i).start()
        stay_here().wait()
        for i in range(10):
            share_line(i).wait_send()
        for j in range(5):
            share_ring_in(j).wait_recv()

    for d in range(1, n_band):
        flag_copy(d).wait()
    total = flag[...]
    for d in range(1, n_band):
        total = total + flag_got[lax.rem(b + d, n_band)]
    flag_ref[0] = jnp.sum(total[0:1, :].astype(F32)).astype(jnp.int32)

    keep.wait()
    hand_on.wait()


def place_kernel(table, final, result, got, made, in_sem, out_sem):
    tiles, groups = VOX // 128, GROUP * MOST // 8

    def load(p):
        cell = jnp.clip(table[1, p] - 1, 0, FINAL - 1)
        return pltpu.make_async_copy(final.at[cell], got.at[p], in_sem.at[p])

    for p in range(GROUP * MOST):

        @pl.when(table[1, p] > 0)
        def _(p=p):
            load(p).start()

    def clear(i, carry):
        made[pl.ds(pl.multiple_of(i * 216, 216), 216), :] = jnp.zeros((216, 128), F32)
        return carry

    lax.fori_loop(0, 3 * groups * tiles * 8 // 216, clear, 0)

    def one(p, carry):
        @pl.when(table[1, p] > 0)
        def _():
            load(p).wait()
            for m in range(PACK // 8):
                v = got[p, 8 * m : 8 * m + 8, :]
                row = 8 * m
                while row < min(8 * m + 8, ROWS):
                    c, tile = row // tiles, row % tiles
                    count = min(8 * m + 8, (c + 1) * tiles) - row
                    start = ((c * groups + p // 8) * tiles + tile) * 8 + p % 8
                    made[pl.ds(start, count, stride=8), :] = v[row - 8 * m : row - 8 * m + count]
                    row = row + count

        return carry

    stores = []
    for t in range(groups):
        lax.fori_loop(8 * t, 8 * t + 8, one, 0)
        for c in range(3):
            span = pl.ds((c * groups + t) * tiles * 8, tiles * 8)
            stores.append(pltpu.make_async_copy(made.at[span], result.at[span], out_sem.at[3 * t + c]))
            stores[-1].start()
    for copy in stores:
        copy.wait()


def place(table, final):
    hbm = pl.BlockSpec(memory_space=pltpu.HBM)
    slots = GROUP * MOST
    result = pl.pallas_call(
        place_kernel,
        out_shape=jax.ShapeDtypeStruct((3 * slots * VOX // 128, 128), F32),
        in_specs=[pl.BlockSpec(memory_space=pltpu.SMEM), hbm],
        out_specs=hbm,
        scratch_shapes=[
            pltpu.VMEM((slots, PACK, 128), F32),
            pltpu.VMEM((3 * slots * VOX // 128, 128), F32),
            pltpu.SemaphoreType.DMA((slots,)),
            pltpu.SemaphoreType.DMA((3 * slots // 8,)),
        ],
        compiler_params=pltpu.CompilerParams(vmem_limit_bytes=60 * 2**20),
        name="place",
    )(table, final)
    return in_place(slots, result)


def in_place(slots, result):
    tiles = result.reshape(3, slots // 8, VOX // 128, 8, 128)
    return tiles.transpose(0, 1, 3, 2, 4).reshape(3, slots, VOX)


def send_all(workers, own, n_gore, slots):
    states = own[:, :ROWS].reshape(CAP, 3, VOX)
    onehot = (workers[:, None] == jnp.arange(n_gore, dtype=jnp.int32)[None, :]).astype(jnp.int32)
    earlier = jnp.cumsum(onehot, axis=0) - onehot
    slot_index = workers * MOST + jnp.sum(earlier * onehot, axis=1)
    outgoing = jnp.zeros((slots, 3, VOX), F32).at[slot_index].set(states)
    arrived = lax.all_to_all(
        outgoing.reshape(n_gore, MOST, 3, VOX), "gore", split_axis=0, concat_axis=0, tiled=True
    )
    return arrived.reshape(slots, 3, VOX).transpose(1, 0, 2)


def local(displacement, stiffness, pressure, yield_points, route, cell_state, weave):
    n_gore, n_band = lax.axis_size("gore"), lax.axis_size("band")
    slots = n_gore * MOST
    nodes_g, nodes_b = stiffness.shape
    plane_high, plane_low, line, weight = tables()
    vmem, hbm = pl.BlockSpec(memory_space=pltpu.VMEM), pl.BlockSpec(memory_space=pltpu.HBM)
    n = G * CAP
    vm, dma = pltpu.VMEM, pltpu.SemaphoreType.DMA
    workers = route.reshape(-1)
    force, flag, table, final, own = pl.pallas_call(
        lambda *refs: kernel(n_gore, n_band, *refs),
        out_shape=(
            jax.ShapeDtypeStruct((3, nodes_g, nodes_b), F32),
            jax.ShapeDtypeStruct((1,), jnp.int32),
            jax.ShapeDtypeStruct((8, 128), jnp.int32),
            jax.ShapeDtypeStruct((FINAL, PACK, 128), F32),
            jax.ShapeDtypeStruct((CAP, PACK, 128), F32),
        ),
        in_specs=[hbm] * 11,
        out_specs=(vmem, pl.BlockSpec(memory_space=pltpu.SMEM), hbm, hbm, hbm),
        scratch_shapes=[
            pltpu.SMEM((CAP,), jnp.int32),
            pltpu.SMEM((CAP,), jnp.int32),
            vm((3, nodes_g, nodes_b), F32),
            vm((nodes_g, nodes_b), F32),
            vm((nodes_g, nodes_b), F32),
            vm((3, CAP, VOX), F32),
            vm((VOX // 128, 128), F32),
            vm((PLANE, PLANE), BF16),
            vm((PLANE, PLANE), BF16),
            vm((2 * n, n), BF16),
            vm((G, 1, PLANE), F32),
            vm((4, 8, nodes_b), F32),
            vm((4, 8, nodes_g), F32),
            vm((4, 8, nodes_b), F32),
            vm((4, 8, nodes_g), F32),
            vm((6, nodes_g, nodes_b), F32),
            vm((3, nodes_g, nodes_b), F32),
            vm((3, n, PLANE), F32),
            vm((n, PLANE), F32),
            vm((n + 16, PLANE), F32),
            vm((n, PLANE), F32),
            vm((2 * n, PLANE), BF16),
            vm((n + 16, PLANE), F32),
            vm((PACK * CAP, 128), F32),
            vm((8, 128), jnp.int32),
            vm((n_gore, 8, 128), jnp.int32),
            vm((8, 128), jnp.int32),
            vm((n_band, 8, 128), jnp.int32),
            vm((8, 128), jnp.int32),
            pltpu.SMEM((8, 128), jnp.int32),
            vm((8, 128), jnp.int32),
            pltpu.SMEM((8, 128), jnp.int32),
            vm((CAP, PACK, 128), F32),
            vm((3 * RING_FIRST, PACK, 128), F32),
            vm((3 * RING_SECOND, PACK, 128), F32),
            vm((NEAR, PACK, 128), F32),
            vm((RING_FIRST, PACK, 128), F32),
            vm((LINE_FIRST, PACK, 128), F32),
            vm((RING_SECOND, PACK, 128), F32),
            dma((11,)),
            dma((8,)),
            dma((8,)),
            dma((n_gore,)),
            dma((n_gore,)),
            dma((n_band,)),
            dma((n_band,)),
            dma((3,)),
            dma((3,)),
            dma((3,)),
            dma((9,)),
            dma((9,)),
            dma((10,)),
            dma((10,)),
            dma((3,)),
        ],
        compiler_params=pltpu.CompilerParams(
            collective_id=0, has_side_effects=True, vmem_limit_bytes=60 * 2**20
        ),
        name="cells",
    )(
        yield_points,
        workers,
        displacement,
        stiffness,
        pressure,
        cell_state.transpose(1, 0, 2),
        weave.reshape(VOX // 128, 128),
        jnp.asarray(plane_high),
        jnp.asarray(plane_low),
        jnp.asarray(line),
        jnp.asarray(weight),
    )
    cell_strain = lax.cond(
        flag[0] == 0,
        lambda table, final, own, workers: place(table, final),
        lambda table, final, own, workers: send_all(workers, own, n_gore, slots),
        table, final, own, workers,
    )
    return force, cell_strain.transpose(1, 0, 2)


def solution(mesh):
    return jax.shard_map(
        local,
        mesh=mesh,
        in_specs=(
            P(None, "gore", "band"),
            P("gore", "band"),
            P("gore", "band"),
            P(("gore", "band")),
            P(("gore", "band"), None),
            P(("gore", "band"), None, None),
            P(),
        ),
        out_specs=(P(None, "gore", "band"), P(("gore", "band"), None, None)),
        check_vma=False,
    )
```
